32 devices in a mesh: gx: 8 (over z, x), gy: 4 (over y, core).
Axes of the slice: x: 2, y: 2, z: 4, core: 2. Of those that a mesh axis runs over, the one named last changes fastest.
Arguments:
- positions: float32 [3, 4096], P(None, ('gx', 'gy')), may hold values from -1 to 128, as said below
- features: bfloat16 [64, 4096], P(None, ('gx', 'gy')), may hold values from -6 to 6
- species: int32 [4096], P(('gx', 'gy')), may hold values from 0 to 4
- edge_list: int32 [2, 114688], P(None, ('gx', 'gy')), may hold values from 0 to 319, as said below
- edge_count: int32 [32], P(('gx', 'gy')), may hold values from 1 to 3136, as said below
- send_list_x: int32 [4096], P(('gx', 'gy')), may hold values from 0 to 127, as said below
- send_list_y: int32 [2048], P(('gx', 'gy')), may hold values from 0 to 255, as said below
- radial_in: float32 [64, 8], replicated, may hold values from -12 to 12
- radial_out: float32 [192, 64], replicated, may hold values from -0.75 to 0.75
- mix_weight: float32 [64, 192], replicated, may hold values from -0.4375 to 0.4375
- out_weight: float32 [64], replicated, may hold values from -0.75 to 0.75
- species_energy: float32 [5], replicated, may hold values from -6 to 6
Outputs:
- energies: float32 [4096], P(('gx', 'gy'))
- forces: float32 [3, 4096], P(None, ('gx', 'gy'))
The draws below stay inside these ranges and needn't reach their ends.
Inputs may be any that keep to these rules, and one draw needn't show every extreme that they name: `positions`: atoms sit on a lattice of cells with random displacements; each device holds the cells of its column in a random slot order. Each pair of lattice neighbours within 2 cells is listed at most once in all, on the device of its first atom, and only if both atoms exist; its second entry never names a copy that no device sends. `edge_list`: row 0 names own slots below 128, row 1 entries of the extended list; slots from edge_count on hold zeros. `edge_count`: every device has at most 3136 live pairs, and some device has exactly 3136 in every draw; counts differ widely between devices. `send_list_x`: each half names 64 distinct own slots. `send_list_y`: each half names 32 distinct entries among own atoms and x copies.
All inputs are finite; a program needn't handle non-finite values.
Results may differ from the reference program's by a relative error of at most 0.00055.
Values sent between devices are 32-bit elements; how exact they have to be, the bound alone decides.
No kernel may reach another device: no remote copies, remote signals or barrier semaphores. Data moves between devices by JAX's collectives and lax.ppermute only.
A program may use at most 64 MiB of HBM per device.

```python
import math
import jax
import jax.numpy as jnp
import numpy as np
from jax import lax

CHANNELS = 64
RADIAL_BASIS = 8
RADIAL_HIDDEN = 64
SPECIES = 5
LX = 4
LY = 16
LAYERS_Z = 2
REACH = 2
ATOMS_DEV = 128
GX = 64
GY = 32
EDGES_DEV = 3584
ATOMS = 4096
N_GX = 8
N_GY = 4


lattice_step = 1.6


def half_offsets():
    rows_list = []
    for layer_step in (0, 1):
        for step_x in range(-REACH, REACH + 1):
            for step_y in range(-REACH, REACH + 1):
                if layer_step == 1 or step_x > 0 or (step_x == 0 and step_y > 0):
                    rows_list.append((step_x, step_y, layer_step))
    return np.array(rows_list, np.int32)


def extended_index(target_x, target_y, target_z, slot_of):
    clip_x = jnp.clip(target_x, 0, LX - 1)
    clip_y = jnp.clip(target_y, 0, LY - 1)
    clip_z = jnp.clip(target_z, 0, LAYERS_Z - 1)
    own_site = (clip_x * LY + clip_y) * LAYERS_Z + clip_z
    own_slot = jnp.take_along_axis(slot_of, own_site.reshape(slot_of.shape[0], -1), axis=1).reshape(own_site.shape)
    lower_x = ATOMS_DEV + ((target_x + REACH) * LY + target_y) * LAYERS_Z + target_z
    upper_x = ATOMS_DEV + GX + ((target_x - LX) * LY + target_y) * LAYERS_Z + target_z
    lower_y = ATOMS_DEV + 2 * GX + ((target_x + REACH) * REACH + target_y + REACH) * LAYERS_Z + target_z
    upper_y = ATOMS_DEV + 2 * GX + GY + ((target_x + REACH) * REACH + target_y - LY) * LAYERS_Z + target_z
    middle = jnp.where(target_x < 0, lower_x, jnp.where(target_x >= LX, upper_x, own_slot))
    return jnp.where(target_y < 0, lower_y, jnp.where(target_y >= LY, upper_y, middle)).astype(jnp.int32)


def section_index(slot_of, column, row_y, layer_index):
    inner_x = jnp.clip(column, 0, LX - 1)
    own_slot = slot_of[:, (inner_x * LY + row_y) * LAYERS_Z + layer_index]
    lower_x = ATOMS_DEV + ((column + REACH) * LY + row_y) * LAYERS_Z + layer_index
    upper_x = ATOMS_DEV + GX + ((column - LX) * LY + row_y) * LAYERS_Z + layer_index
    chosen = jnp.where(column < 0, lower_x, jnp.where(column >= LX, upper_x, 0))
    inside = (column >= 0) & (column < LX)
    return jnp.where(inside[None, :], own_slot, chosen[None, :]).astype(jnp.int32)


def lattice_tables(key):
    device_total = N_GX * N_GY
    subkeys = jax.random.split(jax.random.fold_in(key, 101), device_total)
    site_order = jax.vmap(lambda subkey: jax.random.permutation(subkey, ATOMS_DEV))(subkeys).astype(jnp.int32)
    slot_of = jnp.argsort(site_order, axis=1).astype(jnp.int32)
    device_ids = jnp.arange(device_total, dtype=jnp.int32)
    column_x = (device_ids // N_GY)[:, None, None]
    column_y = (device_ids % N_GY)[:, None, None]
    cell_x = site_order // (LY * LAYERS_Z)
    cell_y = site_order // LAYERS_Z % LY
    cell_z = site_order % LAYERS_Z
    offsets = half_offsets()
    target_x = cell_x[:, :, None] + jnp.asarray(offsets[:, 0])[None, None, :]
    target_y = cell_y[:, :, None] + jnp.asarray(offsets[:, 1])[None, None, :]
    target_z = cell_z[:, :, None] + jnp.asarray(offsets[:, 2])[None, None, :]
    global_x = column_x * LX + target_x
    global_y = column_y * LY + target_y
    inside = (target_z < LAYERS_Z) & (global_x >= 0) & (global_x < N_GX * LX) & (global_y >= 0) & (global_y < N_GY * LY)
    density = jax.random.randint(jax.random.fold_in(key, 102), (device_total,), 1, 9)
    density = density.at[N_GX // 2 * N_GY + N_GY // 2].set(8)
    coin_draw = jax.random.randint(jax.random.fold_in(key, 103), inside.shape, 0, 8)
    kept_edges = inside & (coin_draw < density[:, None, None])
    target_slot = extended_index(target_x, target_y, target_z, slot_of)
    kept_flat = kept_edges.reshape(device_total, -1)
    placed = jnp.cumsum(kept_flat.astype(jnp.int32), axis=1) - 1
    placed = jnp.where(kept_flat, placed, EDGES_DEV)
    owners = jnp.broadcast_to(jnp.arange(ATOMS_DEV, dtype=jnp.int32)[None, :, None], kept_edges.shape).reshape(device_total, -1)
    device_rows = jnp.broadcast_to(device_ids[:, None], placed.shape)
    first_end = jnp.zeros((device_total, EDGES_DEV), jnp.int32).at[device_rows, placed].set(owners, mode='drop')
    second_end = jnp.zeros((device_total, EDGES_DEV), jnp.int32).at[device_rows, placed].set(target_slot.reshape(device_total, -1), mode='drop')
    counts = jnp.sum(kept_flat.astype(jnp.int32), axis=1)
    index_x = jnp.arange(GX, dtype=jnp.int32)
    band_index = index_x // (LY * LAYERS_Z)
    row_y = index_x // LAYERS_Z % LY
    layer_index = index_x % LAYERS_Z
    site_low = (band_index * LY + row_y) * LAYERS_Z + layer_index
    site_high = ((LX - REACH + band_index) * LY + row_y) * LAYERS_Z + layer_index
    list_x = jnp.concatenate([slot_of[:, site_low], slot_of[:, site_high]], axis=1)
    index_y = jnp.arange(GY, dtype=jnp.int32)
    column = index_y // (REACH * LAYERS_Z) - REACH
    band_y = index_y // LAYERS_Z % REACH
    layer_y = index_y % LAYERS_Z
    list_y = jnp.concatenate([section_index(slot_of, column, band_y, layer_y), section_index(slot_of, column, LY - REACH + band_y, layer_y)], axis=1)
    return (first_end, second_end, counts, list_x, list_y, site_order)


def draw_positions(key, part):
    tables = lattice_tables(key)
    site_order = tables[5]
    device_total = N_GX * N_GY
    device_ids = jnp.arange(device_total, dtype=jnp.int32)
    column_x = (device_ids // N_GY)[:, None]
    column_y = (device_ids % N_GY)[:, None]
    cell_x = site_order // (LY * LAYERS_Z)
    cell_y = site_order // LAYERS_Z % LY
    cell_z = site_order % LAYERS_Z
    lattice_points = jnp.stack([column_x * LX + cell_x, column_y * LY + cell_y, cell_z]).astype(jnp.float32) * lattice_step
    noise_key = jax.random.fold_in(key, 104)
    jitter = jnp.clip(0.1 * jax.random.normal(noise_key, lattice_points.shape, jnp.float32), -0.25, 0.25)
    return (lattice_points + jitter).reshape(3, -1)


def draw_edge_list(key, part):
    tables = lattice_tables(key)
    return jnp.stack([tables[0], tables[1]]).reshape(2, -1)


def draw_edge_count(key, part):
    return lattice_tables(key)[2]


def draw_send_list_x(key, part):
    return lattice_tables(key)[3].reshape(-1)


def draw_send_list_y(key, part):
    return lattice_tables(key)[4].reshape(-1)


def place_ends(values, rng, least, top_value):
    longest = values.shape.index(max(values.shape))
    spots = []
    for shift in (0, 1):
        where = [jax.random.randint(jax.random.fold_in(rng, axis), (), 0, length) for axis, length in enumerate(values.shape)]
        where[longest] = (where[longest] + shift) % values.shape[longest]
        spots.append(tuple(where))
    return values.at[spots[0]].set(least).at[spots[1]].set(top_value)


def levels(stream_key, dims, cuts, least, high):
    def one(dim, blocks):
        heights = jax.random.uniform(jax.random.fold_in(jax.random.fold_in(stream_key, 6), dim), (blocks,), jnp.float32, least / len(cuts), high / len(cuts))
        return jnp.repeat(jnp.exp(heights), dims[dim] // blocks).reshape((-1,) + (1,) * (len(dims) - dim - 1))

    level = one(*cuts[0])
    for cut in cuts[1:]:
        level = level * one(*cut)
    return level


def bell_draw(key, dims, spread, bound, cuts=(), held_as=jnp.bfloat16):
    values = jax.random.normal(key, dims, jnp.float32) * spread
    if len(cuts) > 0:
        values = levels(key, dims, cuts, -0.22, 0.18) * values
    return jnp.clip(values, min=-bound, max=bound).astype(held_as)


def setup_inputs(seed: int = 0) -> dict:
    streams_of = jax.random.split(jax.random.key(seed), 13)
    positions = draw_positions(jax.random.fold_in(streams_of[12], 71), 0)
    features = bell_draw(streams_of[1], (CHANNELS, ATOMS), 1.0, 6.0, ((1, 32),))
    species = place_ends(jax.random.randint(streams_of[2], (ATOMS,), 0, SPECIES), jax.random.fold_in(streams_of[2], 1), 0, SPECIES - 1).astype(jnp.int32)
    edge_list = draw_edge_list(jax.random.fold_in(streams_of[12], 71), 0)
    edge_count = draw_edge_count(jax.random.fold_in(streams_of[12], 71), 0)
    send_list_x = draw_send_list_x(jax.random.fold_in(streams_of[12], 71), 0)
    send_list_y = draw_send_list_y(jax.random.fold_in(streams_of[12], 71), 0)
    radial_in = bell_draw(streams_of[7], (RADIAL_HIDDEN, RADIAL_BASIS), 2.0, 12.0, (), jnp.float32)
    radial_out = bell_draw(streams_of[8], (3 * CHANNELS, RADIAL_HIDDEN), RADIAL_HIDDEN ** -0.5, 0.75, (), jnp.float32)
    mix_weight = bell_draw(streams_of[9], (CHANNELS, 3 * CHANNELS), (3 * CHANNELS) ** -0.5, 0.4375, (), jnp.float32)
    out_weight = bell_draw(streams_of[10], (CHANNELS,), CHANNELS ** -0.5, 0.75, (), jnp.float32)
    species_energy = bell_draw(streams_of[11], (SPECIES,), 1.0, 6.0, (), jnp.float32)
    return dict(positions=positions, features=features, species=species, edge_list=edge_list, edge_count=edge_count, send_list_x=send_list_x, send_list_y=send_list_y, radial_in=radial_in, radial_out=radial_out, mix_weight=mix_weight, out_weight=out_weight, species_energy=species_energy)


cutoff_radius = 5.0
message_scale = 0.3
degree_of = np.array([0, 1, 1, 1, 2, 2, 2, 2, 2], np.int32)
parity_sign = np.array([1.0, -1.0, -1.0, -1.0, 1.0, 1.0, 1.0, 1.0, 1.0], np.float32)
highest = lax.Precision.HIGHEST

def harmonics(direction):
    along_x, along_y, along_z = (direction[0], direction[1], direction[2])
    root_three = math.sqrt(3.0)
    root_five = math.sqrt(5.0)
    root_fifteen = math.sqrt(15.0)
    return jnp.stack([jnp.ones_like(along_x), root_three * along_x, root_three * along_y, root_three * along_z, root_fifteen * along_x * along_y, root_fifteen * along_y * along_z, 0.5 * root_five * (3.0 * along_z * along_z - 1.0), root_fifteen * along_x * along_z, 0.5 * root_fifteen * (along_x * along_x - along_y * along_y)])

def edge_messages(relative, live_mask, own_features, other_features, radial_in, radial_out):
    distance = jnp.sqrt(lax.optimization_barrier(jnp.sum(relative * relative, axis=0)))
    direction = relative / distance
    orders = jnp.arange(1, radial_in.shape[1] + 1, dtype=jnp.float32)[:, None]
    bessel = math.sqrt(2.0 / cutoff_radius) * jnp.sin(orders * (math.pi / cutoff_radius) * distance) / distance
    scaled = distance / cutoff_radius
    envelope = jnp.where(distance < cutoff_radius, (1.0 - scaled * scaled) ** 2, 0.0)
    hidden = jax.nn.silu(jnp.dot(radial_in, bessel, precision=highest))
    radial = jnp.dot(radial_out, hidden, precision=highest) * (envelope * live_mask)
    channels = own_features.shape[0]
    edge_total = distance.shape[0]
    radial = radial.reshape(3, channels, edge_total)[degree_of]
    shapes = harmonics(direction) * message_scale
    toward_own = shapes[:, None, :] * radial * other_features[None]
    toward_other = (shapes * parity_sign[:, None])[:, None, :] * radial * own_features[None]
    return (toward_own.reshape(9 * channels, edge_total), toward_other.reshape(9 * channels, edge_total))

def atom_energy(partial_value, feature_rows, mix_weight, out_weight):
    channels = feature_rows.shape[0]
    cube = partial_value.reshape(9, channels, -1)
    square = cube * cube
    invariant = jnp.concatenate([square[0], lax.optimization_barrier(jnp.sum(square[1:4], axis=0)), lax.optimization_barrier(jnp.sum(square[4:9], axis=0))], axis=0)
    mixed = jnp.dot(mix_weight, invariant, precision=highest) + feature_rows
    return jnp.dot(out_weight, jax.nn.silu(mixed), precision=highest)

def species_shift(species, species_energy):
    kinds = jnp.arange(species_energy.shape[0], dtype=jnp.int32)
    onehot = (species[None, :] == kinds[:, None]).astype(jnp.float32)
    return jnp.dot(species_energy, onehot, precision=highest)

def ghost_ids(send_list_x, send_list_y):
    device_total = N_GX * N_GY
    own_ids = jnp.arange(device_total * ATOMS_DEV, dtype=jnp.int32).reshape(N_GX, N_GY, ATOMS_DEV)
    picked = jnp.take_along_axis(own_ids, send_list_x.reshape(N_GX, N_GY, 2 * GX), axis=2)
    blank_x = jnp.full((1, N_GY, GX), -1, jnp.int32)
    lower_x = jnp.concatenate([blank_x, picked[:-1, :, GX:]], axis=0)
    upper_x = jnp.concatenate([picked[1:, :, :GX], blank_x], axis=0)
    section_one = jnp.concatenate([own_ids, lower_x, upper_x], axis=2)
    picked_y = jnp.take_along_axis(section_one, send_list_y.reshape(N_GX, N_GY, 2 * GY), axis=2)
    blank_y = jnp.full((N_GX, 1, GY), -1, jnp.int32)
    lower_y = jnp.concatenate([blank_y, picked_y[:, :-1, GY:]], axis=1)
    upper_y = jnp.concatenate([picked_y[:, 1:, :GY], blank_y], axis=1)
    return jnp.concatenate([section_one, lower_y, upper_y], axis=2).reshape(device_total, -1)

def reference(positions, features, species, edge_list, edge_count, send_list_x, send_list_y, radial_in, radial_out, mix_weight, out_weight, species_energy):
    device_total = N_GX * N_GY
    slot_ids = ghost_ids(send_list_x, send_list_y)
    pair_rows = edge_list.reshape(2, device_total, EDGES_DEV)
    first_end = jnp.take_along_axis(slot_ids, pair_rows[0], axis=1)
    second_end = jnp.take_along_axis(slot_ids, pair_rows[1], axis=1)
    live = jnp.arange(EDGES_DEV, dtype=jnp.int32)[None, :] < edge_count[:, None]
    first_end = jnp.where(live, first_end, 0).astype(jnp.int32)
    second_end = jnp.where(live, second_end, 0).astype(jnp.int32)
    feature_rows = features.astype(jnp.float32)
    filler = jnp.array([[2.0], [0.0], [0.0]], jnp.float32)

    def energy_total(coords):

        def advance(partial_value, block_data):
            first_row, second_row, live_row = block_data
            relative = coords[:, second_row] - coords[:, first_row]
            relative = jnp.where(live_row[None, :], relative, filler)
            toward_first, toward_second = edge_messages(relative, live_row.astype(jnp.float32), feature_rows[:, first_row], feature_rows[:, second_row], radial_in, radial_out)
            partial_value = partial_value.at[:, first_row].add(toward_first).at[:, second_row].add(toward_second)
            return (partial_value, None)
        start_sums = jnp.zeros((9 * feature_rows.shape[0], feature_rows.shape[1]), jnp.float32)
        partial_value, ignored = lax.scan(jax.checkpoint(advance), start_sums, (first_end, second_end, live))
        energy = atom_energy(partial_value, feature_rows, mix_weight, out_weight)
        return (jnp.sum(energy), energy)
    (ignored, energy), gradient = jax.value_and_grad(energy_total, has_aux=True)(positions)
    return (energy + species_shift(species, species_energy), -gradient)
```

```python
import math

import jax
import jax.numpy as jnp
import numpy as np
from jax import lax
from jax.experimental import pallas as pl
from jax.experimental.pallas import tpu as pltpu
from jax.sharding import PartitionSpec as P

cutoff_radius = 5.0
message_scale = 0.3
highest = lax.Precision.HIGHEST
f32 = jnp.float32
bf16 = jnp.bfloat16
i32 = jnp.int32

LANES = 128
EDGE_STEP = 256
OWN_ROWS = 56
GHOST_ROWS = 24
DEGREE_ROWS = ((0, 1), (1, 4), (4, 9))


def nt_dot(left, right):
    return lax.dot_general(left, right, (((1,), (1,)), ((), ())), preferred_element_type=f32)


def plain_dot(left, right):
    return lax.dot_general(left, right, (((1,), (0,)), ((), ())), preferred_element_type=f32)


def list_kernel(count_ref, edges_ref, own_ref, ghost_ref, count_out, own_acc, ghost_acc, own_base, ghost_base):
    ghosts = ghost_base.shape[0]
    live_total = count_ref[0]
    own_acc[...] = jnp.zeros_like(own_acc)
    ghost_acc[...] = jnp.zeros_like(ghost_acc)
    own_base[...] = jnp.zeros_like(own_base)
    ghost_base[...] = jnp.zeros_like(ghost_base)
    count_out[...] = jnp.zeros_like(count_out)
    before = lax.broadcasted_iota(i32, (EDGE_STEP, EDGE_STEP), 0) < lax.broadcasted_iota(
        i32, (EDGE_STEP, EDGE_STEP), 1
    )
    earlier = before.astype(f32).astype(bf16)
    every = jnp.ones((EDGE_STEP, EDGE_STEP), bf16)
    row = jnp.ones((8, EDGE_STEP), bf16)
    own_lane = lax.broadcasted_iota(i32, (LANES, EDGE_STEP), 0)
    ghost_lane = lax.broadcasted_iota(i32, (ghosts, EDGE_STEP), 0) + LANES
    own_rank = lax.broadcasted_iota(i32, (own_acc.shape[0], EDGE_STEP), 0).astype(f32)
    ghost_rank = lax.broadcasted_iota(i32, (ghost_acc.shape[0], EDGE_STEP), 0).astype(f32)

    def step(number, carry):
        offset = pl.multiple_of(number * EDGE_STEP, EDGE_STEP)
        first = edges_ref[0:1, pl.ds(offset, EDGE_STEP)]
        second = edges_ref[1:2, pl.ds(offset, EDGE_STEP)]
        live = offset + lax.broadcasted_iota(i32, (1, EDGE_STEP), 1) < live_total
        first = jnp.where(live, first, -1)
        second = jnp.where(live, second, -1)
        first_hot = (own_lane == first).astype(f32)
        second_hot = (own_lane == second).astype(f32)
        ghost_hot = (ghost_lane == second).astype(f32)
        first_low = first_hot.astype(bf16)
        second_low = second_hot.astype(bf16)
        ghost_low = ghost_hot.astype(bf16)
        base = own_base[...]
        first_rank = jnp.sum(first_hot * (base + plain_dot(first_low, earlier)), axis=0, keepdims=True)
        base = base + plain_dot(first_low, every)
        second_rank = jnp.sum(second_hot * (base + plain_dot(second_low, earlier)), axis=0, keepdims=True)
        own_base[...] = base + plain_dot(second_low, every)
        base = ghost_base[...]
        second_rank += jnp.sum(ghost_hot * (base + plain_dot(ghost_low, earlier)), axis=0, keepdims=True)
        ghost_base[...] = base + plain_dot(ghost_low, every)
        first_code = (first - 160).astype(f32)
        second_code = (second - 160).astype(f32)
        place_first = jnp.where(own_rank == first_rank, second_code, 0.0).astype(bf16)
        place_second = jnp.where(own_rank == second_rank, first_code, 0.0).astype(bf16)
        place_ghost = jnp.where(ghost_rank == second_rank, first_code, 0.0).astype(bf16)
        own_acc[...] += nt_dot(place_first, first_low) + nt_dot(place_second, second_low)
        ghost_acc[:, 0:ghosts] += nt_dot(place_ghost, ghost_low)
        count_out[:, 0:LANES] += nt_dot(row, first_low) + nt_dot(row, second_low)
        count_out[:, LANES : LANES + ghosts] += nt_dot(row, ghost_low)
        return carry

    lax.fori_loop(0, (live_total + EDGE_STEP - 1) // EDGE_STEP, step, 0)
    own_code = (own_acc[0:OWN_ROWS, :] + 160.0).astype(i32)
    ghost_code = (ghost_acc[0:GHOST_ROWS, :] + 160.0).astype(i32)
    counts = count_out[0:1, :].astype(i32)
    own_live = lax.broadcasted_iota(i32, (OWN_ROWS, LANES), 0) < counts[:, 0:LANES]
    ghost_live = lax.broadcasted_iota(i32, ghost_code.shape, 0) < counts[:, LANES:]
    own_ref[...] = jnp.where(own_live, own_code, 0)
    ghost_ref[...] = jnp.where(ghost_live, ghost_code, 0)


def make_lists(edge_list, edge_count, ghosts):
    vmem = pl.BlockSpec(memory_space=pltpu.VMEM)
    return pl.pallas_call(
        list_kernel,
        out_shape=(
            jax.ShapeDtypeStruct((OWN_ROWS, LANES), i32),
            jax.ShapeDtypeStruct((GHOST_ROWS, 2 * LANES), i32),
            jax.ShapeDtypeStruct((8, 3 * LANES), f32),
        ),
        in_specs=[pl.BlockSpec(memory_space=pltpu.SMEM), vmem],
        out_specs=(vmem, vmem, vmem),
        scratch_shapes=[
            pltpu.VMEM((64, LANES), f32),
            pltpu.VMEM((32, 2 * LANES), f32),
            pltpu.VMEM((LANES, EDGE_STEP), f32),
            pltpu.VMEM((ghosts, EDGE_STEP), f32),
        ],
        compiler_params=pltpu.CompilerParams(vmem_limit_bytes=40 * 1024 * 1024),
    )(edge_count, edge_list)


def spread_row(ref, row, rows):
    return jnp.broadcast_to(ref[pl.ds(row, 1), :], (rows, LANES))


def lookup(table_ref, row, tables, slot, block):
    result = None
    for number in range(tables):
        entries = jnp.broadcast_to(
            table_ref[row : row + 1, number * LANES : (number + 1) * LANES], (8, LANES)
        )
        value = jnp.take_along_axis(entries, slot, axis=1)
        result = value if result is None else jnp.where(block == number, value, result)
    return result


def sine_cosine(scaled):
    angle = math.pi * (scaled - 0.5)
    square = angle * angle
    cosine = 1.0
    sine = 1.0
    for order in range(7, 0, -1):
        cosine = 1.0 - square * cosine * (1.0 / ((2 * order - 1) * (2 * order)))
        sine = 1.0 - square * sine * (1.0 / ((2 * order) * (2 * order + 1)))
    return cosine, -(angle * sine)


def pair_geometry(table_ref, codes, live, tables, lane0, basis, tangent, sines_ref, slopes_ref):
    slot = codes & (LANES - 1)
    block = codes >> 7
    relative = []
    for axis in range(3):
        partner = lookup(table_ref, 64 + axis, tables, slot, block)
        target = jnp.broadcast_to(table_ref[64 + axis : 65 + axis, lane0 : lane0 + LANES], (8, LANES))
        relative.append(jnp.where(live, partner - target, 2.0 if axis == 0 else 0.0))
    distance = jnp.sqrt(relative[0] * relative[0] + relative[1] * relative[1] + relative[2] * relative[2])
    inverse = 1.0 / distance
    direction = [part * inverse for part in relative]
    inside = live & (distance < cutoff_radius)
    scaled = jnp.minimum(distance, cutoff_radius) * (1.0 / cutoff_radius)
    room = 1.0 - scaled * scaled
    envelope = jnp.where(inside, message_scale * room * room, 0.0)
    envelope_slope = jnp.where(inside, (-4.0 * message_scale / cutoff_radius) * scaled * room, 0.0)
    sine, cosine = sine_cosine(scaled)
    twice = 2.0 * cosine
    scale = math.sqrt(2.0 / cutoff_radius)
    last_sine, last_cosine = jnp.zeros_like(sine), jnp.ones_like(sine)
    for order in range(1, basis + 1):
        wave = scale * sine * inverse
        sines_ref[(order - 1) * 8 : order * 8, :] = wave
        if tangent:
            slope = (scale * order * math.pi / cutoff_radius) * cosine * inverse - wave * inverse
            slopes_ref[(order - 1) * 8 : order * 8, :] = slope
        sine, last_sine = twice * sine - last_sine, sine
        cosine, last_cosine = twice * cosine - last_cosine, cosine
    return direction, inverse, envelope, envelope_slope, inside


def split_rows(ref, basis):
    pieces = []
    for row in range(8):
        whole = ref[pl.ds(row, basis, stride=8), :]
        high = whole.astype(bf16).astype(f32)
        rest = whole - high
        middle = rest.astype(bf16).astype(f32)
        low = rest - middle
        pieces.append(jnp.concatenate([high, middle, high, middle, low, high], axis=0).astype(bf16))
    return jnp.concatenate(pieces, axis=1)


def high_low(value):
    high = value.astype(bf16)
    low = (value - high.astype(f32)).astype(bf16)
    return high, low


def shapes_of(direction):
    x, y, z = direction
    three, five, fifteen = math.sqrt(3.0), math.sqrt(5.0), math.sqrt(15.0)
    return [
        jnp.ones_like(x),
        three * x,
        three * y,
        three * z,
        fifteen * x * y,
        fifteen * y * z,
        0.5 * five * (3.0 * z * z - 1.0),
        fifteen * x * z,
        0.5 * fifteen * (x * x - y * y),
    ]


def hot_codes(codes_ref, size):
    columns = []
    lane = lax.broadcasted_iota(i32, (size, LANES), 0)
    for row in range(8):
        codes = jnp.broadcast_to(codes_ref[row : row + 1, :], (size, LANES))
        columns.append((lane == codes).astype(f32).astype(bf16))
    return jnp.concatenate(columns, axis=1)


def forward_group(refs, codes_all, counts_ref, lane0, size, out_ref):
    (table_ref, feature_ref, win_ref, wout_ref, codes_ref, sines_ref, env_ref, shape_ref, hidden_ref, radial_ref, partner_ref) = refs
    basis = win_ref.shape[1] // 6
    tables = -(-size // LANES)
    count = jnp.broadcast_to(counts_ref[0:1, lane0 : lane0 + LANES], (8, LANES)).astype(i32)
    steps = (jnp.max(counts_ref[0:1, lane0 : lane0 + LANES]).astype(i32) + 7) // 8
    out_ref[:, lane0 : lane0 + LANES] = jnp.zeros((576, LANES), f32)

    def step(number, carry):
        offset = pl.multiple_of(number * 8, 8)
        codes = codes_all(offset)
        live = offset + lax.broadcasted_iota(i32, (8, LANES), 0) < count
        codes_ref[...] = codes
        direction, inverse, envelope, ignored, inside = pair_geometry(
            table_ref, codes, live, tables, lane0, basis, False, sines_ref, None
        )
        env_ref[...] = envelope
        shapes = shapes_of(direction)
        for q in range(1, 9):
            shape_ref[q * 8 : q * 8 + 8, :] = shapes[q]
        value = plain_dot(win_ref[...], split_rows(sines_ref, basis))
        for row in range(8):
            part = value[:, row * LANES : (row + 1) * LANES]
            hidden = part / (1.0 + jnp.exp(-part)) * spread_row(env_ref, row, 64)
            high, low = high_low(hidden)
            hidden_ref[0:64, row * LANES : (row + 1) * LANES] = high
            hidden_ref[64:128, row * LANES : (row + 1) * LANES] = low
        hidden = hidden_ref[...]
        radial_ref[...] = plain_dot(wout_ref[...], jnp.concatenate([hidden, hidden], axis=0))
        partner_ref[...] = plain_dot(feature_ref[:, 0:size], hot_codes(codes_ref, size))
        for block in range(8):
            sums = [
                out_ref[q * 64 + block * 8 : q * 64 + block * 8 + 8, lane0 : lane0 + LANES]
                for q in range(9)
            ]
            for row in range(8):
                lanes = slice(row * LANES, (row + 1) * LANES)
                feature = partner_ref[block * 8 : block * 8 + 8, lanes]
                for degree, (low, high) in enumerate(DEGREE_ROWS):
                    at = degree * 64 + block * 8
                    weight = radial_ref[at : at + 8, lanes] * feature
                    for q in range(low, high):
                        if q == 0:
                            sums[q] = sums[q] + weight
                        else:
                            sums[q] = sums[q] + weight * spread_row(shape_ref, q * 8 + row, 8)
            for q in range(9):
                out_ref[q * 64 + block * 8 : q * 64 + block * 8 + 8, lane0 : lane0 + LANES] = sums[q]
        return carry

    lax.fori_loop(0, steps, step, 0)


def forward_kernel(own_list, ghost_list, counts_ref, table_ref, win_ref, wout_ref, out_ref, feature_ref, *scratch):
    feature_ref[...] = table_ref[0:64, :].astype(bf16)
    refs = (table_ref, feature_ref, win_ref, wout_ref) + scratch
    forward_group(refs, lambda at: own_list[pl.ds(at, 8), :], counts_ref, 0, 320, out_ref)
    for group in (0, 1):
        lanes = slice(group * LANES, (group + 1) * LANES)
        forward_group(
            refs, lambda at, lanes=lanes: ghost_list[pl.ds(at, 8), lanes], counts_ref, (group + 1) * LANES, LANES, out_ref
        )


def forward_pass(own_list, ghost_list, counts, table, win, wout):
    vmem = pl.BlockSpec(memory_space=pltpu.VMEM)
    wide = 8 * LANES
    return pl.pallas_call(
        forward_kernel,
        out_shape=jax.ShapeDtypeStruct((576, 3 * LANES), f32),
        in_specs=[vmem] * 6,
        out_specs=vmem,
        scratch_shapes=[
            pltpu.VMEM((64, 3 * LANES), bf16),
            pltpu.VMEM((8, LANES), i32),
            pltpu.VMEM((64, LANES), f32),
            pltpu.VMEM((8, LANES), f32),
            pltpu.VMEM((72, LANES), f32),
            pltpu.VMEM((128, wide), bf16),
            pltpu.VMEM((192, wide), f32),
            pltpu.VMEM((64, wide), f32),
        ],
        compiler_params=pltpu.CompilerParams(vmem_limit_bytes=40 * 1024 * 1024),
    )(own_list, ghost_list, counts, table, win, wout)


def backward_group(refs, codes_all, counts_ref, lane0, size, gradient_ref, force_ref, scatter_ref):
    (table_ref, feature_ref, win_ref, wout_ref, codes_ref, sines_ref, slopes_ref, env_ref, shape_ref, hidden_ref, radial_ref, partner_ref, pulled_ref, push_ref) = refs
    basis = win_ref.shape[1] // 6
    tables = -(-size // LANES)
    wide = 8 * LANES
    count = jnp.broadcast_to(counts_ref[0:1, lane0 : lane0 + LANES], (8, LANES)).astype(i32)
    steps = (jnp.max(counts_ref[0:1, lane0 : lane0 + LANES]).astype(i32) + 7) // 8
    three, five, fifteen = math.sqrt(3.0), math.sqrt(5.0), math.sqrt(15.0)

    def step(number, carry):
        offset = pl.multiple_of(number * 8, 8)
        codes = codes_all(offset)
        live = offset + lax.broadcasted_iota(i32, (8, LANES), 0) < count
        codes_ref[...] = codes
        direction, inverse, envelope, envelope_slope, inside = pair_geometry(
            table_ref, codes, live, tables, lane0, basis, True, sines_ref, slopes_ref
        )
        env_ref[0:8, :] = envelope
        env_ref[8:16, :] = envelope_slope
        shapes = shapes_of(direction)
        for q in range(1, 9):
            shape_ref[q * 8 : q * 8 + 8, :] = shapes[q]
        both = jnp.concatenate([split_rows(sines_ref, basis), split_rows(slopes_ref, basis)], axis=1)
        value = plain_dot(win_ref[...], both)
        for row in range(8):
            lanes = slice(row * LANES, (row + 1) * LANES)
            later = slice(wide + row * LANES, wide + (row + 1) * LANES)
            part, part_slope = value[:, lanes], value[:, later]
            gate = 1.0 / (1.0 + jnp.exp(-part))
            hidden = part * gate
            hidden_slope = gate * (1.0 + part * (1.0 - gate)) * part_slope
            scale = spread_row(env_ref, row, 64)
            scale_slope = spread_row(env_ref, 8 + row, 64)
            high, low = high_low(hidden * scale)
            hidden_ref[0:64, lanes] = high
            hidden_ref[64:128, lanes] = low
            high, low = high_low(hidden * scale_slope + hidden_slope * scale)
            hidden_ref[0:64, later] = high
            hidden_ref[64:128, later] = low
        hidden = hidden_ref[...]
        radial_ref[...] = plain_dot(wout_ref[...], jnp.concatenate([hidden, hidden], axis=0))
        hot = hot_codes(codes_ref, size)
        partner_ref[...] = plain_dot(feature_ref[:, 0:size], hot)
        for row in range(8):
            lanes = slice(row * LANES, (row + 1) * LANES)
            later = slice(wide + row * LANES, wide + (row + 1) * LANES)
            pulled = [jnp.zeros((8, LANES), f32) for q in range(9)]
            spoke = jnp.zeros((8, LANES), f32)
            for block in range(8):
                feature = partner_ref[block * 8 : block * 8 + 8, lanes]
                for degree, (low, high) in enumerate(DEGREE_ROWS):
                    at = degree * 64 + block * 8
                    weight = radial_ref[at : at + 8, lanes] * feature
                    weight_slope = radial_ref[at : at + 8, later] * feature
                    mixed = None
                    for q in range(low, high):
                        gradient = gradient_ref[q * 64 + block * 8 : q * 64 + block * 8 + 8, lane0 : lane0 + LANES]
                        if q > 0:
                            pulled[q] = pulled[q] + weight * gradient
                            gradient = gradient * spread_row(shape_ref, q * 8 + row, 8)
                        mixed = gradient if mixed is None else mixed + gradient
                    spoke = spoke + weight_slope * mixed
            for q in range(1, 9):
                pulled_ref[q * 8 + row : q * 8 + row + 1, :] = jnp.sum(pulled[q], axis=0, keepdims=True)
            pulled_ref[row : row + 1, :] = jnp.sum(spoke, axis=0, keepdims=True)
        x, y, z = direction
        p = [pulled_ref[q * 8 : q * 8 + 8, :] for q in range(9)]
        turn = [
            three * p[1] + fifteen * (y * p[4] + z * p[7] + x * p[8]),
            three * p[2] + fifteen * (x * p[4] + z * p[5] - y * p[8]),
            three * p[3] + fifteen * (y * p[5] + x * p[7]) + (3.0 * five) * z * p[6],
        ]
        along = x * turn[0] + y * turn[1] + z * turn[2]
        for axis in range(3):
            part = (turn[axis] - direction[axis] * along) * inverse + direction[axis] * p[0]
            part = jnp.where(inside, part, 0.0)
            force_ref[axis : axis + 1, lane0 : lane0 + LANES] += jnp.sum(part, axis=0, keepdims=True)
            high = part.astype(bf16).astype(f32)
            push_ref[axis * 8 : axis * 8 + 8, :] = high
            push_ref[24 + axis * 8 : 32 + axis * 8, :] = part - high
        push = jnp.concatenate([push_ref[pl.ds(row, 8, stride=8), :] for row in range(8)], axis=1)
        scatter_ref[:, 0:size] += nt_dot(push.astype(bf16), hot)
        return carry

    lax.fori_loop(0, steps, step, 0)


def backward_kernel(own_list, ghost_list, counts_ref, table_ref, win_ref, wout_ref, gradient_ref, out_ref, feature_ref, scatter_ref, *scratch):
    feature_ref[...] = table_ref[0:64, :].astype(bf16)
    refs = (table_ref, feature_ref, win_ref, wout_ref) + scratch
    out_ref[...] = jnp.zeros_like(out_ref)
    scatter_ref[...] = jnp.zeros_like(scatter_ref)
    push_ref = scratch[-1]
    push_ref[...] = jnp.zeros_like(push_ref)
    backward_group(refs, lambda at: own_list[pl.ds(at, 8), :], counts_ref, 0, 320, gradient_ref, out_ref, scatter_ref)
    for group in (0, 1):
        lanes = slice(group * LANES, (group + 1) * LANES)
        backward_group(
            refs, lambda at, lanes=lanes: ghost_list[pl.ds(at, 8), lanes], counts_ref, (group + 1) * LANES, LANES,
            gradient_ref, out_ref, scatter_ref,
        )
    for axis in range(3):
        out_ref[axis : axis + 1, :] -= scatter_ref[axis : axis + 1, :] + scatter_ref[axis + 3 : axis + 4, :]


def backward_pass(own_list, ghost_list, counts, table, win, wout, gradient):
    vmem = pl.BlockSpec(memory_space=pltpu.VMEM)
    wide = 8 * LANES
    return pl.pallas_call(
        backward_kernel,
        out_shape=jax.ShapeDtypeStruct((8, 3 * LANES), f32),
        in_specs=[vmem] * 7,
        out_specs=vmem,
        scratch_shapes=[
            pltpu.VMEM((64, 3 * LANES), bf16),
            pltpu.VMEM((8, 3 * LANES), f32),
            pltpu.VMEM((8, LANES), i32),
            pltpu.VMEM((64, LANES), f32),
            pltpu.VMEM((64, LANES), f32),
            pltpu.VMEM((16, LANES), f32),
            pltpu.VMEM((72, LANES), f32),
            pltpu.VMEM((128, 2 * wide), bf16),
            pltpu.VMEM((192, 2 * wide), f32),
            pltpu.VMEM((64, wide), f32),
            pltpu.VMEM((72, LANES), f32),
            pltpu.VMEM((64, LANES), f32),
        ],
        compiler_params=pltpu.CompilerParams(vmem_limit_bytes=40 * 1024 * 1024),
    )(own_list, ghost_list, counts, table, win, wout, gradient)


def rounded(value):
    return lax.reduce_precision(value, 8, 7)


def stacked_weights(radial_in, radial_out):
    high = rounded(radial_in)
    middle = rounded(radial_in - high)
    low = rounded(radial_in - high - middle)
    win = jnp.concatenate([high, high, middle, middle, high, low], axis=1).astype(bf16)
    high = rounded(radial_out)
    low = rounded(radial_out - high)
    wout = jnp.concatenate([high, high, low, low], axis=1).astype(bf16)
    return win, wout


def ring_pair(low_block, high_block, axis):
    count = lax.axis_size(axis)
    up = [(i, (i + 1) % count) for i in range(count)]
    down = [(target, source) for source, target in up]
    return lax.ppermute(high_block, axis, up), lax.ppermute(low_block, axis, down)


def spread(rows_data, send_list_x, send_list_y):
    ghost_x = send_list_x.shape[0] // 2
    ghost_y = send_list_y.shape[0] // 2
    outgoing = jnp.take(rows_data, send_list_x, axis=1)
    low, high = ring_pair(outgoing[:, :ghost_x], outgoing[:, ghost_x:], "gx")
    section_one = jnp.concatenate([rows_data, low, high], axis=1)
    outgoing = jnp.take(section_one, send_list_y, axis=1)
    low, high = ring_pair(outgoing[:, :ghost_y], outgoing[:, ghost_y:], "gy")
    return jnp.concatenate([section_one, low, high], axis=1)


def collect(extended, atoms_here, send_list_x, send_list_y):
    ghost_x = send_list_x.shape[0] // 2
    ghost_y = send_list_y.shape[0] // 2
    width_one = atoms_here + 2 * ghost_x
    low, high = ring_pair(
        extended[:, width_one : width_one + ghost_y], extended[:, width_one + ghost_y : width_one + 2 * ghost_y], "gy"
    )
    section_one = extended[:, :width_one].at[:, send_list_y].add(jnp.concatenate([low, high], axis=1))
    low, high = ring_pair(section_one[:, atoms_here : atoms_here + ghost_x], section_one[:, atoms_here + ghost_x :], "gx")
    return section_one[:, :atoms_here].at[:, send_list_x].add(jnp.concatenate([low, high], axis=1))


def atom_energy(partial_value, feature_rows, mix_weight, out_weight):
    channels = feature_rows.shape[0]
    cube = partial_value.reshape(9, channels, -1)
    square = cube * cube
    invariant = jnp.concatenate(
        [square[0], jnp.sum(square[1:4], axis=0), jnp.sum(square[4:9], axis=0)], axis=0
    )
    mixed = jnp.dot(mix_weight, invariant, precision=highest) + feature_rows
    return jnp.dot(out_weight, jax.nn.silu(mixed), precision=highest)


def species_shift(species, species_energy):
    kinds = jnp.arange(species_energy.shape[0], dtype=jnp.int32)
    onehot = (species[None, :] == kinds[:, None]).astype(f32)
    return jnp.dot(species_energy, onehot, precision=highest)


def local(
    positions, features, species, edge_list, edge_count, send_list_x, send_list_y,
    radial_in, radial_out, mix_weight, out_weight, species_energy,
):
    atoms_here = positions.shape[1]
    ghosts = send_list_x.shape[0] + send_list_y.shape[0]
    own_features = features.astype(f32)
    own_list, ghost_list, counts = make_lists(edge_list, edge_count, ghosts)
    rows = jnp.concatenate([own_features, positions], axis=0)
    extended = spread(rows, send_list_x, send_list_y)
    table = jnp.pad(extended, ((0, 5), (0, 3 * LANES - extended.shape[1])))
    win, wout = stacked_weights(radial_in, radial_out)
    sums = forward_pass(own_list, ghost_list, counts, table, win, wout)
    own_sums = collect(sums[:, : atoms_here + ghosts], atoms_here, send_list_x, send_list_y)

    def readout_own(sums_in):
        return atom_energy(sums_in, own_features, mix_weight, out_weight)

    energy_own, pullback = jax.vjp(readout_own, own_sums)
    (own_gradient,) = pullback(jnp.ones_like(energy_own))
    gradient = spread(own_gradient, send_list_x, send_list_y)
    gradient = jnp.pad(gradient, ((0, 0), (0, 3 * LANES - gradient.shape[1])))
    force_rows = backward_pass(own_list, ghost_list, counts, table, win, wout, gradient)
    forces = collect(force_rows[:3, : atoms_here + ghosts], atoms_here, send_list_x, send_list_y)
    energies = energy_own + species_shift(species, species_energy)
    return energies, forces


def solution(mesh):
    placed = (
        P(None, ("gx", "gy")), P(None, ("gx", "gy")), P(("gx", "gy")), P(None, ("gx", "gy")), P(("gx", "gy")),
        P(("gx", "gy")), P(("gx", "gy")), P(), P(), P(), P(), P(),
    )
    return jax.shard_map(
        local, mesh=mesh, in_specs=placed, out_specs=(P(("gx", "gy")), P(None, ("gx", "gy"))), check_vma=False,
    )
```

```python
import math

import jax
import jax.numpy as jnp
import numpy as np
from jax import lax
from jax.experimental import pallas as pl
from jax.experimental.pallas import tpu as pltpu
from jax.sharding import PartitionSpec as P

cutoff_radius = 5.0
message_scale = 0.3
highest = lax.Precision.HIGHEST
f32 = jnp.float32
bf16 = jnp.bfloat16
i32 = jnp.int32

LANES = 128
EDGE_STEP = 256
OWN_ROWS = 56
GHOST_ROWS = 24
OWN_AT, X_AT, Y_AT, COUNT_AT, SEND_AT, PAYLOAD = 72, 128, 152, 176, 179, 184
DEGREE_ROWS = ((0, 1), (1, 4), (4, 9))


def nt_dot(left, right):
    return lax.dot_general(left, right, (((1,), (1,)), ((), ())), preferred_element_type=f32)


def plain_dot(left, right):
    return lax.dot_general(left, right, (((1,), (0,)), ((), ())), preferred_element_type=f32)


def list_kernel(count_ref, edges_ref, positions_ref, features_ref, send_x_ref, send_y_ref, out_ref, count_out, own_acc, ghost_acc, own_base, ghost_base):
    ghosts = ghost_base.shape[0]
    live_total = count_ref[0]
    own_acc[...] = jnp.zeros_like(own_acc)
    ghost_acc[...] = jnp.zeros_like(ghost_acc)
    own_base[...] = jnp.zeros_like(own_base)
    ghost_base[...] = jnp.zeros_like(ghost_base)
    count_out[...] = jnp.zeros_like(count_out)
    before = lax.broadcasted_iota(i32, (EDGE_STEP, EDGE_STEP), 0) < lax.broadcasted_iota(
        i32, (EDGE_STEP, EDGE_STEP), 1
    )
    earlier = before.astype(f32).astype(bf16)
    every = jnp.ones((EDGE_STEP, EDGE_STEP), bf16)
    row = jnp.ones((8, EDGE_STEP), bf16)
    own_lane = lax.broadcasted_iota(i32, (LANES, EDGE_STEP), 0)
    ghost_lane = lax.broadcasted_iota(i32, (ghosts, EDGE_STEP), 0) + LANES
    own_rank = lax.broadcasted_iota(i32, (own_acc.shape[0], EDGE_STEP), 0).astype(f32)
    ghost_rank = lax.broadcasted_iota(i32, (ghost_acc.shape[0], EDGE_STEP), 0).astype(f32)

    def step(number, carry):
        offset = pl.multiple_of(number * EDGE_STEP, EDGE_STEP)
        first = edges_ref[0:1, pl.ds(offset, EDGE_STEP)]
        second = edges_ref[1:2, pl.ds(offset, EDGE_STEP)]
        live = offset + lax.broadcasted_iota(i32, (1, EDGE_STEP), 1) < live_total
        first = jnp.where(live, first, -1)
        second = jnp.where(live, second, -1)
        first_hot = (own_lane == first).astype(f32)
        second_hot = (own_lane == second).astype(f32)
        ghost_hot = (ghost_lane == second).astype(f32)
        first_low = first_hot.astype(bf16)
        second_low = second_hot.astype(bf16)
        ghost_low = ghost_hot.astype(bf16)
        base = own_base[...]
        first_rank = jnp.sum(first_hot * (base + plain_dot(first_low, earlier)), axis=0, keepdims=True)
        base = base + plain_dot(first_low, every)
        second_rank = jnp.sum(second_hot * (base + plain_dot(second_low, earlier)), axis=0, keepdims=True)
        own_base[...] = base + plain_dot(second_low, every)
        base = ghost_base[...]
        second_rank += jnp.sum(ghost_hot * (base + plain_dot(ghost_low, earlier)), axis=0, keepdims=True)
        ghost_base[...] = base + plain_dot(ghost_low, every)
        first_code = (first - 160).astype(f32)
        second_code = (second - 160).astype(f32)
        place_first = jnp.where(own_rank == first_rank, second_code, 0.0).astype(bf16)
        place_second = jnp.where(own_rank == second_rank, first_code, 0.0).astype(bf16)
        place_ghost = jnp.where(ghost_rank == second_rank, first_code, 0.0).astype(bf16)
        own_acc[...] += nt_dot(place_first, first_low) + nt_dot(place_second, second_low)
        ghost_acc[:, 0:ghosts] += nt_dot(place_ghost, ghost_low)
        count_out[:, 0:LANES] += nt_dot(row, first_low) + nt_dot(row, second_low)
        count_out[:, LANES : LANES + ghosts] += nt_dot(row, ghost_low)
        return carry

    lax.fori_loop(0, (live_total + EDGE_STEP - 1) // EDGE_STEP, step, 0)
    own_code = (own_acc[0:OWN_ROWS, :] + 160.0).astype(i32)
    ghost_code = (ghost_acc[0:GHOST_ROWS, :] + 160.0).astype(i32)
    counts = count_out[0:1, :].astype(i32)
    own_live = lax.broadcasted_iota(i32, (OWN_ROWS, LANES), 0) < counts[:, 0:LANES]
    ghost_live = lax.broadcasted_iota(i32, ghost_code.shape, 0) < counts[:, LANES:]
    out_ref[...] = jnp.zeros_like(out_ref)
    out_ref[0:64, :] = features_ref[...].astype(f32)
    out_ref[64:67, :] = positions_ref[...]
    out_ref[OWN_AT : OWN_AT + OWN_ROWS, :] = jnp.where(own_live, own_code, 0).astype(f32)
    ghost_code = jnp.where(ghost_live, ghost_code, 0).astype(f32)
    out_ref[X_AT : X_AT + GHOST_ROWS, :] = ghost_code[:, 0:LANES]
    out_ref[Y_AT : Y_AT + GHOST_ROWS, :] = ghost_code[:, LANES:]
    for group in range(3):
        out_ref[COUNT_AT + group : COUNT_AT + group + 1, :] = count_out[0:1, group * LANES : (group + 1) * LANES]
    out_ref[SEND_AT : SEND_AT + 1, :] = send_x_ref[...].astype(f32)
    out_ref[SEND_AT + 1 : SEND_AT + 2, 0 : send_y_ref.shape[1]] = send_y_ref[...].astype(f32)


def make_payload(edge_list, edge_count, positions, features, send_list_x, send_list_y):
    ghosts = send_list_x.shape[0] + send_list_y.shape[0]
    vmem = pl.BlockSpec(memory_space=pltpu.VMEM)
    return pl.pallas_call(
        list_kernel,
        out_shape=jax.ShapeDtypeStruct((PAYLOAD, LANES), f32),
        in_specs=[pl.BlockSpec(memory_space=pltpu.SMEM)] + [vmem] * 5,
        out_specs=vmem,
        scratch_shapes=[
            pltpu.VMEM((8, 3 * LANES), f32),
            pltpu.VMEM((64, LANES), f32),
            pltpu.VMEM((32, 2 * LANES), f32),
            pltpu.VMEM((LANES, EDGE_STEP), f32),
            pltpu.VMEM((ghosts, EDGE_STEP), f32),
        ],
        compiler_params=pltpu.CompilerParams(vmem_limit_bytes=40 * 1024 * 1024),
    )(edge_count, edge_list, positions, features, send_list_x[None, :], send_list_y[None, :])


def spread_row(ref, row, rows):
    return jnp.broadcast_to(ref[pl.ds(row, 1), :], (rows, LANES))


def lookup(table_ref, row, tile0, tiles, slot, block):
    result = None
    for number in range(tiles):
        at = (tile0 + number) * LANES
        entries = jnp.broadcast_to(table_ref[row : row + 1, at : at + LANES], (8, LANES))
        value = jnp.take_along_axis(entries, slot, axis=1)
        result = value if result is None else jnp.where(block == number, value, result)
    return result


def sine_cosine(scaled):
    angle = math.pi * (scaled - 0.5)
    square = angle * angle
    cosine = 1.0
    sine = 1.0
    for order in range(7, 0, -1):
        cosine = 1.0 - square * cosine * (1.0 / ((2 * order - 1) * (2 * order)))
        sine = 1.0 - square * sine * (1.0 / ((2 * order) * (2 * order + 1)))
    return cosine, -(angle * sine)


def pair_geometry(table_ref, codes, live, tile0, tiles, target, basis, tangent, sines_ref, slopes_ref):
    slot = codes & (LANES - 1)
    block = codes >> 7
    relative = []
    for axis in range(3):
        partner = lookup(table_ref, 64 + axis, tile0, tiles, slot, block)
        here = jnp.broadcast_to(
            table_ref[64 + axis : 65 + axis, target * LANES : (target + 1) * LANES], (8, LANES)
        )
        relative.append(jnp.where(live, partner - here, 2.0 if axis == 0 else 0.0))
    distance = jnp.sqrt(relative[0] * relative[0] + relative[1] * relative[1] + relative[2] * relative[2])
    inverse = 1.0 / distance
    direction = [part * inverse for part in relative]
    inside = live & (distance < cutoff_radius)
    scaled = jnp.minimum(distance, cutoff_radius) * (1.0 / cutoff_radius)
    room = 1.0 - scaled * scaled
    envelope = jnp.where(inside, message_scale * room * room, 0.0)
    envelope_slope = jnp.where(inside, (-4.0 * message_scale / cutoff_radius) * scaled * room, 0.0)
    sine, cosine = sine_cosine(scaled)
    twice = 2.0 * cosine
    scale = math.sqrt(2.0 / cutoff_radius)
    last_sine, last_cosine = jnp.zeros_like(sine), jnp.ones_like(sine)
    for order in range(1, basis + 1):
        wave = scale * sine * inverse
        sines_ref[(order - 1) * 8 : order * 8, :] = wave
        if tangent:
            slope = (scale * order * math.pi / cutoff_radius) * cosine * inverse - wave * inverse
            slopes_ref[(order - 1) * 8 : order * 8, :] = slope
        sine, last_sine = twice * sine - last_sine, sine
        cosine, last_cosine = twice * cosine - last_cosine, cosine
    return direction, inverse, envelope, envelope_slope, inside


def split_rows(ref, basis):
    pieces = []
    for row in range(8):
        whole = ref[pl.ds(row, basis, stride=8), :]
        high = whole.astype(bf16).astype(f32)
        rest = whole - high
        middle = rest.astype(bf16).astype(f32)
        low = rest - middle
        pieces.append(jnp.concatenate([high, middle, high, middle, low, high], axis=0).astype(bf16))
    return jnp.concatenate(pieces, axis=1)


def high_low(value):
    high = value.astype(bf16)
    low = (value - high.astype(f32)).astype(bf16)
    return high, low


def shapes_of(direction):
    x, y, z = direction
    three, five, fifteen = math.sqrt(3.0), math.sqrt(5.0), math.sqrt(15.0)
    return [
        jnp.ones_like(x),
        three * x,
        three * y,
        three * z,
        fifteen * x * y,
        fifteen * y * z,
        0.5 * five * (3.0 * z * z - 1.0),
        fifteen * x * z,
        0.5 * fifteen * (x * x - y * y),
    ]


def hot_codes(codes_ref, size):
    columns = []
    lane = lax.broadcasted_iota(i32, (size, LANES), 0)
    for row in range(8):
        codes = jnp.broadcast_to(codes_ref[row : row + 1, :], (size, LANES))
        columns.append((lane == codes).astype(f32).astype(bf16))
    return jnp.concatenate(columns, axis=1)


def forward_group(refs, list_ref, count_row, tile0, tiles, target, lane0, out_ref):
    (table_ref, feature_ref, win_ref, wout_ref, codes_ref, sines_ref, env_ref, shape_ref, hidden_ref, radial_ref, partner_ref) = refs
    basis = win_ref.shape[1] // 6
    size = tiles * LANES
    first = tile0 * LANES
    count = count_row.astype(i32)
    steps = (jnp.max(count_row).astype(i32) + 7) // 8
    out_ref[:, lane0 : lane0 + LANES] = jnp.zeros((576, LANES), f32)

    def step(number, carry):
        offset = pl.multiple_of(number * 8, 8)
        codes = list_ref[pl.ds(offset, 8), :]
        live = (offset + lax.broadcasted_iota(i32, (8, LANES), 0) < count) & (codes >= 0)
        codes_ref[...] = codes
        direction, inverse, envelope, ignored, inside = pair_geometry(
            table_ref, codes, live, tile0, tiles, target, basis, False, sines_ref, None
        )
        env_ref[0:8, :] = envelope
        shapes = shapes_of(direction)
        for q in range(1, 9):
            shape_ref[q * 8 : q * 8 + 8, :] = shapes[q]
        value = plain_dot(win_ref[...], split_rows(sines_ref, basis))
        for row in range(8):
            part = value[:, row * LANES : (row + 1) * LANES]
            hidden = part / (1.0 + jnp.exp(-part)) * spread_row(env_ref, row, 64)
            high, low = high_low(hidden)
            hidden_ref[0:64, row * LANES : (row + 1) * LANES] = high
            hidden_ref[64:128, row * LANES : (row + 1) * LANES] = low
        hidden = hidden_ref[:, 0 : 8 * LANES]
        radial_ref[:, 0 : 8 * LANES] = plain_dot(wout_ref[...], jnp.concatenate([hidden, hidden], axis=0))
        partner_ref[...] = plain_dot(feature_ref[:, first : first + size], hot_codes(codes_ref, size))
        for block in range(8):
            sums = [
                out_ref[q * 64 + block * 8 : q * 64 + block * 8 + 8, lane0 : lane0 + LANES]
                for q in range(9)
            ]
            for row in range(8):
                lanes = slice(row * LANES, (row + 1) * LANES)
                feature = partner_ref[block * 8 : block * 8 + 8, lanes]
                for degree, (low, high) in enumerate(DEGREE_ROWS):
                    at = degree * 64 + block * 8
                    weight = radial_ref[at : at + 8, lanes] * feature
                    for q in range(low, high):
                        if q == 0:
                            sums[q] = sums[q] + weight
                        else:
                            sums[q] = sums[q] + weight * spread_row(shape_ref, q * 8 + row, 8)
            for q in range(9):
                out_ref[q * 64 + block * 8 : q * 64 + block * 8 + 8, lane0 : lane0 + LANES] = sums[q]
        return carry

    lax.fori_loop(0, steps, step, 0)


def backward_group(refs, list_ref, count_row, tile0, tiles, target, lane0, own_at, gradient_ref, force_ref, scatter_ref):
    (table_ref, feature_ref, win_ref, wout_ref, codes_ref, sines_ref, slopes_ref, env_ref, shape_ref, hidden_ref, radial_ref, partner_ref, pulled_ref, push_ref) = refs
    basis = win_ref.shape[1] // 6
    size = tiles * LANES
    first = tile0 * LANES
    wide = 8 * LANES
    count = count_row.astype(i32)
    steps = (jnp.max(count_row).astype(i32) + 7) // 8
    three, five, fifteen = math.sqrt(3.0), math.sqrt(5.0), math.sqrt(15.0)

    def step(number, carry):
        offset = pl.multiple_of(number * 8, 8)
        codes = list_ref[pl.ds(offset, 8), :]
        live = (offset + lax.broadcasted_iota(i32, (8, LANES), 0) < count) & (codes >= 0)
        codes_ref[...] = codes
        direction, inverse, envelope, envelope_slope, inside = pair_geometry(
            table_ref, codes, live, tile0, tiles, target, basis, True, sines_ref, slopes_ref
        )
        env_ref[0:8, :] = envelope
        env_ref[8:16, :] = envelope_slope
        shapes = shapes_of(direction)
        for q in range(1, 9):
            shape_ref[q * 8 : q * 8 + 8, :] = shapes[q]
        both = jnp.concatenate([split_rows(sines_ref, basis), split_rows(slopes_ref, basis)], axis=1)
        value = plain_dot(win_ref[...], both)
        for row in range(8):
            lanes = slice(row * LANES, (row + 1) * LANES)
            later = slice(wide + row * LANES, wide + (row + 1) * LANES)
            part, part_slope = value[:, lanes], value[:, later]
            gate = 1.0 / (1.0 + jnp.exp(-part))
            hidden = part * gate
            hidden_slope = gate * (1.0 + part * (1.0 - gate)) * part_slope
            scale = spread_row(env_ref, row, 64)
            scale_slope = spread_row(env_ref, 8 + row, 64)
            high, low = high_low(hidden * scale)
            hidden_ref[0:64, lanes] = high
            hidden_ref[64:128, lanes] = low
            high, low = high_low(hidden * scale_slope + hidden_slope * scale)
            hidden_ref[0:64, later] = high
            hidden_ref[64:128, later] = low
        hidden = hidden_ref[...]
        radial_ref[...] = plain_dot(wout_ref[...], jnp.concatenate([hidden, hidden], axis=0))
        hot = hot_codes(codes_ref, size)
        partner_ref[...] = plain_dot(feature_ref[:, first : first + size], hot)
        for row in range(8):
            lanes = slice(row * LANES, (row + 1) * LANES)
            later = slice(wide + row * LANES, wide + (row + 1) * LANES)
            pulled = [jnp.zeros((8, LANES), f32) for q in range(9)]
            spoke = jnp.zeros((8, LANES), f32)
            for block in range(8):
                feature = partner_ref[block * 8 : block * 8 + 8, lanes]
                for degree, (low, high) in enumerate(DEGREE_ROWS):
                    at = degree * 64 + block * 8
                    weight = radial_ref[at : at + 8, lanes] * feature
                    weight_slope = radial_ref[at : at + 8, later] * feature
                    mixed = None
                    for q in range(low, high):
                        gradient = gradient_ref[q * 64 + block * 8 : q * 64 + block * 8 + 8, lane0 : lane0 + LANES]
                        if q > 0:
                            pulled[q] = pulled[q] + weight * gradient
                            gradient = gradient * spread_row(shape_ref, q * 8 + row, 8)
                        mixed = gradient if mixed is None else mixed + gradient
                    spoke = spoke + weight_slope * mixed
            for q in range(1, 9):
                pulled_ref[q * 8 + row : q * 8 + row + 1, :] = jnp.sum(pulled[q], axis=0, keepdims=True)
            pulled_ref[row : row + 1, :] = jnp.sum(spoke, axis=0, keepdims=True)
        x, y, z = direction
        p = [pulled_ref[q * 8 : q * 8 + 8, :] for q in range(9)]
        turn = [
            three * p[1] + fifteen * (y * p[4] + z * p[7] + x * p[8]),
            three * p[2] + fifteen * (x * p[4] + z * p[5] - y * p[8]),
            three * p[3] + fifteen * (y * p[5] + x * p[7]) + (3.0 * five) * z * p[6],
        ]
        along = x * turn[0] + y * turn[1] + z * turn[2]
        for axis in range(3):
            part = (turn[axis] - direction[axis] * along) * inverse + direction[axis] * p[0]
            part = jnp.where(inside, part, 0.0)
            if force_ref is not None:
                force_ref[axis : axis + 1, :] += jnp.sum(part, axis=0, keepdims=True)
            high = part.astype(bf16).astype(f32)
            push_ref[axis * 8 : axis * 8 + 8, :] = high
            push_ref[24 + axis * 8 : 32 + axis * 8, :] = part - high
        push = jnp.concatenate([push_ref[pl.ds(row, 8, stride=8), :] for row in range(8)], axis=1)
        scatter_ref[...] += nt_dot(push.astype(bf16), hot[own_at * LANES : (own_at + 1) * LANES, :])
        return carry

    lax.fori_loop(0, steps, step, 0)


def rounded(value):
    return lax.reduce_precision(value, 8, 7)


def stacked_weights(radial_in, radial_out):
    high = rounded(radial_in)
    middle = rounded(radial_in - high)
    low = rounded(radial_in - high - middle)
    win = jnp.concatenate([high, high, middle, middle, high, low], axis=1).astype(bf16)
    high = rounded(radial_out)
    low = rounded(radial_out - high)
    wout = jnp.concatenate([high, high, low, low], axis=1).astype(bf16)
    return win, wout


HALF = LANES // 2
QUARTER = LANES // 4
MIDDLE = 4
AROUND = (0, 1, 2, 6, 7, 8)
TILE_OF = {0: 0, 1: 1, 2: 2, 6: 3, 7: 4, 8: 5, 3: 6, 5: 7, 4: 8}
TILE_LR, TILE_OWN, TILE_X, TILE_Y, TILES = 9, 10, 11, 12, 13
LIST_ROWS = 64


def rep(row):
    return jnp.broadcast_to(row, (8, LANES))


def tall(value, rows):
    return jnp.concatenate([value] * (rows // 8), axis=0)


def pick(values, slots):
    return jnp.take_along_axis(values, tall(slots, values.shape[0]) if slots.shape[0] != values.shape[0] else slots, axis=1)


def merge(base, count, segment, more):
    rows = base.shape[0]
    if segment.shape[0] < rows:
        segment = jnp.concatenate([segment, jnp.zeros((rows - segment.shape[0], LANES), i32)], axis=0)
    shift = tall(count, rows)
    for bit in (1, 2, 4, 8, 16, 32):
        segment = jnp.where((shift & bit) != 0, pltpu.roll(segment, bit, axis=0), segment)
    row = lax.broadcasted_iota(i32, (rows, LANES), 0)
    return jnp.where(row < shift, base, segment), count + more


def join(pieces):
    codes, count = pieces[0]
    for other, number in pieces[1:]:
        codes = jnp.where(tall(number, other.shape[0]) > 0, other, codes)
        count = count + number
    return codes, count


def main_kernel(strip_ref, low_ref, high_ref, win_ref, wout_ref, mix_ref, outw_ref, species_ref, kind_ref,
                energy_ref, force_out, table_ref, feature_ref, column_ref, list_own, list_x, list_y, back_x, back_y,
                sums_ref, force_ref, scatter_ref, codes_ref, sines_ref, slopes_ref, env_ref, shape_ref, hidden_ref,
                radial_ref, partner_ref, pulled_ref, push_ref):
    refs = (low_ref, strip_ref, high_ref)

    def rows_of(block, at, size):
        start = (block % 3) * PAYLOAD + at
        return refs[block // 3][start : start + size, :]

    def row_of(block, at):
        return rep(rows_of(block, at, 1).astype(i32))

    lane = lax.broadcasted_iota(i32, (8, LANES), 1)
    none = jnp.full((8, LANES), -1, i32)

    x_home = {}
    for block in range(9):
        dx = block % 3
        lower = (block - 1) * LANES + pltpu.roll(row_of(block - 1, SEND_AT), HALF, axis=1) if dx > 0 else none
        upper = (block + 1) * LANES + pltpu.roll(row_of(block + 1, SEND_AT), HALF, axis=1) if dx < 2 else none
        x_home[block] = jnp.where(lane < HALF, lower, upper)

    def section_home(block, entry):
        copies = jnp.take_along_axis(x_home[block], entry & (LANES - 1), axis=1)
        return jnp.where(entry < LANES, block * LANES + entry, copies)

    y_home = {}
    for block in range(9):
        dy = block // 3
        if dy > 0:
            lower = section_home(block - 3, pltpu.roll(row_of(block - 3, SEND_AT + 1), LANES - QUARTER, axis=1))
        else:
            lower = none
        if dy < 2:
            upper = section_home(block + 3, pltpu.roll(row_of(block + 3, SEND_AT + 1), QUARTER, axis=1))
        else:
            upper = none
        y_home[block] = jnp.where(lane < QUARTER, lower, jnp.where(lane < HALF, upper, none))

    x_here = x_home[MIDDLE]
    y_here = y_home[MIDDLE]
    y_twice = jnp.where(lane < HALF, y_here, pltpu.roll(y_here, HALF, axis=1))
    y_sides = jnp.where(lane < HALF, y_home[3], pltpu.roll(y_home[5], HALF, axis=1))

    column_ref[...] = jnp.zeros_like(column_ref)
    slots = {}

    def as_column(name, value):
        slots[name] = len(slots)
        column_ref[slots[name] : slots[name] + 1, :] = value[0:1, :].astype(f32)

    as_column("sent", row_of(MIDDLE, SEND_AT))
    as_column("x", x_here)
    as_column("y", y_here)
    as_column("sides", y_sides)
    for block in range(9):
        if block != MIDDLE:
            as_column(("y", block), y_home[block])
    for block in AROUND:
        as_column(("x", block), x_home[block])
    columns = jnp.transpose(column_ref[...])
    place = lax.broadcasted_iota(i32, (LANES, LANES), 0).astype(f32)

    def match(name, target, low=0, high=LANES):
        number = slots[name]
        same = columns[low:high, number : number + 1] == target[0:1, :].astype(f32)
        return rep(jnp.max(jnp.where(same, place[low:high, :], -1.0), axis=0, keepdims=True).astype(i32))

    def gathered(home, blocks, rows, at):
        block_of = home >> 7
        slot = home & (LANES - 1)
        result = jnp.zeros((rows, LANES), f32)
        for block in blocks:
            result = jnp.where(tall(block_of, rows) == block, pick(rows_of(block, at, rows), slot), result)
        return result

    for block, tile in TILE_OF.items():
        table_ref[:, tile * LANES : (tile + 1) * LANES] = rows_of(block, 0, 72)
    table_ref[:, TILE_OWN * LANES : (TILE_OWN + 1) * LANES] = rows_of(MIDDLE, 0, 72)
    table_ref[:, TILE_X * LANES : (TILE_X + 1) * LANES] = gathered(x_here, (3, 5), 72, 0)
    table_ref[:, TILE_Y * LANES : (TILE_Y + 1) * LANES] = gathered(y_twice, AROUND, 72, 0)
    table_ref[:, TILE_LR * LANES : (TILE_LR + 1) * LANES] = gathered(y_sides, AROUND, 72, 0)
    feature_ref[...] = table_ref[0:64, :].astype(bf16)

    def aligned(block, at, rows, count_at, found):
        at_lane = jnp.maximum(found, 0)
        codes = pick(rows_of(block, at, rows).astype(i32), at_lane)
        count = jnp.take_along_axis(row_of(block, count_at), at_lane, axis=1)
        return codes, jnp.where(found >= 0, count, 0)

    def renamed(codes, table, offset):
        found = pick(jnp.concatenate([table] * (codes.shape[0] // 8), axis=0), codes & (LANES - 1))
        return jnp.where(found >= 0, found + offset, -1)

    own_home = MIDDLE * LANES + lane
    codes = jnp.concatenate([rows_of(MIDDLE, OWN_AT, OWN_ROWS).astype(i32), jnp.zeros((LIST_ROWS - OWN_ROWS, LANES), i32)], axis=0)
    count = row_of(MIDDLE, COUNT_AT)
    found_low = match("sent", lane, 0, HALF)
    found_low = jnp.where(found_low >= 0, found_low + HALF, -1)
    found_high = match("sent", lane, HALF, LANES)
    found_high = jnp.where(found_high >= 0, found_high - HALF, -1)
    pieces = []
    for block, found in ((3, found_low), (5, found_high)):
        piece, number = aligned(block, X_AT, GHOST_ROWS, COUNT_AT + 1, found)
        pieces.append((renamed(piece, match("x", block * LANES + lane), LANES), number))
    codes, count = merge(codes, count, *join(pieces))
    y_lane = {block: match("y", block * LANES + lane) for block in AROUND}
    for blocks in ((1, 7), (0, 2, 6, 8)):
        pieces = []
        for block in blocks:
            piece, number = aligned(block, Y_AT, GHOST_ROWS, COUNT_AT + 2, match(("y", block), own_home, 0, HALF))
            pieces.append((renamed(piece, y_lane[block], 2 * LANES), number))
        codes, count = merge(codes, count, *join(pieces))
    list_own[...] = codes
    count_own = count

    pieces = []
    for block, tile in ((3, 0), (5, 1)):
        found = jnp.where(x_here >> 7 == block, x_here & (LANES - 1), -1)
        piece, number = aligned(block, OWN_AT, OWN_ROWS, COUNT_AT, found)
        home = pick(jnp.concatenate([x_home[block]] * (OWN_ROWS // 8), axis=0), piece & (LANES - 1))
        copy = jnp.where(home >> 7 == MIDDLE, 2 * LANES + (home & (LANES - 1)), -1)
        piece = jnp.where(
            piece < LANES, piece + tile * LANES, jnp.where(piece < 2 * LANES, copy, piece + LANES + tile * HALF)
        )
        pieces.append((piece, number))
    codes, count = join(pieces)
    codes = jnp.concatenate([codes, jnp.zeros((LIST_ROWS - OWN_ROWS, LANES), i32)], axis=0)
    codes, count = merge(
        codes, count, rows_of(MIDDLE, X_AT, GHOST_ROWS).astype(i32) + 2 * LANES, row_of(MIDDLE, COUNT_AT + 1)
    )
    side_lane = {block: match("sides", block * LANES + lane) for block in AROUND}
    for blocks in ((1, 7), (0, 2, 6, 8)):
        pieces = []
        for block in blocks:
            piece, number = aligned(block, Y_AT, GHOST_ROWS, COUNT_AT + 2, match(("y", block), x_here, 0, HALF))
            pieces.append((renamed(piece, side_lane[block], 3 * LANES), number))
        codes, count = merge(codes, count, *join(pieces))
    list_x[...] = codes
    count_x = count

    def tiled(home):
        block = home >> 7
        tile = jnp.where(block < 3, block, jnp.where(block > 5, block - 3, jnp.where(block == 3, 6, jnp.where(block == 5, 7, 8))))
        return jnp.where(home >= 0, tile * LANES + (home & (LANES - 1)), -1)

    pieces = []
    for block in AROUND:
        found = jnp.where(y_here >> 7 == block, y_here & (LANES - 1), -1)
        piece, number = aligned(block, OWN_AT, OWN_ROWS, COUNT_AT, found)
        slot = piece & (LANES - 1)
        copy_x = pick(jnp.concatenate([tiled(x_home[block])] * (OWN_ROWS // 8), axis=0), slot)
        copy_y = pick(jnp.concatenate([tiled(y_home[block])] * (OWN_ROWS // 8), axis=0), slot)
        piece = jnp.where(
            piece < LANES, piece + TILE_OF[block] * LANES, jnp.where(piece < 2 * LANES, copy_x, copy_y)
        )
        pieces.append((piece, number))
    codes, count = join(pieces)
    codes = jnp.concatenate([codes, jnp.zeros((LIST_ROWS - OWN_ROWS, LANES), i32)], axis=0)
    pieces = []
    for block in AROUND:
        piece, number = aligned(block, X_AT, GHOST_ROWS, COUNT_AT + 1, match(("x", block), y_here))
        pieces.append((piece + TILE_OF[block] * LANES, number))
    codes, count = merge(codes, count, *join(pieces))
    codes, count = merge(
        codes, count, rows_of(MIDDLE, Y_AT, GHOST_ROWS).astype(i32) + TILE_OF[MIDDLE] * LANES, row_of(MIDDLE, COUNT_AT + 2)
    )
    pieces = []
    for block in (3, 5):
        piece, number = aligned(block, Y_AT, GHOST_ROWS, COUNT_AT + 2, match(("y", block), y_here, 0, HALF))
        pieces.append((piece + TILE_OF[block] * LANES, number))
    codes, count = merge(codes, count, *join(pieces))
    count = jnp.where(lane < HALF, count, 0)
    codes_y, count_y = codes, count
    split = GHOST_ROWS
    half = tall(lane, split + 8) < HALF
    list_y[...] = jnp.where(half, codes[0 : split + 8, :], pltpu.roll(codes[split : LIST_ROWS - 8, :], HALF, axis=1))
    count_pack = jnp.where(
        lane < HALF, jnp.minimum(count, split), jnp.maximum(pltpu.roll(count, HALF, axis=1) - split, 0)
    )

    earlier = (
        lax.broadcasted_iota(i32, (LIST_ROWS, LIST_ROWS), 1) < lax.broadcasted_iota(i32, (LIST_ROWS, LIST_ROWS), 0)
    ).astype(f32).astype(bf16)
    row = lax.broadcasted_iota(i32, (LIST_ROWS, LANES), 0)

    def own_partners(codes, count, first, out_ref):
        kept = (row < tall(count, LIST_ROWS)) & (codes >= first) & (codes < first + LANES)
        weight = kept.astype(f32)
        rank = jnp.where(kept, plain_dot(earlier, weight.astype(bf16)), -1.0)
        value = (codes - first).astype(f32)
        for number in range(GHOST_ROWS):
            out_ref[number : number + 1, :] = jnp.sum(
                jnp.where(rank == float(number), value, 0.0), axis=0, keepdims=True
            ).astype(i32)
        return rep(jnp.sum(weight, axis=0, keepdims=True))

    count_back_x = own_partners(list_x[...], count_x, 2 * LANES, back_x)
    count_back_y = own_partners(codes_y, count_y, TILE_OF[MIDDLE] * LANES, back_y)

    wide = 8 * LANES
    scratch = (table_ref, feature_ref, win_ref, wout_ref, codes_ref, sines_ref, env_ref, shape_ref, hidden_ref, radial_ref, partner_ref)
    forward_group(scratch, list_own, count_own.astype(f32), TILE_OWN, 3, TILE_OWN, 0, sums_ref)
    forward_group(scratch, list_x, count_x.astype(f32), 6, 4, TILE_X, LANES, sums_ref)
    forward_group(scratch, list_y, count_pack.astype(f32), 0, 9, TILE_Y, 2 * LANES, sums_ref)
    sums_y = sums_ref[:, 2 * LANES : 3 * LANES]
    sums_ref[:, 2 * LANES : 3 * LANES] = sums_y + pltpu.roll(sums_y, HALF, axis=1)

    sums = sums_ref[...]
    square = sums * sums
    degree_one = square[64:128] + square[128:192] + square[192:256]
    degree_two = square[256:320] + square[320:384] + square[384:448] + square[448:512] + square[512:576]
    invariant = jnp.concatenate([square[0:64], degree_one, degree_two], axis=0)
    mixed = lax.dot_general(
        mix_ref[...], invariant, (((1,), (0,)), ((), ())), precision=highest, preferred_element_type=f32
    ) + table_ref[0:64, TILE_OWN * LANES : (TILE_Y + 1) * LANES]
    gate = 1.0 / (1.0 + jnp.exp(-mixed))
    weight = outw_ref[...]
    energy = jnp.sum(weight * (mixed * gate)[:, 0:LANES], axis=0, keepdims=True)
    kinds = species_ref[...]
    for kind in range(kind_ref.shape[0]):
        energy = energy + jnp.where(kinds == kind, kind_ref[kind], 0.0)
    energy_ref[...] = energy
    slope = weight * (gate * (1.0 + mixed * (1.0 - gate)))
    pulled = 2.0 * lax.dot_general(
        mix_ref[...], slope, (((0,), (0,)), ((), ())), precision=highest, preferred_element_type=f32
    )
    for q in range(9):
        degree = (0, 1, 1, 1, 2, 2, 2, 2, 2)[q]
        sums_ref[q * 64 : q * 64 + 64, :] = sums[q * 64 : q * 64 + 64] * pulled[degree * 64 : degree * 64 + 64]

    force_ref[...] = jnp.zeros_like(force_ref)
    scatter_ref[...] = jnp.zeros_like(scatter_ref)
    push_ref[...] = jnp.zeros_like(push_ref)
    scratch = (table_ref, feature_ref, win_ref, wout_ref, codes_ref, sines_ref, slopes_ref, env_ref, shape_ref, hidden_ref, radial_ref, partner_ref, pulled_ref, push_ref)
    backward_group(scratch, list_own, count_own.astype(f32), TILE_OWN, 3, TILE_OWN, 0, 0, sums_ref, force_ref, scatter_ref)
    backward_group(scratch, back_x, count_back_x, TILE_OWN, 1, TILE_X, LANES, 0, sums_ref, None, scatter_ref)
    backward_group(scratch, back_y, count_back_y, TILE_OWN, 1, TILE_Y, 2 * LANES, 0, sums_ref, None, scatter_ref)
    force_out[...] = force_ref[0:3, :] - scatter_ref[0:3, :] - scatter_ref[3:6, :]


def main_pass(strip, low, high, win, wout, mix_weight, out_weight, species, species_energy):
    vmem = pl.BlockSpec(memory_space=pltpu.VMEM)
    wide = 8 * LANES
    return pl.pallas_call(
        main_kernel,
        out_shape=(jax.ShapeDtypeStruct((1, LANES), f32), jax.ShapeDtypeStruct((3, LANES), f32)),
        in_specs=[vmem] * 8 + [pl.BlockSpec(memory_space=pltpu.SMEM)],
        out_specs=(vmem, vmem),
        scratch_shapes=[
            pltpu.VMEM((72, TILES * LANES), f32),
            pltpu.VMEM((64, TILES * LANES), bf16),
            pltpu.VMEM((LANES, LANES), f32),
            pltpu.VMEM((LIST_ROWS, LANES), i32),
            pltpu.VMEM((LIST_ROWS, LANES), i32),
            pltpu.VMEM((32, LANES), i32),
            pltpu.VMEM((GHOST_ROWS, LANES), i32),
            pltpu.VMEM((GHOST_ROWS, LANES), i32),
            pltpu.VMEM((576, 3 * LANES), f32),
            pltpu.VMEM((8, LANES), f32),
            pltpu.VMEM((8, LANES), f32),
            pltpu.VMEM((8, LANES), i32),
            pltpu.VMEM((64, LANES), f32),
            pltpu.VMEM((64, LANES), f32),
            pltpu.VMEM((16, LANES), f32),
            pltpu.VMEM((72, LANES), f32),
            pltpu.VMEM((128, 2 * wide), bf16),
            pltpu.VMEM((192, 2 * wide), f32),
            pltpu.VMEM((64, wide), f32),
            pltpu.VMEM((72, LANES), f32),
            pltpu.VMEM((64, LANES), f32),
        ],
        compiler_params=pltpu.CompilerParams(vmem_limit_bytes=48 * 1024 * 1024),
    )(strip, low, high, win, wout, mix_weight, out_weight[:, None], species[None, :], species_energy)


def from_both_sides(block, axis):
    count = lax.axis_size(axis)
    up = [(i, (i + 1) % count) for i in range(count)]
    down = [(target, source) for source, target in up]
    return lax.ppermute(block, axis, up), lax.ppermute(block, axis, down)


def local(
    positions, features, species, edge_list, edge_count, send_list_x, send_list_y,
    radial_in, radial_out, mix_weight, out_weight, species_energy,
):
    own = make_payload(edge_list, edge_count, positions, features, send_list_x, send_list_y)
    left, right = from_both_sides(own, "gx")
    strip = jnp.concatenate([left, own, right], axis=0)
    low, high = from_both_sides(strip, "gy")
    win, wout = stacked_weights(radial_in, radial_out)
    energies, forces = main_pass(strip, low, high, win, wout, mix_weight, out_weight, species, species_energy)
    return energies[0], forces


def solution(mesh):
    placed = (
        P(None, ("gx", "gy")), P(None, ("gx", "gy")), P(("gx", "gy")), P(None, ("gx", "gy")), P(("gx", "gy")),
        P(("gx", "gy")), P(("gx", "gy")), P(), P(), P(), P(), P(),
    )
    return jax.shard_map(
        local, mesh=mesh, in_specs=placed, out_specs=(P(("gx", "gy")), P(None, ("gx", "gy"))), check_vma=False,
    )
```

```python
import math

import jax
import jax.numpy as jnp
import numpy as np
from jax import lax
from jax.experimental import pallas as pl
from jax.experimental.pallas import tpu as pltpu
from jax.sharding import PartitionSpec as P

cutoff_radius = 5.0
message_scale = 0.3
highest = lax.Precision.HIGHEST
f32 = jnp.float32
bf16 = jnp.bfloat16
i32 = jnp.int32

LANES = 128
EDGE_STEP = 256
OWN_ROWS = 56
GHOST_ROWS = 24
OWN_AT, X_AT, Y_AT, COUNT_AT, SEND_AT, PAYLOAD = 72, 128, 152, 176, 179, 184
DEGREE_ROWS = ((0, 1), (1, 4), (4, 9))


def nt_dot(left, right):
    return lax.dot_general(left, right, (((1,), (1,)), ((), ())), preferred_element_type=f32)


def plain_dot(left, right):
    return lax.dot_general(left, right, (((1,), (0,)), ((), ())), preferred_element_type=f32)


def list_kernel(count_ref, edges_ref, positions_ref, features_ref, send_x_ref, send_y_ref, out_ref, count_out, own_acc, ghost_acc, own_base, ghost_base):
    ghosts = ghost_base.shape[0]
    live_total = count_ref[0]
    own_acc[...] = jnp.zeros_like(own_acc)
    ghost_acc[...] = jnp.zeros_like(ghost_acc)
    own_base[...] = jnp.zeros_like(own_base)
    ghost_base[...] = jnp.zeros_like(ghost_base)
    count_out[...] = jnp.zeros_like(count_out)
    before = lax.broadcasted_iota(i32, (EDGE_STEP, EDGE_STEP), 0) < lax.broadcasted_iota(
        i32, (EDGE_STEP, EDGE_STEP), 1
    )
    earlier = before.astype(f32).astype(bf16)
    every = jnp.ones((EDGE_STEP, EDGE_STEP), bf16)
    row = jnp.ones((8, EDGE_STEP), bf16)
    own_lane = lax.broadcasted_iota(i32, (LANES, EDGE_STEP), 0)
    ghost_lane = lax.broadcasted_iota(i32, (ghosts, EDGE_STEP), 0) + LANES
    own_rank = lax.broadcasted_iota(i32, (own_acc.shape[0], EDGE_STEP), 0).astype(f32)
    ghost_rank = lax.broadcasted_iota(i32, (ghost_acc.shape[0], EDGE_STEP), 0).astype(f32)

    def step(number, carry):
        offset = pl.multiple_of(number * EDGE_STEP, EDGE_STEP)
        first = edges_ref[0:1, pl.ds(offset, EDGE_STEP)]
        second = edges_ref[1:2, pl.ds(offset, EDGE_STEP)]
        live = offset + lax.broadcasted_iota(i32, (1, EDGE_STEP), 1) < live_total
        first = jnp.where(live, first, -1)
        second = jnp.where(live, second, -1)
        first_hot = (own_lane == first).astype(f32)
        second_hot = (own_lane == second).astype(f32)
        ghost_hot = (ghost_lane == second).astype(f32)
        first_low = first_hot.astype(bf16)
        second_low = second_hot.astype(bf16)
        ghost_low = ghost_hot.astype(bf16)
        base = own_base[...]
        first_rank = jnp.sum(first_hot * (base + plain_dot(first_low, earlier)), axis=0, keepdims=True)
        base = base + plain_dot(first_low, every)
        second_rank = jnp.sum(second_hot * (base + plain_dot(second_low, earlier)), axis=0, keepdims=True)
        own_base[...] = base + plain_dot(second_low, every)
        base = ghost_base[...]
        second_rank += jnp.sum(ghost_hot * (base + plain_dot(ghost_low, earlier)), axis=0, keepdims=True)
        ghost_base[...] = base + plain_dot(ghost_low, every)
        first_code = (first - 160).astype(f32)
        second_code = (second - 160).astype(f32)
        place_first = jnp.where(own_rank == first_rank, second_code, 0.0).astype(bf16)
        place_second = jnp.where(own_rank == second_rank, first_code, 0.0).astype(bf16)
        place_ghost = jnp.where(ghost_rank == second_rank, first_code, 0.0).astype(bf16)
        own_acc[...] += nt_dot(place_first, first_low) + nt_dot(place_second, second_low)
        ghost_acc[:, 0:ghosts] += nt_dot(place_ghost, ghost_low)
        count_out[:, 0:LANES] += nt_dot(row, first_low) + nt_dot(row, second_low)
        count_out[:, LANES : LANES + ghosts] += nt_dot(row, ghost_low)
        return carry

    lax.fori_loop(0, (live_total + EDGE_STEP - 1) // EDGE_STEP, step, 0)
    own_code = (own_acc[0:OWN_ROWS, :] + 160.0).astype(i32)
    ghost_code = (ghost_acc[0:GHOST_ROWS, :] + 160.0).astype(i32)
    counts = count_out[0:1, :].astype(i32)
    own_live = lax.broadcasted_iota(i32, (OWN_ROWS, LANES), 0) < counts[:, 0:LANES]
    ghost_live = lax.broadcasted_iota(i32, ghost_code.shape, 0) < counts[:, LANES:]
    out_ref[...] = jnp.zeros_like(out_ref)
    out_ref[0:64, :] = features_ref[...].astype(f32)
    out_ref[64:67, :] = positions_ref[...]
    out_ref[OWN_AT : OWN_AT + OWN_ROWS, :] = jnp.where(own_live, own_code, 0).astype(f32)
    ghost_code = jnp.where(ghost_live, ghost_code, 0).astype(f32)
    out_ref[X_AT : X_AT + GHOST_ROWS, :] = ghost_code[:, 0:LANES]
    out_ref[Y_AT : Y_AT + GHOST_ROWS, :] = ghost_code[:, LANES:]
    for group in range(3):
        out_ref[COUNT_AT + group : COUNT_AT + group + 1, :] = count_out[0:1, group * LANES : (group + 1) * LANES]
    out_ref[SEND_AT : SEND_AT + 1, :] = send_x_ref[...].astype(f32)
    out_ref[SEND_AT + 1 : SEND_AT + 2, 0 : send_y_ref.shape[1]] = send_y_ref[...].astype(f32)


def make_payload(edge_list, edge_count, positions, features, send_list_x, send_list_y):
    ghosts = send_list_x.shape[0] + send_list_y.shape[0]
    vmem = pl.BlockSpec(memory_space=pltpu.VMEM)
    return pl.pallas_call(
        list_kernel,
        out_shape=jax.ShapeDtypeStruct((PAYLOAD, LANES), f32),
        in_specs=[pl.BlockSpec(memory_space=pltpu.SMEM)] + [vmem] * 5,
        out_specs=vmem,
        scratch_shapes=[
            pltpu.VMEM((8, 3 * LANES), f32),
            pltpu.VMEM((64, LANES), f32),
            pltpu.VMEM((32, 2 * LANES), f32),
            pltpu.VMEM((LANES, EDGE_STEP), f32),
            pltpu.VMEM((ghosts, EDGE_STEP), f32),
        ],
        compiler_params=pltpu.CompilerParams(vmem_limit_bytes=40 * 1024 * 1024),
    )(edge_count, edge_list, positions, features, send_list_x[None, :], send_list_y[None, :])


def spread_row(ref, row, rows):
    return jnp.broadcast_to(ref[pl.ds(row, 1), :], (rows, LANES))


def lookup(table_ref, row, tile0, tiles, slot, block):
    result = None
    for number in range(tiles):
        at = (tile0 + number) * LANES
        entries = jnp.broadcast_to(table_ref[row : row + 1, at : at + LANES], (8, LANES))
        value = jnp.take_along_axis(entries, slot, axis=1)
        result = value if result is None else jnp.where(block == number, value, result)
    return result


def sine_cosine(scaled):
    angle = math.pi * (scaled - 0.5)
    square = angle * angle
    cosine = 1.0
    sine = 1.0
    for order in range(7, 0, -1):
        cosine = 1.0 - square * cosine * (1.0 / ((2 * order - 1) * (2 * order)))
        sine = 1.0 - square * sine * (1.0 / ((2 * order) * (2 * order + 1)))
    return cosine, -(angle * sine)


def pair_geometry(table_ref, codes, live, tile0, tiles, target, basis, tangent, sines_ref, slopes_ref):
    slot = codes & (LANES - 1)
    block = codes >> 7
    relative = []
    for axis in range(3):
        partner = lookup(table_ref, 64 + axis, tile0, tiles, slot, block)
        here = jnp.broadcast_to(
            table_ref[64 + axis : 65 + axis, target * LANES : (target + 1) * LANES], (8, LANES)
        )
        relative.append(jnp.where(live, partner - here, 2.0 if axis == 0 else 0.0))
    distance = jnp.sqrt(relative[0] * relative[0] + relative[1] * relative[1] + relative[2] * relative[2])
    inverse = 1.0 / distance
    direction = [part * inverse for part in relative]
    inside = live & (distance < cutoff_radius)
    scaled = jnp.minimum(distance, cutoff_radius) * (1.0 / cutoff_radius)
    room = 1.0 - scaled * scaled
    envelope = jnp.where(inside, message_scale * room * room, 0.0)
    envelope_slope = jnp.where(inside, (-4.0 * message_scale / cutoff_radius) * scaled * room, 0.0)
    sine, cosine = sine_cosine(scaled)
    twice = 2.0 * cosine
    scale = math.sqrt(2.0 / cutoff_radius)
    last_sine, last_cosine = jnp.zeros_like(sine), jnp.ones_like(sine)
    for order in range(1, basis + 1):
        wave = scale * sine * inverse
        sines_ref[(order - 1) * 8 : order * 8, :] = wave
        if tangent:
            slope = (scale * order * math.pi / cutoff_radius) * cosine * inverse - wave * inverse
            slopes_ref[(order - 1) * 8 : order * 8, :] = slope
        sine, last_sine = twice * sine - last_sine, sine
        cosine, last_cosine = twice * cosine - last_cosine, cosine
    return direction, inverse, envelope, envelope_slope, inside


def split_rows(ref, basis, at):
    pieces = []
    for row in range(8):
        whole = ref[pl.ds(at + row, basis, stride=8), :]
        high = whole.astype(bf16).astype(f32)
        rest = whole - high
        middle = rest.astype(bf16).astype(f32)
        low = rest - middle
        pieces.append(jnp.concatenate([high, middle, high, middle, low, high], axis=0).astype(bf16))
    return jnp.concatenate(pieces, axis=1)


def high_low(value):
    high = value.astype(bf16)
    low = (value - high.astype(f32)).astype(bf16)
    return high, low


def shapes_of(direction):
    x, y, z = direction
    three, five, fifteen = math.sqrt(3.0), math.sqrt(5.0), math.sqrt(15.0)
    return [
        jnp.ones_like(x),
        three * x,
        three * y,
        three * z,
        fifteen * x * y,
        fifteen * y * z,
        0.5 * five * (3.0 * z * z - 1.0),
        fifteen * x * z,
        0.5 * fifteen * (x * x - y * y),
    ]


def hot_codes(list_ref, offset, size, first):
    columns = []
    lane = lax.broadcasted_iota(i32, (size, LANES), 0) + first
    for row in range(8):
        codes = jnp.broadcast_to(list_ref[pl.ds(offset + row, 1), :], (size, LANES))
        columns.append((lane == codes).astype(f32).astype(bf16))
    return jnp.concatenate(columns, axis=1)


def forward_pairs(refs, list_ref, count_row, tile0, tiles, target, lane0, slot0, tangent, start, stop, out_ref):
    (table_ref, feature_ref, win_ref, wout_ref, sines_ref, slopes_ref, env_ref, shape_ref, geometry_ref, hidden_ref, radial_ref, partner_ref) = refs
    basis = win_ref.shape[1] // 6
    size = tiles * LANES
    first = tile0 * LANES
    wide = 8 * LANES
    count = count_row.astype(i32)
    rows_in = 8 * basis

    def step(number, carry):
        both = (0, 1)
        offset = [pl.multiple_of(number * 16 + part * 8, 8) for part in both]
        slot = [slot0 + part + (number * 2 if tangent else 0) for part in both]
        for part in both:
            codes = list_ref[pl.ds(offset[part], 8), :]
            live = (offset[part] + lax.broadcasted_iota(i32, (8, LANES), 0) < count) & (codes >= 0)
            direction, inverse, envelope, envelope_slope, inside = pair_geometry(
                table_ref, codes, live, tile0, tiles, target, basis, tangent,
                sines_ref.at[pl.ds(part * rows_in, rows_in), :], slopes_ref.at[pl.ds(part * rows_in, rows_in), :],
            )
            env_ref[part * 16 : part * 16 + 8, :] = envelope
            shapes = shapes_of(direction)
            for q in range(1, 9):
                shape_ref[slot[part], q * 8 : q * 8 + 8, :] = shapes[q]
            if tangent:
                env_ref[part * 16 + 8 : part * 16 + 16, :] = envelope_slope
                for axis in range(3):
                    geometry_ref[slot[part], axis * 8 : axis * 8 + 8, :] = direction[axis]
                geometry_ref[slot[part], 24:32, :] = inverse
                geometry_ref[slot[part], 32:40, :] = inside.astype(f32)
        value = []
        for part in both:
            stacked = split_rows(sines_ref, basis, part * rows_in)
            if tangent:
                stacked = jnp.concatenate([stacked, split_rows(slopes_ref, basis, part * rows_in)], axis=1)
            value.append(plain_dot(win_ref[...], stacked))
        for part in both:
            if tiles > 4:
                hot = hot_codes(list_ref, offset[part], size, 0)
                partner_ref[slot[part]] = plain_dot(feature_ref[:, first : first + size], hot)
            else:
                for row in range(8):
                    codes = jnp.broadcast_to(list_ref[pl.ds(offset[part] + row, 1), :], (8, LANES))
                    at_lane = codes & (LANES - 1)
                    tile = codes >> 7
                    for block in range(8):
                        result = None
                        for other in range(tiles):
                            entries = table_ref[block * 8 : block * 8 + 8, first + other * LANES : first + (other + 1) * LANES]
                            entry = jnp.take_along_axis(entries, at_lane, axis=1)
                            result = entry if result is None else jnp.where(tile == other, entry, result)
                        partner_ref[slot[part], block * 8 : block * 8 + 8, row * LANES : (row + 1) * LANES] = result
        for part in both:
            top = part * 128
            for row in range(8):
                lanes = slice(row * LANES, (row + 1) * LANES)
                here = value[part][:, lanes]
                scale = spread_row(env_ref, part * 16 + row, 64)
                gate = 1.0 / (1.0 + jnp.exp(-here))
                hidden = here * gate
                high, low = high_low(hidden * scale)
                hidden_ref[top : top + 64, lanes] = high
                hidden_ref[top + 64 : top + 128, lanes] = low
                if tangent:
                    later = slice(wide + row * LANES, wide + (row + 1) * LANES)
                    hidden_slope = gate * (1.0 + here * (1.0 - gate)) * value[part][:, later]
                    scale_slope = spread_row(env_ref, part * 16 + 8 + row, 64)
                    high, low = high_low(hidden * scale_slope + hidden_slope * scale)
                    hidden_ref[top : top + 64, later] = high
                    hidden_ref[top + 64 : top + 128, later] = low
        span = 2 * wide if tangent else wide
        for part in both:
            hidden = hidden_ref[part * 128 : part * 128 + 128, 0:span]
            radial_ref[slot[part], :, 0:span] = plain_dot(wout_ref[...], jnp.concatenate([hidden, hidden], axis=0))
        for block in range(8):
            sums = [
                out_ref[q * 64 + block * 8 : q * 64 + block * 8 + 8, lane0 : lane0 + LANES]
                for q in range(9)
            ]
            for part in both:
                for row in range(8):
                    lanes = slice(row * LANES, (row + 1) * LANES)
                    feature = partner_ref[slot[part], block * 8 : block * 8 + 8, lanes]
                    for degree, (low, high) in enumerate(DEGREE_ROWS):
                        at = degree * 64 + block * 8
                        weight = radial_ref[slot[part], at : at + 8, lanes] * feature
                        for q in range(low, high):
                            if q == 0:
                                sums[q] = sums[q] + weight
                            else:
                                shape = jnp.broadcast_to(shape_ref[slot[part], q * 8 + row : q * 8 + row + 1, :], (8, LANES))
                                sums[q] = sums[q] + weight * shape
            for q in range(9):
                out_ref[q * 64 + block * 8 : q * 64 + block * 8 + 8, lane0 : lane0 + LANES] = sums[q]
        return carry

    lax.fori_loop(start, stop, step, 0)


def backward_steps(refs, list_ref, steps, slot0, own_code, lane0, gradient_ref, force_ref, scatter_ref):
    (shape_ref, geometry_ref, radial_ref, partner_ref, pulled_ref, push_ref) = refs
    wide = 8 * LANES
    three, five, fifteen = math.sqrt(3.0), math.sqrt(5.0), math.sqrt(15.0)

    def step(number, carry):
        slot = slot0 + number
        for row in range(8):
            lanes = slice(row * LANES, (row + 1) * LANES)
            later = slice(wide + row * LANES, wide + (row + 1) * LANES)
            pulled = [jnp.zeros((8, LANES), f32) for q in range(9)]
            spoke = jnp.zeros((8, LANES), f32)
            shapes = [None] + [
                jnp.broadcast_to(shape_ref[slot, q * 8 + row : q * 8 + row + 1, :], (8, LANES)) for q in range(1, 9)
            ]
            for block in range(8):
                feature = partner_ref[slot, block * 8 : block * 8 + 8, lanes]
                for degree, (low, high) in enumerate(DEGREE_ROWS):
                    at = degree * 64 + block * 8
                    weight = radial_ref[slot, at : at + 8, lanes] * feature
                    weight_slope = radial_ref[slot, at : at + 8, later] * feature
                    mixed = None
                    for q in range(low, high):
                        gradient = gradient_ref[q * 64 + block * 8 : q * 64 + block * 8 + 8, lane0 : lane0 + LANES]
                        if q > 0:
                            pulled[q] = pulled[q] + weight * gradient
                            gradient = gradient * shapes[q]
                        mixed = gradient if mixed is None else mixed + gradient
                    spoke = spoke + weight_slope * mixed
            for q in range(1, 9):
                pulled_ref[q * 8 + row : q * 8 + row + 1, :] = jnp.sum(pulled[q], axis=0, keepdims=True)
            pulled_ref[row : row + 1, :] = jnp.sum(spoke, axis=0, keepdims=True)
        x, y, z = direction = [geometry_ref[slot, axis * 8 : axis * 8 + 8, :] for axis in range(3)]
        inverse = geometry_ref[slot, 24:32, :]
        inside = geometry_ref[slot, 32:40, :] > 0.5
        p = [pulled_ref[q * 8 : q * 8 + 8, :] for q in range(9)]
        turn = [
            three * p[1] + fifteen * (y * p[4] + z * p[7] + x * p[8]),
            three * p[2] + fifteen * (x * p[4] + z * p[5] - y * p[8]),
            three * p[3] + fifteen * (y * p[5] + x * p[7]) + (3.0 * five) * z * p[6],
        ]
        along = x * turn[0] + y * turn[1] + z * turn[2]
        for axis in range(3):
            part = (turn[axis] - direction[axis] * along) * inverse + direction[axis] * p[0]
            part = jnp.where(inside, part, 0.0)
            if force_ref is not None:
                force_ref[axis : axis + 1, :] += jnp.sum(part, axis=0, keepdims=True)
            high = part.astype(bf16).astype(f32)
            push_ref[axis * 8 : axis * 8 + 8, :] = high
            push_ref[24 + axis * 8 : 32 + axis * 8, :] = part - high
        push = jnp.concatenate([push_ref[pl.ds(row, 8, stride=8), :] for row in range(8)], axis=1)
        hot = hot_codes(list_ref, pl.multiple_of(number * 8, 8), LANES, own_code)
        scatter_ref[...] += nt_dot(push.astype(bf16), hot)
        return carry

    lax.fori_loop(0, steps, step, 0)


def rounded(value):
    return lax.reduce_precision(value, 8, 7)


def stacked_weights(radial_in, radial_out):
    high = rounded(radial_in)
    middle = rounded(radial_in - high)
    low = rounded(radial_in - high - middle)
    win = jnp.concatenate([high, high, middle, middle, high, low], axis=1).astype(bf16)
    high = rounded(radial_out)
    low = rounded(radial_out - high)
    wout = jnp.concatenate([high, high, low, low], axis=1).astype(bf16)
    return win, wout


HALF = LANES // 2
QUARTER = LANES // 4
MIDDLE = 4
AROUND = (0, 1, 2, 6, 7, 8)
TILE_OF = {0: 0, 1: 1, 2: 2, 6: 3, 7: 4, 8: 5, 3: 6, 5: 7, 4: 8}
TILE_LR, TILE_OWN, TILE_X, TILE_Y, TILES = 9, 10, 11, 12, 13
LIST_ROWS = 64
MOST_PAIRS = 49
SLOT_OWN, SLOT_X, SLOT_Y, SLOT_FREE, SLOTS = 0, 8, 12, 14, 16


def rep(row):
    return jnp.broadcast_to(row, (8, LANES))


def tall(value, rows):
    return jnp.concatenate([value] * (rows // 8), axis=0)


def pick(values, slots):
    return jnp.take_along_axis(values, tall(slots, values.shape[0]) if slots.shape[0] != values.shape[0] else slots, axis=1)


def merge(base, count, segment, more):
    rows = base.shape[0]
    if segment.shape[0] < rows:
        segment = jnp.concatenate([segment, jnp.zeros((rows - segment.shape[0], LANES), i32)], axis=0)
    shift = tall(count, rows)
    for bit in (1, 2, 4, 8, 16, 32):
        segment = jnp.where((shift & bit) != 0, pltpu.roll(segment, bit, axis=0), segment)
    row = lax.broadcasted_iota(i32, (rows, LANES), 0)
    return jnp.where(row < shift, base, segment), count + more


def join(pieces):
    codes, count = pieces[0]
    for other, number in pieces[1:]:
        codes = jnp.where(tall(number, other.shape[0]) > 0, other, codes)
        count = count + number
    return codes, count


def main_kernel(strip_ref, low_ref, high_ref, win_ref, wout_ref, mix_ref, outw_ref, species_ref, kind_ref,
                energy_ref, force_out, table_ref, feature_ref, column_ref, list_own, list_x, list_y,
                sums_ref, force_ref, scatter_ref, sines_ref, slopes_ref, env_ref, shape_ref, geometry_ref, hidden_ref,
                radial_ref, partner_ref, pulled_ref, push_ref):
    refs = (low_ref, strip_ref, high_ref)

    def rows_of(block, at, size):
        start = (block % 3) * PAYLOAD + at
        return refs[block // 3][start : start + size, :]

    def row_of(block, at):
        return rep(rows_of(block, at, 1).astype(i32))

    lane = lax.broadcasted_iota(i32, (8, LANES), 1)
    none = jnp.full((8, LANES), -1, i32)

    x_home = {}
    for block in range(9):
        dx = block % 3
        lower = (block - 1) * LANES + pltpu.roll(row_of(block - 1, SEND_AT), HALF, axis=1) if dx > 0 else none
        upper = (block + 1) * LANES + pltpu.roll(row_of(block + 1, SEND_AT), HALF, axis=1) if dx < 2 else none
        x_home[block] = jnp.where(lane < HALF, lower, upper)

    def section_home(block, entry):
        copies = jnp.take_along_axis(x_home[block], entry & (LANES - 1), axis=1)
        return jnp.where(entry < LANES, block * LANES + entry, copies)

    y_home = {}
    for block in range(9):
        dy = block // 3
        if dy > 0:
            lower = section_home(block - 3, pltpu.roll(row_of(block - 3, SEND_AT + 1), LANES - QUARTER, axis=1))
        else:
            lower = none
        if dy < 2:
            upper = section_home(block + 3, pltpu.roll(row_of(block + 3, SEND_AT + 1), QUARTER, axis=1))
        else:
            upper = none
        y_home[block] = jnp.where(lane < QUARTER, lower, jnp.where(lane < HALF, upper, none))

    x_here = x_home[MIDDLE]
    y_here = y_home[MIDDLE]
    y_twice = jnp.where(lane < HALF, y_here, pltpu.roll(y_here, HALF, axis=1))
    y_sides = jnp.where(lane < HALF, y_home[3], pltpu.roll(y_home[5], HALF, axis=1))

    column_ref[...] = jnp.zeros_like(column_ref)
    slots = {}

    def as_column(name, value):
        slots[name] = len(slots)
        column_ref[slots[name] : slots[name] + 1, :] = value[0:1, :].astype(f32)

    as_column("sent", row_of(MIDDLE, SEND_AT))
    as_column("x", x_here)
    as_column("y", y_here)
    as_column("sides", y_sides)
    for block in range(9):
        if block != MIDDLE:
            as_column(("y", block), y_home[block])
    for block in AROUND:
        as_column(("x", block), x_home[block])
    columns = jnp.transpose(column_ref[...])
    place = lax.broadcasted_iota(i32, (LANES, LANES), 0).astype(f32)

    def match(name, target, low=0, high=LANES):
        number = slots[name]
        same = columns[low:high, number : number + 1] == target[0:1, :].astype(f32)
        return rep(jnp.max(jnp.where(same, place[low:high, :], -1.0), axis=0, keepdims=True).astype(i32))

    def gathered(home, blocks, rows, at):
        block_of = home >> 7
        slot = home & (LANES - 1)
        result = jnp.zeros((rows, LANES), f32)
        for block in blocks:
            result = jnp.where(tall(block_of, rows) == block, pick(rows_of(block, at, rows), slot), result)
        return result

    for block, tile in TILE_OF.items():
        table_ref[:, tile * LANES : (tile + 1) * LANES] = rows_of(block, 0, 72)
    table_ref[:, TILE_OWN * LANES : (TILE_OWN + 1) * LANES] = rows_of(MIDDLE, 0, 72)
    table_ref[:, TILE_X * LANES : (TILE_X + 1) * LANES] = gathered(x_here, (3, 5), 72, 0)
    table_ref[:, TILE_Y * LANES : (TILE_Y + 1) * LANES] = gathered(y_twice, AROUND, 72, 0)
    table_ref[:, TILE_LR * LANES : (TILE_LR + 1) * LANES] = gathered(y_sides, AROUND, 72, 0)
    feature_ref[...] = table_ref[0:64, :].astype(bf16)

    def aligned(block, at, rows, count_at, found):
        at_lane = jnp.maximum(found, 0)
        codes = pick(rows_of(block, at, rows).astype(i32), at_lane)
        count = jnp.take_along_axis(row_of(block, count_at), at_lane, axis=1)
        return codes, jnp.where(found >= 0, count, 0)

    def renamed(codes, table, offset):
        found = pick(jnp.concatenate([table] * (codes.shape[0] // 8), axis=0), codes & (LANES - 1))
        return jnp.where(found >= 0, found + offset, -1)

    own_home = MIDDLE * LANES + lane
    codes = jnp.concatenate([rows_of(MIDDLE, OWN_AT, OWN_ROWS).astype(i32), jnp.zeros((LIST_ROWS - OWN_ROWS, LANES), i32)], axis=0)
    count = row_of(MIDDLE, COUNT_AT)
    found_low = match("sent", lane, 0, HALF)
    found_low = jnp.where(found_low >= 0, found_low + HALF, -1)
    found_high = match("sent", lane, HALF, LANES)
    found_high = jnp.where(found_high >= 0, found_high - HALF, -1)
    pieces = []
    for block, found in ((3, found_low), (5, found_high)):
        piece, number = aligned(block, X_AT, GHOST_ROWS, COUNT_AT + 1, found)
        pieces.append((renamed(piece, match("x", block * LANES + lane), LANES), number))
    codes, count = merge(codes, count, *join(pieces))
    y_lane = {block: match("y", block * LANES + lane) for block in AROUND}
    for blocks in ((1, 7), (0, 2, 6, 8)):
        pieces = []
        for block in blocks:
            piece, number = aligned(block, Y_AT, GHOST_ROWS, COUNT_AT + 2, match(("y", block), own_home, 0, HALF))
            pieces.append((renamed(piece, y_lane[block], 2 * LANES), number))
        codes, count = merge(codes, count, *join(pieces))
    list_own[...] = codes
    count_own = count

    pieces = []
    for block, tile in ((3, 0), (5, 1)):
        found = jnp.where(x_here >> 7 == block, x_here & (LANES - 1), -1)
        piece, number = aligned(block, OWN_AT, OWN_ROWS, COUNT_AT, found)
        home = pick(jnp.concatenate([x_home[block]] * (OWN_ROWS // 8), axis=0), piece & (LANES - 1))
        copy = jnp.where(home >> 7 == MIDDLE, 2 * LANES + (home & (LANES - 1)), -1)
        piece = jnp.where(
            piece < LANES, piece + tile * LANES, jnp.where(piece < 2 * LANES, copy, piece + LANES + tile * HALF)
        )
        pieces.append((piece, number))
    codes, count = join(pieces)
    codes = jnp.concatenate([codes, jnp.zeros((LIST_ROWS - OWN_ROWS, LANES), i32)], axis=0)
    codes, count = merge(
        codes, count, rows_of(MIDDLE, X_AT, GHOST_ROWS).astype(i32) + 2 * LANES, row_of(MIDDLE, COUNT_AT + 1)
    )
    side_lane = {block: match("sides", block * LANES + lane) for block in AROUND}
    for blocks in ((1, 7), (0, 2, 6, 8)):
        pieces = []
        for block in blocks:
            piece, number = aligned(block, Y_AT, GHOST_ROWS, COUNT_AT + 2, match(("y", block), x_here, 0, HALF))
            pieces.append((renamed(piece, side_lane[block], 3 * LANES), number))
        codes, count = merge(codes, count, *join(pieces))
    codes_x, count_x = codes, count

    def tiled(home):
        block = home >> 7
        tile = jnp.where(block < 3, block, jnp.where(block > 5, block - 3, jnp.where(block == 3, 6, jnp.where(block == 5, 7, 8))))
        return jnp.where(home >= 0, tile * LANES + (home & (LANES - 1)), -1)

    pieces = []
    for block in AROUND:
        found = jnp.where(y_here >> 7 == block, y_here & (LANES - 1), -1)
        piece, number = aligned(block, OWN_AT, OWN_ROWS, COUNT_AT, found)
        slot = piece & (LANES - 1)
        copy_x = pick(jnp.concatenate([tiled(x_home[block])] * (OWN_ROWS // 8), axis=0), slot)
        copy_y = pick(jnp.concatenate([tiled(y_home[block])] * (OWN_ROWS // 8), axis=0), slot)
        piece = jnp.where(
            piece < LANES, piece + TILE_OF[block] * LANES, jnp.where(piece < 2 * LANES, copy_x, copy_y)
        )
        pieces.append((piece, number))
    codes, count = join(pieces)
    codes = jnp.concatenate([codes, jnp.zeros((LIST_ROWS - OWN_ROWS, LANES), i32)], axis=0)
    pieces = []
    for block in AROUND:
        piece, number = aligned(block, X_AT, GHOST_ROWS, COUNT_AT + 1, match(("x", block), y_here))
        pieces.append((piece + TILE_OF[block] * LANES, number))
    codes, count = merge(codes, count, *join(pieces))
    codes, count = merge(
        codes, count, rows_of(MIDDLE, Y_AT, GHOST_ROWS).astype(i32) + TILE_OF[MIDDLE] * LANES, row_of(MIDDLE, COUNT_AT + 2)
    )
    pieces = []
    for block in (3, 5):
        piece, number = aligned(block, Y_AT, GHOST_ROWS, COUNT_AT + 2, match(("y", block), y_here, 0, HALF))
        pieces.append((piece + TILE_OF[block] * LANES, number))
    codes, count = merge(codes, count, *join(pieces))
    count = jnp.where(lane < HALF, count, 0)
    codes_y, count_y = codes, count

    earlier = (
        lax.broadcasted_iota(i32, (LIST_ROWS, LIST_ROWS), 1) < lax.broadcasted_iota(i32, (LIST_ROWS, LIST_ROWS), 0)
    ).astype(f32).astype(bf16)
    row = lax.broadcasted_iota(i32, (LIST_ROWS, LANES), 0)

    def own_first(codes, count, first):
        live = row < tall(count, LIST_ROWS)
        kept = live & (codes >= first) & (codes < first + LANES)
        weight = kept.astype(f32)
        total = jnp.sum(weight, axis=0, keepdims=True)
        rest = live.astype(f32) - weight
        rank = plain_dot(earlier, jnp.concatenate([weight, rest], axis=1).astype(bf16))
        place_at = jnp.where(kept, rank[:, 0:LANES], jnp.where(live, rank[:, LANES:] + total, -1.0))
        value = codes.astype(f32)
        rows = [
            jnp.sum(jnp.where(place_at == float(number), value, 0.0), axis=0, keepdims=True).astype(i32)
            for number in range(MOST_PAIRS)
        ]
        return rows, rep(total)

    list_x[...] = jnp.zeros_like(list_x)
    list_y[...] = jnp.zeros_like(list_y)
    rows_x, back_x = own_first(codes_x, count_x, 2 * LANES)
    for number in range(MOST_PAIRS):
        list_x[number : number + 1, :] = rows_x[number]
    rows_y, back_y = own_first(codes_y, count_y, TILE_OF[MIDDLE] * LANES)
    blank = jnp.zeros((1, LANES), i32)
    for number in range(0, MOST_PAIRS, 2):
        odd = rows_y[number + 1] if number + 1 < MOST_PAIRS else blank
        odd = pltpu.roll(rep(odd), HALF, axis=1)
        list_y[number // 2 : number // 2 + 1, :] = jnp.where(lane < HALF, rep(rows_y[number]), odd)[0:1, :]
    count_pack = jnp.where(lane < HALF, (count_y + 1) >> 1, pltpu.roll(count_y, HALF, axis=1) >> 1)

    sums_ref[...] = jnp.zeros_like(sums_ref)

    def most(count):
        return jnp.max(count.astype(f32)).astype(i32)

    pairs_own = (most(count_own) + 15) // 16
    pairs_x = (most(count_x) + 15) // 16
    pairs_y = (most(count_pack) + 15) // 16
    scratch = (table_ref, feature_ref, win_ref, wout_ref, sines_ref, slopes_ref, env_ref, shape_ref, geometry_ref, hidden_ref, radial_ref, partner_ref)
    forward_pairs(scratch, list_own, count_own, TILE_OWN, 3, TILE_OWN, 0, SLOT_OWN, True, 0, pairs_own, sums_ref)
    forward_pairs(scratch, list_x, count_x, 6, 4, TILE_X, LANES, SLOT_X, True, 0, jnp.minimum(pairs_x, 2), sums_ref)
    forward_pairs(scratch, list_x, count_x, 6, 4, TILE_X, LANES, SLOT_FREE, False, 2, pairs_x, sums_ref)
    forward_pairs(scratch, list_y, count_pack, 0, 9, TILE_Y, 2 * LANES, SLOT_Y, True, 0, jnp.minimum(pairs_y, 1), sums_ref)
    forward_pairs(scratch, list_y, count_pack, 0, 9, TILE_Y, 2 * LANES, SLOT_FREE, False, 1, pairs_y, sums_ref)
    sums_y = sums_ref[:, 2 * LANES : 3 * LANES]
    sums_ref[:, 2 * LANES : 3 * LANES] = sums_y + pltpu.roll(sums_y, HALF, axis=1)

    sums = sums_ref[...]
    square = sums * sums
    degree_one = square[64:128] + square[128:192] + square[192:256]
    degree_two = square[256:320] + square[320:384] + square[384:448] + square[448:512] + square[512:576]
    invariant = jnp.concatenate([square[0:64], degree_one, degree_two], axis=0)
    mixed = lax.dot_general(
        mix_ref[...], invariant, (((1,), (0,)), ((), ())), precision=highest, preferred_element_type=f32
    ) + table_ref[0:64, TILE_OWN * LANES : (TILE_Y + 1) * LANES]
    gate = 1.0 / (1.0 + jnp.exp(-mixed))
    weight = outw_ref[...]
    energy = jnp.sum(weight * (mixed * gate)[:, 0:LANES], axis=0, keepdims=True)
    kinds = species_ref[...]
    for kind in range(kind_ref.shape[0]):
        energy = energy + jnp.where(kinds == kind, kind_ref[kind], 0.0)
    energy_ref[...] = energy
    slope = weight * (gate * (1.0 + mixed * (1.0 - gate)))
    pulled = 2.0 * lax.dot_general(
        mix_ref[...], slope, (((0,), (0,)), ((), ())), precision=highest, preferred_element_type=f32
    )
    for q in range(9):
        degree = (0, 1, 1, 1, 2, 2, 2, 2, 2)[q]
        sums_ref[q * 64 : q * 64 + 64, :] = sums[q * 64 : q * 64 + 64] * pulled[degree * 64 : degree * 64 + 64]

    force_ref[...] = jnp.zeros_like(force_ref)
    scatter_ref[...] = jnp.zeros_like(scatter_ref)
    push_ref[...] = jnp.zeros_like(push_ref)
    scratch = (shape_ref, geometry_ref, radial_ref, partner_ref, pulled_ref, push_ref)
    backward_steps(scratch, list_own, (most(count_own) + 7) // 8, SLOT_OWN, 0, 0, sums_ref, force_ref, scatter_ref)
    backward_steps(scratch, list_x, (most(back_x) + 7) // 8, SLOT_X, 2 * LANES, LANES, sums_ref, None, scatter_ref)
    backward_steps(
        scratch, list_y, (most(back_y) + 15) // 16, SLOT_Y, TILE_OF[MIDDLE] * LANES, 2 * LANES, sums_ref, None, scatter_ref
    )
    force_out[...] = force_ref[0:3, :] - scatter_ref[0:3, :] - scatter_ref[3:6, :]


def main_pass(strip, low, high, win, wout, mix_weight, out_weight, species, species_energy):
    vmem = pl.BlockSpec(memory_space=pltpu.VMEM)
    wide = 8 * LANES
    return pl.pallas_call(
        main_kernel,
        out_shape=(jax.ShapeDtypeStruct((1, LANES), f32), jax.ShapeDtypeStruct((3, LANES), f32)),
        in_specs=[vmem] * 8 + [pl.BlockSpec(memory_space=pltpu.SMEM)],
        out_specs=(vmem, vmem),
        scratch_shapes=[
            pltpu.VMEM((72, TILES * LANES), f32),
            pltpu.VMEM((64, TILES * LANES), bf16),
            pltpu.VMEM((LANES, LANES), f32),
            pltpu.VMEM((LIST_ROWS, LANES), i32),
            pltpu.VMEM((LIST_ROWS, LANES), i32),
            pltpu.VMEM((32, LANES), i32),
            pltpu.VMEM((576, 3 * LANES), f32),
            pltpu.VMEM((8, LANES), f32),
            pltpu.VMEM((8, LANES), f32),
            pltpu.VMEM((128, LANES), f32),
            pltpu.VMEM((128, LANES), f32),
            pltpu.VMEM((32, LANES), f32),
            pltpu.VMEM((SLOTS, 72, LANES), f32),
            pltpu.VMEM((SLOTS, 40, LANES), f32),
            pltpu.VMEM((256, 2 * wide), bf16),
            pltpu.VMEM((SLOTS, 192, 2 * wide), f32),
            pltpu.VMEM((SLOTS, 64, wide), f32),
            pltpu.VMEM((72, LANES), f32),
            pltpu.VMEM((64, LANES), f32),
        ],
        compiler_params=pltpu.CompilerParams(vmem_limit_bytes=48 * 1024 * 1024),
    )(strip, low, high, win, wout, mix_weight, out_weight[:, None], species[None, :], species_energy)


def from_both_sides(block, axis):
    count = lax.axis_size(axis)
    up = [(i, (i + 1) % count) for i in range(count)]
    down = [(target, source) for source, target in up]
    return lax.ppermute(block, axis, up), lax.ppermute(block, axis, down)


def local(
    positions, features, species, edge_list, edge_count, send_list_x, send_list_y,
    radial_in, radial_out, mix_weight, out_weight, species_energy,
):
    own = make_payload(edge_list, edge_count, positions, features, send_list_x, send_list_y)
    left, right = from_both_sides(own, "gx")
    strip = jnp.concatenate([left, own, right], axis=0)
    low, high = from_both_sides(strip, "gy")
    win, wout = stacked_weights(radial_in, radial_out)
    energies, forces = main_pass(strip, low, high, win, wout, mix_weight, out_weight, species, species_energy)
    return energies[0], forces


def solution(mesh):
    placed = (
        P(None, ("gx", "gy")), P(None, ("gx", "gy")), P(("gx", "gy")), P(None, ("gx", "gy")), P(("gx", "gy")),
        P(("gx", "gy")), P(("gx", "gy")), P(), P(), P(), P(), P(),
    )
    return jax.shard_map(
        local, mesh=mesh, in_specs=placed, out_specs=(P(("gx", "gy")), P(None, ("gx", "gy"))), check_vma=False,
    )
```

```python
import math

import jax
import jax.numpy as jnp
import numpy as np
from jax import lax
from jax.experimental import pallas as pl
from jax.experimental.pallas import tpu as pltpu
from jax.sharding import PartitionSpec as P

cutoff_radius = 5.0
message_scale = 0.3
highest = lax.Precision.HIGHEST
f32 = jnp.float32
bf16 = jnp.bfloat16
i32 = jnp.int32

LANES = 128
EDGE_STEP = 256
OWN_ROWS = 56
GHOST_ROWS = 24
COUNT_AT, SEND_AT, OWN_AT, X_AT, Y_AT, PAYLOAD = 67, 70, 72, 128, 152, 168
EDGE_PARTS = 7
DEGREE_ROWS = ((0, 1), (1, 4), (4, 9))


def nt_dot(left, right):
    return lax.dot_general(left, right, (((1,), (1,)), ((), ())), preferred_element_type=f32)


def plain_dot(left, right):
    return lax.dot_general(left, right, (((1,), (0,)), ((), ())), preferred_element_type=f32)


def list_kernel(count_ref, edges_hbm, positions_hbm, features_hbm, send_x_hbm, send_y_hbm, out_ref, edges_ref, positions_ref,
                features_ref, send_x_ref, send_y_ref, arrived, count_out, own_acc, ghost_acc, own_base, ghost_base):
    copies = [
        pltpu.make_async_copy(source, target, arrived.at[number])
        for number, (source, target) in enumerate(
            (
                (edges_hbm, edges_ref),
                (positions_hbm, positions_ref),
                (features_hbm, features_ref),
                (send_x_hbm, send_x_ref),
                (send_y_hbm, send_y_ref),
            )
        )
    ]
    for copy in copies:
        copy.start()
    ghosts = ghost_base.shape[0]
    live_total = count_ref[0]
    own_acc[...] = jnp.zeros_like(own_acc)
    ghost_acc[...] = jnp.zeros_like(ghost_acc)
    own_base[...] = jnp.zeros_like(own_base)
    ghost_base[...] = jnp.zeros_like(ghost_base)
    count_out[...] = jnp.zeros_like(count_out)
    out_ref[...] = jnp.zeros_like(out_ref)
    before = lax.broadcasted_iota(i32, (EDGE_STEP, EDGE_STEP), 0) < lax.broadcasted_iota(
        i32, (EDGE_STEP, EDGE_STEP), 1
    )
    earlier = before.astype(f32).astype(bf16)
    every = jnp.ones((EDGE_STEP, EDGE_STEP), bf16)
    row = jnp.ones((8, EDGE_STEP), bf16)
    own_lane = lax.broadcasted_iota(i32, (LANES, EDGE_STEP), 0)
    ghost_lane = lax.broadcasted_iota(i32, (ghosts, EDGE_STEP), 0) + LANES
    own_rank = lax.broadcasted_iota(i32, (own_acc.shape[0], EDGE_STEP), 0).astype(f32)
    ghost_rank = lax.broadcasted_iota(i32, (ghost_acc.shape[0], EDGE_STEP), 0).astype(f32)
    span = EDGE_PARTS * EDGE_STEP
    copies[0].wait()

    def step(number, carry):
        blocks = []
        for part in range(EDGE_PARTS):
            offset = pl.multiple_of(number * span + part * EDGE_STEP, EDGE_STEP)
            first = edges_ref[0:1, pl.ds(offset, EDGE_STEP)]
            second = edges_ref[1:2, pl.ds(offset, EDGE_STEP)]
            live = offset + lax.broadcasted_iota(i32, (1, EDGE_STEP), 1) < live_total
            first = jnp.where(live, first, -1)
            second = jnp.where(live, second, -1)
            hot = [(own_lane == first).astype(f32), (own_lane == second).astype(f32), (ghost_lane == second).astype(f32)]
            low = [one.astype(bf16) for one in hot]
            ahead = [plain_dot(one, earlier) for one in low]
            total = [plain_dot(one, every) for one in low]
            blocks.append(((first - 160).astype(f32), (second - 160).astype(f32), hot, low, ahead, total))
        own_start = own_base[...]
        ghost_start = ghost_base[...]
        own_new, ghost_new = own_acc[...], ghost_acc[:, 0:ghosts]
        own_count, ghost_count = count_out[:, 0:LANES], count_out[:, LANES : LANES + ghosts]
        for first_code, second_code, hot, low, ahead, total in blocks:
            first_rank = jnp.sum(hot[0] * (own_start + ahead[0]), axis=0, keepdims=True)
            own_start = own_start + total[0]
            second_rank = jnp.sum(hot[1] * (own_start + ahead[1]), axis=0, keepdims=True)
            own_start = own_start + total[1]
            second_rank += jnp.sum(hot[2] * (ghost_start + ahead[2]), axis=0, keepdims=True)
            ghost_start = ghost_start + total[2]
            place_first = jnp.where(own_rank == first_rank, second_code, 0.0).astype(bf16)
            place_second = jnp.where(own_rank == second_rank, first_code, 0.0).astype(bf16)
            place_ghost = jnp.where(ghost_rank == second_rank, first_code, 0.0).astype(bf16)
            own_new = own_new + nt_dot(place_first, low[0]) + nt_dot(place_second, low[1])
            ghost_new = ghost_new + nt_dot(place_ghost, low[2])
            own_count = own_count + nt_dot(row, low[0]) + nt_dot(row, low[1])
            ghost_count = ghost_count + nt_dot(row, low[2])
        own_base[...] = own_start
        ghost_base[...] = ghost_start
        own_acc[...] = own_new
        ghost_acc[:, 0:ghosts] = ghost_new
        count_out[:, 0:LANES] = own_count
        count_out[:, LANES : LANES + ghosts] = ghost_count
        return carry

    lax.fori_loop(0, (live_total + span - 1) // span, step, 0)
    for copy in copies[1:]:
        copy.wait()
    own_code = own_acc[0:OWN_ROWS, :] + 160.0
    ghost_code = ghost_acc[0:GHOST_ROWS, :] + 160.0
    counts = count_out[0:1, :].astype(i32)
    own_live = lax.broadcasted_iota(i32, (OWN_ROWS, LANES), 0) < counts[:, 0:LANES]
    ghost_live = lax.broadcasted_iota(i32, ghost_code.shape, 0) < counts[:, LANES:]
    out_ref[0:64, :] = features_ref[...].astype(f32)
    out_ref[64:67, :] = positions_ref[...]
    out_ref[OWN_AT : OWN_AT + OWN_ROWS, :] = jnp.where(own_live, own_code, 0.0)
    ghost_code = jnp.where(ghost_live, ghost_code, 0.0)
    out_ref[X_AT : X_AT + GHOST_ROWS, :] = ghost_code[:, 0:LANES]
    copies_y = ghost_code[:, LANES:]
    out_ref[Y_AT : Y_AT + 16, :] = copies_y[0:16, :]
    lane = lax.broadcasted_iota(i32, (8, LANES), 1)
    out_ref[Y_AT : Y_AT + 8, :] = jnp.where(lane < LANES // 2, copies_y[0:8, :], pltpu.roll(copies_y[16:24, :], LANES // 2, axis=1))
    for group in range(3):
        out_ref[COUNT_AT + group : COUNT_AT + group + 1, :] = count_out[0:1, group * LANES : (group + 1) * LANES]
    out_ref[SEND_AT : SEND_AT + 1, :] = send_x_ref[...].astype(f32)
    out_ref[SEND_AT + 1 : SEND_AT + 2, 0 : send_y_ref.shape[1]] = send_y_ref[...].astype(f32)


def make_payload(edge_list, edge_count, positions, features, send_list_x, send_list_y):
    ghosts = send_list_x.shape[0] + send_list_y.shape[0]
    operands = (edge_list, positions, features, send_list_x[None, :], send_list_y[None, :])
    return pl.pallas_call(
        list_kernel,
        out_shape=jax.ShapeDtypeStruct((PAYLOAD, LANES), f32),
        in_specs=[pl.BlockSpec(memory_space=pltpu.SMEM)] + [pl.BlockSpec(memory_space=pl.ANY)] * 5,
        out_specs=pl.BlockSpec(memory_space=pltpu.VMEM),
        scratch_shapes=[pltpu.VMEM(operand.shape, operand.dtype) for operand in operands]
        + [
            pltpu.SemaphoreType.DMA((5,)),
            pltpu.VMEM((8, 3 * LANES), f32),
            pltpu.VMEM((64, LANES), f32),
            pltpu.VMEM((32, 2 * LANES), f32),
            pltpu.VMEM((LANES, EDGE_STEP), f32),
            pltpu.VMEM((ghosts, EDGE_STEP), f32),
        ],
        compiler_params=pltpu.CompilerParams(vmem_limit_bytes=56 * 1024 * 1024),
    )(edge_count, *operands)


def spread_row(ref, row, rows):
    return jnp.broadcast_to(ref[pl.ds(row, 1), :], (rows, LANES))


def lookup(table_ref, row, tile0, tiles, slot, block):
    result = None
    for number in range(tiles):
        at = (tile0 + number) * LANES
        entries = jnp.broadcast_to(table_ref[row : row + 1, at : at + LANES], (8, LANES))
        value = jnp.take_along_axis(entries, slot, axis=1)
        result = value if result is None else jnp.where(block == number, value, result)
    return result


def sine_cosine(scaled):
    angle = math.pi * (scaled - 0.5)
    square = angle * angle
    cosine = 1.0
    sine = 1.0
    for order in range(7, 0, -1):
        cosine = 1.0 - square * cosine * (1.0 / ((2 * order - 1) * (2 * order)))
        sine = 1.0 - square * sine * (1.0 / ((2 * order) * (2 * order + 1)))
    return cosine, -(angle * sine)


def pair_geometry(table_ref, codes, live, tile0, tiles, target, basis, tangent, sines_ref, slopes_ref):
    slot = codes & (LANES - 1)
    block = codes >> 7
    relative = []
    for axis in range(3):
        partner = lookup(table_ref, 64 + axis, tile0, tiles, slot, block)
        here = jnp.broadcast_to(
            table_ref[64 + axis : 65 + axis, target * LANES : (target + 1) * LANES], (8, LANES)
        )
        relative.append(jnp.where(live, partner - here, 2.0 if axis == 0 else 0.0))
    distance = jnp.sqrt(relative[0] * relative[0] + relative[1] * relative[1] + relative[2] * relative[2])
    inverse = 1.0 / distance
    direction = [part * inverse for part in relative]
    inside = live & (distance < cutoff_radius)
    scaled = jnp.minimum(distance, cutoff_radius) * (1.0 / cutoff_radius)
    room = 1.0 - scaled * scaled
    envelope = jnp.where(inside, message_scale * room * room, 0.0)
    envelope_slope = jnp.where(inside, (-4.0 * message_scale / cutoff_radius) * scaled * room, 0.0)
    sine, cosine = sine_cosine(scaled)
    twice = 2.0 * cosine
    scale = math.sqrt(2.0 / cutoff_radius)
    last_sine, last_cosine = jnp.zeros_like(sine), jnp.ones_like(sine)
    for order in range(1, basis + 1):
        wave = scale * sine * inverse
        sines_ref[(order - 1) * 8 : order * 8, :] = wave
        if tangent:
            slope = (scale * order * math.pi / cutoff_radius) * cosine * inverse - wave * inverse
            slopes_ref[(order - 1) * 8 : order * 8, :] = slope
        sine, last_sine = twice * sine - last_sine, sine
        cosine, last_cosine = twice * cosine - last_cosine, cosine
    return direction, inverse, envelope, envelope_slope, inside


def split_rows(ref, basis, at):
    pieces = []
    for row in range(8):
        whole = ref[pl.ds(at + row, basis, stride=8), :]
        high = whole.astype(bf16).astype(f32)
        rest = whole - high
        middle = rest.astype(bf16).astype(f32)
        low = rest - middle
        pieces.append(jnp.concatenate([high, middle, high, middle, low, high], axis=0).astype(bf16))
    return jnp.concatenate(pieces, axis=1)


def high_low(value):
    high = value.astype(bf16)
    low = (value - high.astype(f32)).astype(bf16)
    return high, low


def shapes_of(direction):
    x, y, z = direction
    three, five, fifteen = math.sqrt(3.0), math.sqrt(5.0), math.sqrt(15.0)
    return [
        jnp.ones_like(x),
        three * x,
        three * y,
        three * z,
        fifteen * x * y,
        fifteen * y * z,
        0.5 * five * (3.0 * z * z - 1.0),
        fifteen * x * z,
        0.5 * fifteen * (x * x - y * y),
    ]


def hot_codes(list_ref, offset, size, first):
    columns = []
    lane = lax.broadcasted_iota(i32, (size, LANES), 0) + first
    for row in range(8):
        codes = jnp.broadcast_to(list_ref[pl.ds(offset + row, 1), :], (size, LANES))
        columns.append((lane == codes).astype(f32).astype(bf16))
    return jnp.concatenate(columns, axis=1)


def forward_pairs(refs, list_ref, count_row, tile0, tiles, target, lane0, slot0, tangent, start, stop, out_ref):
    (table_ref, feature_ref, win_ref, wout_ref, sines_ref, slopes_ref, env_ref, shape_ref, geometry_ref, hidden_ref, radial_ref, partner_ref) = refs
    basis = win_ref.shape[1] // 6
    size = tiles * LANES
    first = tile0 * LANES
    wide = 8 * LANES
    count = count_row.astype(i32)
    rows_in = 8 * basis

    def step(number, carry):
        both = (0, 1)
        offset = [pl.multiple_of(number * 16 + part * 8, 8) for part in both]
        slot = [slot0 + part + (number * 2 if tangent else 0) for part in both]
        for part in both:
            codes = list_ref[pl.ds(offset[part], 8), :]
            live = (offset[part] + lax.broadcasted_iota(i32, (8, LANES), 0) < count) & (codes >= 0)
            direction, inverse, envelope, envelope_slope, inside = pair_geometry(
                table_ref, codes, live, tile0, tiles, target, basis, tangent,
                sines_ref.at[pl.ds(part * rows_in, rows_in), :], slopes_ref.at[pl.ds(part * rows_in, rows_in), :],
            )
            env_ref[part * 16 : part * 16 + 8, :] = envelope
            shapes = shapes_of(direction)
            for q in range(1, 9):
                shape_ref[slot[part], q * 8 : q * 8 + 8, :] = shapes[q]
            if tangent:
                env_ref[part * 16 + 8 : part * 16 + 16, :] = envelope_slope
                for axis in range(3):
                    geometry_ref[slot[part], axis * 8 : axis * 8 + 8, :] = direction[axis]
                geometry_ref[slot[part], 24:32, :] = inverse
                geometry_ref[slot[part], 32:40, :] = inside.astype(f32)
        value = []
        for part in both:
            stacked = split_rows(sines_ref, basis, part * rows_in)
            if tangent:
                stacked = jnp.concatenate([stacked, split_rows(slopes_ref, basis, part * rows_in)], axis=1)
            value.append(plain_dot(win_ref[...], stacked))
        for part in both:
            if tiles > 4:
                hot = hot_codes(list_ref, offset[part], size, 0)
                partner_ref[slot[part]] = plain_dot(feature_ref[:, first : first + size], hot)
            else:
                for row in range(8):
                    codes = jnp.broadcast_to(list_ref[pl.ds(offset[part] + row, 1), :], (8, LANES))
                    at_lane = codes & (LANES - 1)
                    tile = codes >> 7
                    for block in range(8):
                        result = None
                        for other in range(tiles):
                            entries = table_ref[block * 8 : block * 8 + 8, first + other * LANES : first + (other + 1) * LANES]
                            entry = jnp.take_along_axis(entries, at_lane, axis=1)
                            result = entry if result is None else jnp.where(tile == other, entry, result)
                        partner_ref[slot[part], block * 8 : block * 8 + 8, row * LANES : (row + 1) * LANES] = result
        for part in both:
            top = part * 128
            for row in range(8):
                lanes = slice(row * LANES, (row + 1) * LANES)
                here = value[part][:, lanes]
                scale = spread_row(env_ref, part * 16 + row, 64)
                gate = 1.0 / (1.0 + jnp.exp(-here))
                hidden = here * gate
                high, low = high_low(hidden * scale)
                hidden_ref[top : top + 64, lanes] = high
                hidden_ref[top + 64 : top + 128, lanes] = low
                if tangent:
                    later = slice(wide + row * LANES, wide + (row + 1) * LANES)
                    hidden_slope = gate * (1.0 + here * (1.0 - gate)) * value[part][:, later]
                    scale_slope = spread_row(env_ref, part * 16 + 8 + row, 64)
                    high, low = high_low(hidden * scale_slope + hidden_slope * scale)
                    hidden_ref[top : top + 64, later] = high
                    hidden_ref[top + 64 : top + 128, later] = low
        span = 2 * wide if tangent else wide
        for part in both:
            hidden = hidden_ref[part * 128 : part * 128 + 128, 0:span]
            radial_ref[slot[part], :, 0:span] = plain_dot(wout_ref[...], jnp.concatenate([hidden, hidden], axis=0))
        for block in range(8):
            sums = [
                out_ref[q * 64 + block * 8 : q * 64 + block * 8 + 8, lane0 : lane0 + LANES]
                for q in range(9)
            ]
            for part in both:
                for row in range(8):
                    lanes = slice(row * LANES, (row + 1) * LANES)
                    feature = partner_ref[slot[part], block * 8 : block * 8 + 8, lanes]
                    for degree, (low, high) in enumerate(DEGREE_ROWS):
                        at = degree * 64 + block * 8
                        weight = radial_ref[slot[part], at : at + 8, lanes] * feature
                        for q in range(low, high):
                            if q == 0:
                                sums[q] = sums[q] + weight
                            else:
                                shape = jnp.broadcast_to(shape_ref[slot[part], q * 8 + row : q * 8 + row + 1, :], (8, LANES))
                                sums[q] = sums[q] + weight * shape
            for q in range(9):
                out_ref[q * 64 + block * 8 : q * 64 + block * 8 + 8, lane0 : lane0 + LANES] = sums[q]
        return carry

    lax.fori_loop(start, stop, step, 0)


def backward_steps(refs, list_ref, steps, slot0, own_code, lane0, gradient_ref, force_ref, scatter_ref):
    (shape_ref, geometry_ref, radial_ref, partner_ref, pulled_ref, push_ref) = refs
    wide = 8 * LANES
    three, five, fifteen = math.sqrt(3.0), math.sqrt(5.0), math.sqrt(15.0)

    def step(number, carry):
        slot = slot0 + number
        for row in range(8):
            lanes = slice(row * LANES, (row + 1) * LANES)
            later = slice(wide + row * LANES, wide + (row + 1) * LANES)
            pulled = [jnp.zeros((8, LANES), f32) for q in range(9)]
            spoke = jnp.zeros((8, LANES), f32)
            shapes = [None] + [
                jnp.broadcast_to(shape_ref[slot, q * 8 + row : q * 8 + row + 1, :], (8, LANES)) for q in range(1, 9)
            ]
            for block in range(8):
                feature = partner_ref[slot, block * 8 : block * 8 + 8, lanes]
                for degree, (low, high) in enumerate(DEGREE_ROWS):
                    at = degree * 64 + block * 8
                    weight = radial_ref[slot, at : at + 8, lanes] * feature
                    weight_slope = radial_ref[slot, at : at + 8, later] * feature
                    mixed = None
                    for q in range(low, high):
                        gradient = gradient_ref[q * 64 + block * 8 : q * 64 + block * 8 + 8, lane0 : lane0 + LANES]
                        if q > 0:
                            pulled[q] = pulled[q] + weight * gradient
                            gradient = gradient * shapes[q]
                        mixed = gradient if mixed is None else mixed + gradient
                    spoke = spoke + weight_slope * mixed
            for q in range(1, 9):
                pulled_ref[q * 8 + row : q * 8 + row + 1, :] = jnp.sum(pulled[q], axis=0, keepdims=True)
            pulled_ref[row : row + 1, :] = jnp.sum(spoke, axis=0, keepdims=True)
        x, y, z = direction = [geometry_ref[slot, axis * 8 : axis * 8 + 8, :] for axis in range(3)]
        inverse = geometry_ref[slot, 24:32, :]
        inside = geometry_ref[slot, 32:40, :] > 0.5
        p = [pulled_ref[q * 8 : q * 8 + 8, :] for q in range(9)]
        turn = [
            three * p[1] + fifteen * (y * p[4] + z * p[7] + x * p[8]),
            three * p[2] + fifteen * (x * p[4] + z * p[5] - y * p[8]),
            three * p[3] + fifteen * (y * p[5] + x * p[7]) + (3.0 * five) * z * p[6],
        ]
        along = x * turn[0] + y * turn[1] + z * turn[2]
        for axis in range(3):
            part = (turn[axis] - direction[axis] * along) * inverse + direction[axis] * p[0]
            part = jnp.where(inside, part, 0.0)
            if force_ref is not None:
                force_ref[axis : axis + 1, :] += jnp.sum(part, axis=0, keepdims=True)
            high = part.astype(bf16).astype(f32)
            push_ref[axis * 8 : axis * 8 + 8, :] = high
            push_ref[24 + axis * 8 : 32 + axis * 8, :] = part - high
        push = jnp.concatenate([push_ref[pl.ds(row, 8, stride=8), :] for row in range(8)], axis=1)
        hot = hot_codes(list_ref, pl.multiple_of(number * 8, 8), LANES, own_code)
        scatter_ref[...] += nt_dot(push.astype(bf16), hot)
        return carry

    lax.fori_loop(0, steps, step, 0)


def rounded(value):
    return lax.reduce_precision(value, 8, 7)


def stacked_weights(radial_in, radial_out):
    high = rounded(radial_in)
    middle = rounded(radial_in - high)
    low = rounded(radial_in - high - middle)
    win = jnp.concatenate([high, high, middle, middle, high, low], axis=1).astype(bf16)
    high = rounded(radial_out)
    low = rounded(radial_out - high)
    wout = jnp.concatenate([high, high, low, low], axis=1).astype(bf16)
    return win, wout


HALF = LANES // 2
QUARTER = LANES // 4
MIDDLE = 4
AROUND = (0, 1, 2, 6, 7, 8)
TILE_OF = {0: 0, 1: 1, 2: 2, 6: 3, 7: 4, 8: 5, 3: 6, 5: 7, 4: 8}
TILE_LR, TILE_OWN, TILE_X, TILE_Y, TILES = 9, 10, 11, 12, 13
LIST_ROWS = 64
MOST_PAIRS = 49
SLOT_OWN, SLOT_X, SLOT_Y, SLOT_FREE, SLOTS = 0, 8, 12, 14, 16


def rep(row):
    return jnp.broadcast_to(row, (8, LANES))


def tall(value, rows):
    return jnp.concatenate([value] * (rows // 8), axis=0)


def pick(values, slots):
    return jnp.take_along_axis(values, tall(slots, values.shape[0]) if slots.shape[0] != values.shape[0] else slots, axis=1)


def merge(base, count, segment, more):
    rows = base.shape[0]
    if segment.shape[0] < rows:
        segment = jnp.concatenate([segment, jnp.zeros((rows - segment.shape[0], LANES), i32)], axis=0)
    shift = tall(count, rows)
    for bit in (1, 2, 4, 8, 16, 32):
        segment = jnp.where((shift & bit) != 0, pltpu.roll(segment, bit, axis=0), segment)
    row = lax.broadcasted_iota(i32, (rows, LANES), 0)
    return jnp.where(row < shift, base, segment), count + more


def join(pieces):
    codes, count = pieces[0]
    for other, number in pieces[1:]:
        codes = jnp.where(tall(number, other.shape[0]) > 0, other, codes)
        count = count + number
    return codes, count


def main_kernel(strip_ref, low_ref, high_ref, win_ref, wout_ref, mix_ref, outw_ref, species_ref, kind_ref,
                energy_ref, force_out, table_ref, feature_ref, column_ref, list_own, list_x, list_y,
                sums_ref, force_ref, scatter_ref, sines_ref, slopes_ref, env_ref, shape_ref, geometry_ref, hidden_ref,
                radial_ref, partner_ref, pulled_ref, push_ref):
    refs = (low_ref, strip_ref, high_ref)

    def rows_of(block, at, size):
        start = (block % 3) * PAYLOAD + at
        return refs[block // 3][start : start + size, :]

    def list_of(block, at):
        if at == X_AT:
            return rows_of(block, at, GHOST_ROWS).astype(i32)
        folded = rows_of(block, at, 16)
        return jnp.concatenate([folded, pltpu.roll(folded[0:8, :], HALF, axis=1)], axis=0).astype(i32)

    def row_of(block, at):
        return rep(rows_of(block, at, 1).astype(i32))

    lane = lax.broadcasted_iota(i32, (8, LANES), 1)
    none = jnp.full((8, LANES), -1, i32)

    x_home = {}
    for block in range(9):
        dx = block % 3
        lower = (block - 1) * LANES + pltpu.roll(row_of(block - 1, SEND_AT), HALF, axis=1) if dx > 0 else none
        upper = (block + 1) * LANES + pltpu.roll(row_of(block + 1, SEND_AT), HALF, axis=1) if dx < 2 else none
        x_home[block] = jnp.where(lane < HALF, lower, upper)

    def section_home(block, entry):
        copies = jnp.take_along_axis(x_home[block], entry & (LANES - 1), axis=1)
        return jnp.where(entry < LANES, block * LANES + entry, copies)

    y_home = {}
    for block in range(9):
        dy = block // 3
        if dy > 0:
            lower = section_home(block - 3, pltpu.roll(row_of(block - 3, SEND_AT + 1), LANES - QUARTER, axis=1))
        else:
            lower = none
        if dy < 2:
            upper = section_home(block + 3, pltpu.roll(row_of(block + 3, SEND_AT + 1), QUARTER, axis=1))
        else:
            upper = none
        y_home[block] = jnp.where(lane < QUARTER, lower, jnp.where(lane < HALF, upper, none))

    x_here = x_home[MIDDLE]
    y_here = y_home[MIDDLE]
    y_twice = jnp.where(lane < HALF, y_here, pltpu.roll(y_here, HALF, axis=1))
    y_sides = jnp.where(lane < HALF, y_home[3], pltpu.roll(y_home[5], HALF, axis=1))

    column_ref[...] = jnp.zeros_like(column_ref)
    slots = {}

    def as_column(name, value):
        slots[name] = len(slots)
        column_ref[slots[name] : slots[name] + 1, :] = value[0:1, :].astype(f32)

    as_column("sent", row_of(MIDDLE, SEND_AT))
    as_column("x", x_here)
    as_column("y", y_here)
    as_column("sides", y_sides)
    for block in range(9):
        if block != MIDDLE:
            as_column(("y", block), y_home[block])
    for block in AROUND:
        as_column(("x", block), x_home[block])
    columns = jnp.transpose(column_ref[...])
    place = lax.broadcasted_iota(i32, (LANES, LANES), 0).astype(f32)

    def match(name, target, low=0, high=LANES):
        number = slots[name]
        same = columns[low:high, number : number + 1] == target[0:1, :].astype(f32)
        return rep(jnp.max(jnp.where(same, place[low:high, :], -1.0), axis=0, keepdims=True).astype(i32))

    def gathered(home, blocks, rows, at):
        block_of = home >> 7
        slot = home & (LANES - 1)
        result = jnp.zeros((rows, LANES), f32)
        for block in blocks:
            result = jnp.where(tall(block_of, rows) == block, pick(rows_of(block, at, rows), slot), result)
        return result

    for block, tile in TILE_OF.items():
        table_ref[:, tile * LANES : (tile + 1) * LANES] = rows_of(block, 0, 72)
    table_ref[:, TILE_OWN * LANES : (TILE_OWN + 1) * LANES] = rows_of(MIDDLE, 0, 72)
    table_ref[:, TILE_X * LANES : (TILE_X + 1) * LANES] = gathered(x_here, (3, 5), 72, 0)
    table_ref[:, TILE_Y * LANES : (TILE_Y + 1) * LANES] = gathered(y_twice, AROUND, 72, 0)
    table_ref[:, TILE_LR * LANES : (TILE_LR + 1) * LANES] = gathered(y_sides, AROUND, 72, 0)
    feature_ref[...] = table_ref[0:64, :].astype(bf16)

    def aligned(block, at, rows, count_at, found):
        at_lane = jnp.maximum(found, 0)
        codes = rows_of(block, at, rows).astype(i32) if at == OWN_AT else list_of(block, at)
        codes = pick(codes, at_lane)
        count = jnp.take_along_axis(row_of(block, count_at), at_lane, axis=1)
        return codes, jnp.where(found >= 0, count, 0)

    def renamed(codes, table, offset):
        found = pick(jnp.concatenate([table] * (codes.shape[0] // 8), axis=0), codes & (LANES - 1))
        return jnp.where(found >= 0, found + offset, -1)

    own_home = MIDDLE * LANES + lane
    codes = jnp.concatenate([rows_of(MIDDLE, OWN_AT, OWN_ROWS).astype(i32), jnp.zeros((LIST_ROWS - OWN_ROWS, LANES), i32)], axis=0)
    count = row_of(MIDDLE, COUNT_AT)
    found_low = match("sent", lane, 0, HALF)
    found_low = jnp.where(found_low >= 0, found_low + HALF, -1)
    found_high = match("sent", lane, HALF, LANES)
    found_high = jnp.where(found_high >= 0, found_high - HALF, -1)
    pieces = []
    for block, found in ((3, found_low), (5, found_high)):
        piece, number = aligned(block, X_AT, GHOST_ROWS, COUNT_AT + 1, found)
        pieces.append((renamed(piece, match("x", block * LANES + lane), LANES), number))
    codes, count = merge(codes, count, *join(pieces))
    y_lane = {block: match("y", block * LANES + lane) for block in AROUND}
    for blocks in ((1, 7), (0, 2, 6, 8)):
        pieces = []
        for block in blocks:
            piece, number = aligned(block, Y_AT, GHOST_ROWS, COUNT_AT + 2, match(("y", block), own_home, 0, HALF))
            pieces.append((renamed(piece, y_lane[block], 2 * LANES), number))
        codes, count = merge(codes, count, *join(pieces))
    list_own[...] = codes
    count_own = count

    pieces = []
    for block, tile in ((3, 0), (5, 1)):
        found = jnp.where(x_here >> 7 == block, x_here & (LANES - 1), -1)
        piece, number = aligned(block, OWN_AT, OWN_ROWS, COUNT_AT, found)
        home = pick(jnp.concatenate([x_home[block]] * (OWN_ROWS // 8), axis=0), piece & (LANES - 1))
        copy = jnp.where(home >> 7 == MIDDLE, 2 * LANES + (home & (LANES - 1)), -1)
        piece = jnp.where(
            piece < LANES, piece + tile * LANES, jnp.where(piece < 2 * LANES, copy, piece + LANES + tile * HALF)
        )
        pieces.append((piece, number))
    codes, count = join(pieces)
    codes = jnp.concatenate([codes, jnp.zeros((LIST_ROWS - OWN_ROWS, LANES), i32)], axis=0)
    codes, count = merge(
        codes, count, list_of(MIDDLE, X_AT) + 2 * LANES, row_of(MIDDLE, COUNT_AT + 1)
    )
    side_lane = {block: match("sides", block * LANES + lane) for block in AROUND}
    for blocks in ((1, 7), (0, 2, 6, 8)):
        pieces = []
        for block in blocks:
            piece, number = aligned(block, Y_AT, GHOST_ROWS, COUNT_AT + 2, match(("y", block), x_here, 0, HALF))
            pieces.append((renamed(piece, side_lane[block], 3 * LANES), number))
        codes, count = merge(codes, count, *join(pieces))
    codes_x, count_x = codes, count

    def tiled(home):
        block = home >> 7
        tile = jnp.where(block < 3, block, jnp.where(block > 5, block - 3, jnp.where(block == 3, 6, jnp.where(block == 5, 7, 8))))
        return jnp.where(home >= 0, tile * LANES + (home & (LANES - 1)), -1)

    pieces = []
    for block in AROUND:
        found = jnp.where(y_here >> 7 == block, y_here & (LANES - 1), -1)
        piece, number = aligned(block, OWN_AT, OWN_ROWS, COUNT_AT, found)
        slot = piece & (LANES - 1)
        copy_x = pick(jnp.concatenate([tiled(x_home[block])] * (OWN_ROWS // 8), axis=0), slot)
        copy_y = pick(jnp.concatenate([tiled(y_home[block])] * (OWN_ROWS // 8), axis=0), slot)
        piece = jnp.where(
            piece < LANES, piece + TILE_OF[block] * LANES, jnp.where(piece < 2 * LANES, copy_x, copy_y)
        )
        pieces.append((piece, number))
    codes, count = join(pieces)
    codes = jnp.concatenate([codes, jnp.zeros((LIST_ROWS - OWN_ROWS, LANES), i32)], axis=0)
    pieces = []
    for block in AROUND:
        piece, number = aligned(block, X_AT, GHOST_ROWS, COUNT_AT + 1, match(("x", block), y_here))
        pieces.append((piece + TILE_OF[block] * LANES, number))
    codes, count = merge(codes, count, *join(pieces))
    codes, count = merge(
        codes, count, list_of(MIDDLE, Y_AT) + TILE_OF[MIDDLE] * LANES, row_of(MIDDLE, COUNT_AT + 2)
    )
    pieces = []
    for block in (3, 5):
        piece, number = aligned(block, Y_AT, GHOST_ROWS, COUNT_AT + 2, match(("y", block), y_here, 0, HALF))
        pieces.append((piece + TILE_OF[block] * LANES, number))
    codes, count = merge(codes, count, *join(pieces))
    count = jnp.where(lane < HALF, count, 0)
    codes_y, count_y = codes, count

    earlier = (
        lax.broadcasted_iota(i32, (LIST_ROWS, LIST_ROWS), 1) < lax.broadcasted_iota(i32, (LIST_ROWS, LIST_ROWS), 0)
    ).astype(f32).astype(bf16)
    row = lax.broadcasted_iota(i32, (LIST_ROWS, LANES), 0)

    def own_first(codes, count, first):
        live = row < tall(count, LIST_ROWS)
        kept = live & (codes >= first) & (codes < first + LANES)
        weight = kept.astype(f32)
        total = jnp.sum(weight, axis=0, keepdims=True)
        rest = live.astype(f32) - weight
        rank = plain_dot(earlier, jnp.concatenate([weight, rest], axis=1).astype(bf16))
        place_at = jnp.where(kept, rank[:, 0:LANES], jnp.where(live, rank[:, LANES:] + total, -1.0))
        value = codes.astype(f32)
        rows = [
            jnp.sum(jnp.where(place_at == float(number), value, 0.0), axis=0, keepdims=True).astype(i32)
            for number in range(MOST_PAIRS)
        ]
        return rows, rep(total)

    list_x[...] = jnp.zeros_like(list_x)
    list_y[...] = jnp.zeros_like(list_y)
    rows_x, back_x = own_first(codes_x, count_x, 2 * LANES)
    for number in range(MOST_PAIRS):
        list_x[number : number + 1, :] = rows_x[number]
    rows_y, back_y = own_first(codes_y, count_y, TILE_OF[MIDDLE] * LANES)
    blank = jnp.zeros((1, LANES), i32)
    for number in range(0, MOST_PAIRS, 2):
        odd = rows_y[number + 1] if number + 1 < MOST_PAIRS else blank
        odd = pltpu.roll(rep(odd), HALF, axis=1)
        list_y[number // 2 : number // 2 + 1, :] = jnp.where(lane < HALF, rep(rows_y[number]), odd)[0:1, :]
    count_pack = jnp.where(lane < HALF, (count_y + 1) >> 1, pltpu.roll(count_y, HALF, axis=1) >> 1)

    sums_ref[...] = jnp.zeros_like(sums_ref)

    def most(count):
        return jnp.max(count.astype(f32)).astype(i32)

    pairs_own = (most(count_own) + 15) // 16
    pairs_x = (most(count_x) + 15) // 16
    pairs_y = (most(count_pack) + 15) // 16
    scratch = (table_ref, feature_ref, win_ref, wout_ref, sines_ref, slopes_ref, env_ref, shape_ref, geometry_ref, hidden_ref, radial_ref, partner_ref)
    forward_pairs(scratch, list_own, count_own, TILE_OWN, 3, TILE_OWN, 0, SLOT_OWN, True, 0, pairs_own, sums_ref)
    forward_pairs(scratch, list_x, count_x, 6, 4, TILE_X, LANES, SLOT_X, True, 0, jnp.minimum(pairs_x, 2), sums_ref)
    forward_pairs(scratch, list_x, count_x, 6, 4, TILE_X, LANES, SLOT_FREE, False, 2, pairs_x, sums_ref)
    forward_pairs(scratch, list_y, count_pack, 0, 9, TILE_Y, 2 * LANES, SLOT_Y, True, 0, jnp.minimum(pairs_y, 1), sums_ref)
    forward_pairs(scratch, list_y, count_pack, 0, 9, TILE_Y, 2 * LANES, SLOT_FREE, False, 1, pairs_y, sums_ref)
    sums_y = sums_ref[:, 2 * LANES : 3 * LANES]
    sums_ref[:, 2 * LANES : 3 * LANES] = sums_y + pltpu.roll(sums_y, HALF, axis=1)

    sums = sums_ref[...]
    square = sums * sums
    degree_one = square[64:128] + square[128:192] + square[192:256]
    degree_two = square[256:320] + square[320:384] + square[384:448] + square[448:512] + square[512:576]
    invariant = jnp.concatenate([square[0:64], degree_one, degree_two], axis=0)
    mixed = lax.dot_general(
        mix_ref[...], invariant, (((1,), (0,)), ((), ())), precision=highest, preferred_element_type=f32
    ) + table_ref[0:64, TILE_OWN * LANES : (TILE_Y + 1) * LANES]
    gate = 1.0 / (1.0 + jnp.exp(-mixed))
    weight = outw_ref[...]
    energy = jnp.sum(weight * (mixed * gate)[:, 0:LANES], axis=0, keepdims=True)
    kinds = species_ref[...]
    for kind in range(kind_ref.shape[0]):
        energy = energy + jnp.where(kinds == kind, kind_ref[kind], 0.0)
    energy_ref[...] = energy
    slope = weight * (gate * (1.0 + mixed * (1.0 - gate)))
    pulled = 2.0 * lax.dot_general(
        mix_ref[...], slope, (((0,), (0,)), ((), ())), precision=highest, preferred_element_type=f32
    )
    for q in range(9):
        degree = (0, 1, 1, 1, 2, 2, 2, 2, 2)[q]
        sums_ref[q * 64 : q * 64 + 64, :] = sums[q * 64 : q * 64 + 64] * pulled[degree * 64 : degree * 64 + 64]

    force_ref[...] = jnp.zeros_like(force_ref)
    scatter_ref[...] = jnp.zeros_like(scatter_ref)
    push_ref[...] = jnp.zeros_like(push_ref)
    scratch = (shape_ref, geometry_ref, radial_ref, partner_ref, pulled_ref, push_ref)
    backward_steps(scratch, list_own, (most(count_own) + 7) // 8, SLOT_OWN, 0, 0, sums_ref, force_ref, scatter_ref)
    backward_steps(scratch, list_x, (most(back_x) + 7) // 8, SLOT_X, 2 * LANES, LANES, sums_ref, None, scatter_ref)
    backward_steps(
        scratch, list_y, (most(back_y) + 15) // 16, SLOT_Y, TILE_OF[MIDDLE] * LANES, 2 * LANES, sums_ref, None, scatter_ref
    )
    force_out[...] = force_ref[0:3, :] - scatter_ref[0:3, :] - scatter_ref[3:6, :]


def main_pass(strip, low, high, win, wout, mix_weight, out_weight, species, species_energy):
    vmem = pl.BlockSpec(memory_space=pltpu.VMEM)
    wide = 8 * LANES
    return pl.pallas_call(
        main_kernel,
        out_shape=(jax.ShapeDtypeStruct((1, LANES), f32), jax.ShapeDtypeStruct((3, LANES), f32)),
        in_specs=[vmem] * 8 + [pl.BlockSpec(memory_space=pltpu.SMEM)],
        out_specs=(vmem, vmem),
        scratch_shapes=[
            pltpu.VMEM((72, TILES * LANES), f32),
            pltpu.VMEM((64, TILES * LANES), bf16),
            pltpu.VMEM((LANES, LANES), f32),
            pltpu.VMEM((LIST_ROWS, LANES), i32),
            pltpu.VMEM((LIST_ROWS, LANES), i32),
            pltpu.VMEM((32, LANES), i32),
            pltpu.VMEM((576, 3 * LANES), f32),
            pltpu.VMEM((8, LANES), f32),
            pltpu.VMEM((8, LANES), f32),
            pltpu.VMEM((128, LANES), f32),
            pltpu.VMEM((128, LANES), f32),
            pltpu.VMEM((32, LANES), f32),
            pltpu.VMEM((SLOTS, 72, LANES), f32),
            pltpu.VMEM((SLOTS, 40, LANES), f32),
            pltpu.VMEM((256, 2 * wide), bf16),
            pltpu.VMEM((SLOTS, 192, 2 * wide), f32),
            pltpu.VMEM((SLOTS, 64, wide), f32),
            pltpu.VMEM((72, LANES), f32),
            pltpu.VMEM((64, LANES), f32),
        ],
        compiler_params=pltpu.CompilerParams(vmem_limit_bytes=48 * 1024 * 1024),
    )(strip, low, high, win, wout, mix_weight, out_weight[:, None], species[None, :], species_energy)


def from_ring(block, axis):
    count = lax.axis_size(axis)
    up = [(i, (i + 1) % count) for i in range(count)]
    down = [(target, source) for source, target in up]
    return lax.ppermute(block, axis, up), lax.ppermute(block, axis, down)


def from_both_sides(block, axis):
    count = lax.axis_size(axis)

    def swapped(start):
        pairs = []
        for number in range(count):
            other = number + 1 if (number - start) % 2 == 0 else number - 1
            pairs.append((number, other if 0 <= other < count else number))
        return lax.ppermute(block, axis, pairs)

    even, odd = swapped(0), swapped(1)
    here = lax.axis_index(axis)
    upper_first = here % 2 == 0
    low = jnp.where(here > 0, jnp.where(upper_first, odd, even), 0.0)
    high = jnp.where(here < count - 1, jnp.where(upper_first, even, odd), 0.0)
    return low, high


def local(
    positions, features, species, edge_list, edge_count, send_list_x, send_list_y,
    radial_in, radial_out, mix_weight, out_weight, species_energy,
):
    own = make_payload(edge_list, edge_count, positions, features, send_list_x, send_list_y)
    left, right = from_ring(own, "gx")
    strip = jnp.concatenate([left, own, right], axis=0)
    low, high = from_both_sides(strip, "gy")
    win, wout = stacked_weights(radial_in, radial_out)
    energies, forces = main_pass(strip, low, high, win, wout, mix_weight, out_weight, species, species_energy)
    return energies[0], forces


def solution(mesh):
    placed = (
        P(None, ("gx", "gy")), P(None, ("gx", "gy")), P(("gx", "gy")), P(None, ("gx", "gy")), P(("gx", "gy")),
        P(("gx", "gy")), P(("gx", "gy")), P(), P(), P(), P(), P(),
    )
    return jax.shard_map(
        local, mesh=mesh, in_specs=placed, out_specs=(P(("gx", "gy")), P(None, ("gx", "gy"))), check_vma=False,
    )
```

```python
import math

import jax
import jax.numpy as jnp
import numpy as np
from jax import lax
from jax.experimental import pallas as pl
from jax.experimental.pallas import tpu as pltpu
from jax.sharding import PartitionSpec as P

cutoff_radius = 5.0
message_scale = 0.3
highest = lax.Precision.HIGHEST
f32 = jnp.float32
bf16 = jnp.bfloat16
i32 = jnp.int32

LANES = 128
EDGE_STEP = 256
OWN_ROWS = 56
GHOST_ROWS = 24
COUNT_AT, SEND_AT, OWN_AT, X_AT, Y_AT, PAYLOAD = 67, 70, 72, 128, 152, 168
EDGE_PARTS = 7
DEGREE_ROWS = ((0, 1), (1, 4), (4, 9))


def nt_dot(left, right):
    return lax.dot_general(left, right, (((1,), (1,)), ((), ())), preferred_element_type=f32)


def plain_dot(left, right):
    return lax.dot_general(left, right, (((1,), (0,)), ((), ())), preferred_element_type=f32)


def list_kernel(count_ref, edges_hbm, positions_hbm, features_hbm, send_x_hbm, send_y_hbm, out_ref, edges_ref, positions_ref,
                features_ref, send_x_ref, send_y_ref, arrived, count_out, own_acc, ghost_acc, own_base, ghost_base):
    copies = [
        pltpu.make_async_copy(source, target, arrived.at[number])
        for number, (source, target) in enumerate(
            (
                (edges_hbm, edges_ref),
                (positions_hbm, positions_ref),
                (features_hbm, features_ref),
                (send_x_hbm, send_x_ref),
                (send_y_hbm, send_y_ref),
            )
        )
    ]
    for copy in copies:
        copy.start()
    ghosts = ghost_base.shape[0]
    live_total = count_ref[0]
    own_acc[...] = jnp.zeros_like(own_acc)
    ghost_acc[...] = jnp.zeros_like(ghost_acc)
    own_base[...] = jnp.zeros_like(own_base)
    ghost_base[...] = jnp.zeros_like(ghost_base)
    count_out[...] = jnp.zeros_like(count_out)
    out_ref[...] = jnp.zeros_like(out_ref)
    before = lax.broadcasted_iota(i32, (EDGE_STEP, EDGE_STEP), 0) < lax.broadcasted_iota(
        i32, (EDGE_STEP, EDGE_STEP), 1
    )
    earlier = before.astype(f32).astype(bf16)
    every = jnp.ones((EDGE_STEP, EDGE_STEP), bf16)
    row = jnp.ones((8, EDGE_STEP), bf16)
    own_lane = lax.broadcasted_iota(i32, (LANES, EDGE_STEP), 0)
    ghost_lane = lax.broadcasted_iota(i32, (ghosts, EDGE_STEP), 0) + LANES
    own_rank = lax.broadcasted_iota(i32, (own_acc.shape[0], EDGE_STEP), 0).astype(f32)
    ghost_rank = lax.broadcasted_iota(i32, (ghost_acc.shape[0], EDGE_STEP), 0).astype(f32)
    span = EDGE_PARTS * EDGE_STEP
    copies[0].wait()

    def step(number, carry):
        blocks = []
        for part in range(EDGE_PARTS):
            offset = pl.multiple_of(number * span + part * EDGE_STEP, EDGE_STEP)
            first = edges_ref[0:1, pl.ds(offset, EDGE_STEP)]
            second = edges_ref[1:2, pl.ds(offset, EDGE_STEP)]
            live = offset + lax.broadcasted_iota(i32, (1, EDGE_STEP), 1) < live_total
            first = jnp.where(live, first, -1)
            second = jnp.where(live, second, -1)
            hot = [(own_lane == first).astype(f32), (own_lane == second).astype(f32), (ghost_lane == second).astype(f32)]
            low = [one.astype(bf16) for one in hot]
            ahead = [plain_dot(one, earlier) for one in low]
            total = [plain_dot(one, every) for one in low]
            blocks.append(((first - 160).astype(f32), (second - 160).astype(f32), hot, low, ahead, total))
        own_start = own_base[...]
        ghost_start = ghost_base[...]
        own_new, ghost_new = own_acc[...], ghost_acc[:, 0:ghosts]
        own_count, ghost_count = count_out[:, 0:LANES], count_out[:, LANES : LANES + ghosts]
        for first_code, second_code, hot, low, ahead, total in blocks:
            first_rank = jnp.sum(hot[0] * (own_start + ahead[0]), axis=0, keepdims=True)
            own_start = own_start + total[0]
            second_rank = jnp.sum(hot[1] * (own_start + ahead[1]), axis=0, keepdims=True)
            own_start = own_start + total[1]
            second_rank += jnp.sum(hot[2] * (ghost_start + ahead[2]), axis=0, keepdims=True)
            ghost_start = ghost_start + total[2]
            place_first = jnp.where(own_rank == first_rank, second_code, 0.0).astype(bf16)
            place_second = jnp.where(own_rank == second_rank, first_code, 0.0).astype(bf16)
            place_ghost = jnp.where(ghost_rank == second_rank, first_code, 0.0).astype(bf16)
            own_new = own_new + nt_dot(place_first, low[0]) + nt_dot(place_second, low[1])
            ghost_new = ghost_new + nt_dot(place_ghost, low[2])
            own_count = own_count + nt_dot(row, low[0]) + nt_dot(row, low[1])
            ghost_count = ghost_count + nt_dot(row, low[2])
        own_base[...] = own_start
        ghost_base[...] = ghost_start
        own_acc[...] = own_new
        ghost_acc[:, 0:ghosts] = ghost_new
        count_out[:, 0:LANES] = own_count
        count_out[:, LANES : LANES + ghosts] = ghost_count
        return carry

    lax.fori_loop(0, (live_total + span - 1) // span, step, 0)
    for copy in copies[1:]:
        copy.wait()
    own_code = own_acc[0:OWN_ROWS, :] + 160.0
    ghost_code = ghost_acc[0:GHOST_ROWS, :] + 160.0
    counts = count_out[0:1, :].astype(i32)
    own_live = lax.broadcasted_iota(i32, (OWN_ROWS, LANES), 0) < counts[:, 0:LANES]
    ghost_live = lax.broadcasted_iota(i32, ghost_code.shape, 0) < counts[:, LANES:]
    out_ref[0:64, :] = features_ref[...].astype(f32)
    out_ref[64:67, :] = positions_ref[...]
    out_ref[OWN_AT : OWN_AT + OWN_ROWS, :] = jnp.where(own_live, own_code, 0.0)
    ghost_code = jnp.where(ghost_live, ghost_code, 0.0)
    out_ref[X_AT : X_AT + GHOST_ROWS, :] = ghost_code[:, 0:LANES]
    copies_y = ghost_code[:, LANES:]
    out_ref[Y_AT : Y_AT + 16, :] = copies_y[0:16, :]
    lane = lax.broadcasted_iota(i32, (8, LANES), 1)
    out_ref[Y_AT : Y_AT + 8, :] = jnp.where(lane < LANES // 2, copies_y[0:8, :], pltpu.roll(copies_y[16:24, :], LANES // 2, axis=1))
    for group in range(3):
        out_ref[COUNT_AT + group : COUNT_AT + group + 1, :] = count_out[0:1, group * LANES : (group + 1) * LANES]
    out_ref[SEND_AT : SEND_AT + 1, :] = send_x_ref[...].astype(f32)
    out_ref[SEND_AT + 1 : SEND_AT + 2, 0 : send_y_ref.shape[1]] = send_y_ref[...].astype(f32)


def make_payload(edge_list, edge_count, positions, features, send_list_x, send_list_y):
    ghosts = send_list_x.shape[0] + send_list_y.shape[0]
    operands = (edge_list, positions, features, send_list_x[None, :], send_list_y[None, :])
    return pl.pallas_call(
        list_kernel,
        out_shape=jax.ShapeDtypeStruct((PAYLOAD, LANES), f32),
        in_specs=[pl.BlockSpec(memory_space=pltpu.SMEM)] + [pl.BlockSpec(memory_space=pl.ANY)] * 5,
        out_specs=pl.BlockSpec(memory_space=pltpu.VMEM),
        scratch_shapes=[pltpu.VMEM(operand.shape, operand.dtype) for operand in operands]
        + [
            pltpu.SemaphoreType.DMA((5,)),
            pltpu.VMEM((8, 3 * LANES), f32),
            pltpu.VMEM((64, LANES), f32),
            pltpu.VMEM((32, 2 * LANES), f32),
            pltpu.VMEM((LANES, EDGE_STEP), f32),
            pltpu.VMEM((ghosts, EDGE_STEP), f32),
        ],
        compiler_params=pltpu.CompilerParams(vmem_limit_bytes=56 * 1024 * 1024),
    )(edge_count, *operands)


def spread_row(ref, row, rows):
    return jnp.broadcast_to(ref[pl.ds(row, 1), :], (rows, LANES))


def lookup(table_ref, row, tile0, tiles, slot, block):
    result = None
    for number in range(tiles):
        at = (tile0 + number) * LANES
        entries = jnp.broadcast_to(table_ref[row : row + 1, at : at + LANES], (8, LANES))
        value = jnp.take_along_axis(entries, slot, axis=1)
        result = value if result is None else jnp.where(block == number, value, result)
    return result


def sine_cosine(scaled):
    angle = math.pi * (scaled - 0.5)
    square = angle * angle
    cosine = 1.0
    sine = 1.0
    for order in range(7, 0, -1):
        cosine = 1.0 - square * cosine * (1.0 / ((2 * order - 1) * (2 * order)))
        sine = 1.0 - square * sine * (1.0 / ((2 * order) * (2 * order + 1)))
    return cosine, -(angle * sine)


def pair_geometry(table_ref, codes, live, tile0, tiles, target, basis, tangent, sines_ref, slopes_ref):
    slot = codes & (LANES - 1)
    block = codes >> 7
    relative = []
    for axis in range(3):
        partner = lookup(table_ref, 64 + axis, tile0, tiles, slot, block)
        here = jnp.broadcast_to(
            table_ref[64 + axis : 65 + axis, target * LANES : (target + 1) * LANES], (8, LANES)
        )
        relative.append(jnp.where(live, partner - here, 2.0 if axis == 0 else 0.0))
    distance = jnp.sqrt(relative[0] * relative[0] + relative[1] * relative[1] + relative[2] * relative[2])
    inverse = 1.0 / distance
    direction = [part * inverse for part in relative]
    inside = live & (distance < cutoff_radius)
    scaled = jnp.minimum(distance, cutoff_radius) * (1.0 / cutoff_radius)
    room = 1.0 - scaled * scaled
    envelope = jnp.where(inside, message_scale * room * room, 0.0)
    envelope_slope = jnp.where(inside, (-4.0 * message_scale / cutoff_radius) * scaled * room, 0.0)
    sine, cosine = sine_cosine(scaled)
    twice = 2.0 * cosine
    scale = math.sqrt(2.0 / cutoff_radius)
    last_sine, last_cosine = jnp.zeros_like(sine), jnp.ones_like(sine)
    for order in range(1, basis + 1):
        wave = scale * sine * inverse
        sines_ref[(order - 1) * 8 : order * 8, :] = wave
        if tangent:
            slope = (scale * order * math.pi / cutoff_radius) * cosine * inverse - wave * inverse
            slopes_ref[(order - 1) * 8 : order * 8, :] = slope
        sine, last_sine = twice * sine - last_sine, sine
        cosine, last_cosine = twice * cosine - last_cosine, cosine
    return direction, inverse, envelope, envelope_slope, inside


def split_rows(ref, basis, at):
    pieces = []
    for row in range(8):
        whole = ref[pl.ds(at + row, basis, stride=8), :]
        high = whole.astype(bf16).astype(f32)
        rest = whole - high
        middle = rest.astype(bf16).astype(f32)
        low = rest - middle
        pieces.append(jnp.concatenate([high, middle, high, middle, low, high], axis=0).astype(bf16))
    return jnp.concatenate(pieces, axis=1)


def high_low(value):
    high = value.astype(bf16)
    low = (value - high.astype(f32)).astype(bf16)
    return high, low


def shapes_of(direction):
    x, y, z = direction
    three, five, fifteen = math.sqrt(3.0), math.sqrt(5.0), math.sqrt(15.0)
    return [
        jnp.ones_like(x),
        three * x,
        three * y,
        three * z,
        fifteen * x * y,
        fifteen * y * z,
        0.5 * five * (3.0 * z * z - 1.0),
        fifteen * x * z,
        0.5 * fifteen * (x * x - y * y),
    ]


def hot_codes(list_ref, offset, size, first):
    columns = []
    lane = lax.broadcasted_iota(i32, (size, LANES), 0) + first
    for row in range(8):
        codes = jnp.broadcast_to(list_ref[pl.ds(offset + row, 1), :], (size, LANES))
        columns.append((lane == codes).astype(f32).astype(bf16))
    return jnp.concatenate(columns, axis=1)


def forward_pairs(refs, list_ref, count_row, tile0, tiles, target, lane0, slot0, tangent, start, stop, out_ref):
    (table_ref, feature_ref, win_ref, wout_ref, sines_ref, slopes_ref, env_ref, shape_ref, geometry_ref, hidden_ref, radial_ref, partner_ref) = refs
    basis = win_ref.shape[1] // 6
    size = tiles * LANES
    first = tile0 * LANES
    wide = 8 * LANES
    count = count_row.astype(i32)
    rows_in = 8 * basis

    def step(number, carry):
        both = (0, 1)
        offset = [pl.multiple_of(number * 16 + part * 8, 8) for part in both]
        slot = slot0 + number if tangent else slot0
        for part in both:
            codes = list_ref[pl.ds(offset[part], 8), :]
            live = (offset[part] + lax.broadcasted_iota(i32, (8, LANES), 0) < count) & (codes >= 0)
            direction, inverse, envelope, envelope_slope, inside = pair_geometry(
                table_ref, codes, live, tile0, tiles, target, basis, tangent,
                sines_ref.at[pl.ds(part * rows_in, rows_in), :], slopes_ref.at[pl.ds(part * rows_in, rows_in), :],
            )
            env_ref[part * 16 : part * 16 + 8, :] = envelope
            shapes = shapes_of(direction)
            for q in range(1, 9):
                shape_ref[part][slot, q * 8 : q * 8 + 8, :] = shapes[q]
            if tangent:
                env_ref[part * 16 + 8 : part * 16 + 16, :] = envelope_slope
                for axis in range(3):
                    geometry_ref[part][slot, axis * 8 : axis * 8 + 8, :] = direction[axis]
                geometry_ref[part][slot, 24:32, :] = inverse
                geometry_ref[part][slot, 32:40, :] = inside.astype(f32)
        span = 2 * wide if tangent else wide
        stacked = []
        for part in both:
            stacked.append(split_rows(sines_ref, basis, part * rows_in))
            if tangent:
                stacked.append(split_rows(slopes_ref, basis, part * rows_in))
        value = plain_dot(win_ref[...], jnp.concatenate(stacked, axis=1))
        for part in both:
            if tiles > 4:
                hot = hot_codes(list_ref, offset[part], size, 0)
                partner_ref[part][slot] = plain_dot(feature_ref[:, first : first + size], hot)
            else:
                for row in range(8):
                    codes = jnp.broadcast_to(list_ref[pl.ds(offset[part] + row, 1), :], (8, LANES))
                    at_lane = codes & (LANES - 1)
                    tile = codes >> 7
                    for block in range(8):
                        result = None
                        for other in range(tiles):
                            entries = table_ref[block * 8 : block * 8 + 8, first + other * LANES : first + (other + 1) * LANES]
                            entry = jnp.take_along_axis(entries, at_lane, axis=1)
                            result = entry if result is None else jnp.where(tile == other, entry, result)
                        partner_ref[part][slot, block * 8 : block * 8 + 8, row * LANES : (row + 1) * LANES] = result
        for part in both:
            for row in range(8):
                lanes = slice(part * span + row * LANES, part * span + (row + 1) * LANES)
                here = value[:, lanes]
                scale = spread_row(env_ref, part * 16 + row, 64)
                gate = 1.0 / (1.0 + jnp.exp(-here))
                hidden = here * gate
                high, low = high_low(hidden * scale)
                hidden_ref[0:64, lanes] = high
                hidden_ref[64:128, lanes] = low
                if tangent:
                    later = slice(lanes.start + wide, lanes.stop + wide)
                    hidden_slope = gate * (1.0 + here * (1.0 - gate)) * value[:, later]
                    scale_slope = spread_row(env_ref, part * 16 + 8 + row, 64)
                    high, low = high_low(hidden * scale_slope + hidden_slope * scale)
                    hidden_ref[0:64, later] = high
                    hidden_ref[64:128, later] = low
        hidden = hidden_ref[:, 0 : 2 * span]
        radial = plain_dot(wout_ref[...], jnp.concatenate([hidden, hidden], axis=0))
        for part in both:
            radial_ref[part][slot, :, 0:span] = radial[:, part * span : (part + 1) * span]
        for block in range(8):
            sums = [
                out_ref[q * 64 + block * 8 : q * 64 + block * 8 + 8, lane0 : lane0 + LANES]
                for q in range(9)
            ]
            for part in both:
                for row in range(8):
                    lanes = slice(row * LANES, (row + 1) * LANES)
                    feature = partner_ref[part][slot, block * 8 : block * 8 + 8, lanes]
                    for degree, (low, high) in enumerate(DEGREE_ROWS):
                        at = degree * 64 + block * 8
                        weight = radial_ref[part][slot, at : at + 8, lanes] * feature
                        for q in range(low, high):
                            if q == 0:
                                sums[q] = sums[q] + weight
                            else:
                                shape = jnp.broadcast_to(shape_ref[part][slot, q * 8 + row : q * 8 + row + 1, :], (8, LANES))
                                sums[q] = sums[q] + weight * shape
            for q in range(9):
                out_ref[q * 64 + block * 8 : q * 64 + block * 8 + 8, lane0 : lane0 + LANES] = sums[q]
        return carry

    lax.fori_loop(start, stop, step, 0)


def backward_steps(refs, steps, slot0, chunk0, lane0, gradient_ref):
    shape_ref, geometry_ref, radial_ref, partner_ref, pulled_ref = refs
    wide = 8 * LANES

    def block_step(number, part, chunk):
        slot = slot0 + number
        for row in range(8):
            lanes = slice(row * LANES, (row + 1) * LANES)
            later = slice(wide + row * LANES, wide + (row + 1) * LANES)
            pulled = [jnp.zeros((8, LANES), f32) for q in range(9)]
            spoke = pulled[0]
            shapes = [None] + [
                jnp.broadcast_to(shape_ref[part][slot, q * 8 + row : q * 8 + row + 1, :], (8, LANES)) for q in range(1, 9)
            ]
            for block in range(8):
                feature = partner_ref[part][slot, block * 8 : block * 8 + 8, lanes]
                for degree, (low, high) in enumerate(DEGREE_ROWS):
                    at = degree * 64 + block * 8
                    weight = radial_ref[part][slot, at : at + 8, lanes] * feature
                    weight_slope = radial_ref[part][slot, at : at + 8, later] * feature
                    mixed = None
                    for q in range(low, high):
                        gradient = gradient_ref[q * 64 + block * 8 : q * 64 + block * 8 + 8, lane0 : lane0 + LANES]
                        if q > 0:
                            pulled[q] = pulled[q] + weight * gradient
                            gradient = gradient * shapes[q]
                        mixed = gradient if mixed is None else mixed + gradient
                    spoke = spoke + weight_slope * mixed
            pulled[0] = spoke
            for q in range(9):
                pulled_ref[chunk, q * 64 + row * 8 : q * 64 + row * 8 + 8, :] = pulled[q]

    def step(number, carry):
        block_step(number, 0, chunk0 + number * 2)

        @pl.when(number * 2 + 1 < steps)
        def _():
            block_step(number, 1, chunk0 + number * 2 + 1)

        return carry

    lax.fori_loop(0, (steps + 1) // 2, step, 0)


def pair_forces(refs, list_ref, chunks, steps, slot0, chunk0, own_code, push_ref):
    shape_ref, geometry_ref, radial_ref, partner_ref, pulled_ref = refs
    three, five, fifteen = math.sqrt(3.0), math.sqrt(5.0), math.sqrt(15.0)
    on_target = [jnp.zeros((8, LANES), f32) for axis in range(3)]
    on_partner = jnp.zeros((8, LANES), f32)
    for chunk in range(chunks):
        part, slot = chunk % 2, slot0 + chunk // 2
        x, y, z = direction = [geometry_ref[part][slot, axis * 8 : axis * 8 + 8, :] for axis in range(3)]
        inverse = geometry_ref[part][slot, 24:32, :]
        inside = (geometry_ref[part][slot, 32:40, :] > 0.5) & (chunk < steps)
        p = []
        for q in range(9):
            parts = [pulled_ref[chunk0 + chunk, pl.ds(q * 64 + sub, 8, stride=8), :] for sub in range(8)]
            while len(parts) > 1:
                parts = [parts[i] + parts[i + 1] for i in range(0, len(parts), 2)]
            p.append(parts[0])
        turn = [
            three * p[1] + fifteen * (y * p[4] + z * p[7] + x * p[8]),
            three * p[2] + fifteen * (x * p[4] + z * p[5] - y * p[8]),
            three * p[3] + fifteen * (y * p[5] + x * p[7]) + (3.0 * five) * z * p[6],
        ]
        along = x * turn[0] + y * turn[1] + z * turn[2]
        base = (chunk0 + chunk) * 64
        for axis in range(3):
            force = (turn[axis] - direction[axis] * along) * inverse + direction[axis] * p[0]
            force = jnp.where(inside, force, 0.0)
            on_target[axis] = on_target[axis] + force
            high = force.astype(bf16).astype(f32)
            push_ref[base + axis * 8 : base + axis * 8 + 8, :] = high
            push_ref[base + 24 + axis * 8 : base + 32 + axis * 8, :] = force - high
        push = jnp.concatenate([push_ref[pl.ds(base + row, 8, stride=8), :] for row in range(8)], axis=1)
        hot = hot_codes(list_ref, chunk * 8, LANES, own_code)
        on_partner = on_partner + nt_dot(push.astype(bf16), hot)
    return on_target, on_partner


def rounded(value):
    return lax.reduce_precision(value, 8, 7)


def stacked_weights(radial_in, radial_out):
    high = rounded(radial_in)
    middle = rounded(radial_in - high)
    low = rounded(radial_in - high - middle)
    win = jnp.concatenate([high, high, middle, middle, high, low], axis=1).astype(bf16)
    high = rounded(radial_out)
    low = rounded(radial_out - high)
    wout = jnp.concatenate([high, high, low, low], axis=1).astype(bf16)
    return win, wout


HALF = LANES // 2
QUARTER = LANES // 4
MIDDLE = 4
AROUND = (0, 1, 2, 6, 7, 8)
TILE_OF = {0: 0, 1: 1, 2: 2, 6: 3, 7: 4, 8: 5, 3: 6, 5: 7, 4: 8}
TILE_LR, TILE_OWN, TILE_X, TILE_Y, TILES = 9, 10, 11, 12, 13
LIST_ROWS = 64
MOST_PAIRS = 49
SLOT_OWN, SLOT_X, SLOT_Y, SLOT_FREE, SLOTS = 0, 4, 6, 7, 8


def rep(row):
    return jnp.broadcast_to(row, (8, LANES))


def tall(value, rows):
    return jnp.concatenate([value] * (rows // 8), axis=0)


def pick(values, slots):
    return jnp.take_along_axis(values, tall(slots, values.shape[0]) if slots.shape[0] != values.shape[0] else slots, axis=1)


def merge(base, count, segment, more):
    rows = base.shape[0]
    if segment.shape[0] < rows:
        segment = jnp.concatenate([segment, jnp.zeros((rows - segment.shape[0], LANES), i32)], axis=0)
    shift = tall(count, rows)
    for bit in (1, 2, 4, 8, 16, 32):
        segment = jnp.where((shift & bit) != 0, pltpu.roll(segment, bit, axis=0), segment)
    row = lax.broadcasted_iota(i32, (rows, LANES), 0)
    return jnp.where(row < shift, base, segment), count + more


def join(pieces):
    codes, count = pieces[0]
    for other, number in pieces[1:]:
        codes = jnp.where(tall(number, other.shape[0]) > 0, other, codes)
        count = count + number
    return codes, count


def main_kernel(strip_ref, low_ref, high_ref, win_ref, wout_ref, mix_ref, outw_ref, shift_ref,
                energy_ref, force_out, table_ref, feature_ref, column_ref, list_own, list_x, list_y,
                sums_ref, sines_ref, slopes_ref, env_ref, hidden_ref, pulled_ref, push_ref, *kept):
    shape_ref, geometry_ref, radial_ref, partner_ref = (kept[number : number + 2] for number in range(0, 8, 2))
    refs = (low_ref, strip_ref, high_ref)

    def rows_of(block, at, size):
        start = (block % 3) * PAYLOAD + at
        return refs[block // 3][start : start + size, :]

    def list_of(block, at):
        if at == X_AT:
            return rows_of(block, at, GHOST_ROWS).astype(i32)
        folded = rows_of(block, at, 16)
        return jnp.concatenate([folded, pltpu.roll(folded[0:8, :], HALF, axis=1)], axis=0).astype(i32)

    def row_of(block, at):
        return rep(rows_of(block, at, 1).astype(i32))

    lane = lax.broadcasted_iota(i32, (8, LANES), 1)
    none = jnp.full((8, LANES), -1, i32)

    x_home = {}
    for block in range(9):
        dx = block % 3
        lower = (block - 1) * LANES + pltpu.roll(row_of(block - 1, SEND_AT), HALF, axis=1) if dx > 0 else none
        upper = (block + 1) * LANES + pltpu.roll(row_of(block + 1, SEND_AT), HALF, axis=1) if dx < 2 else none
        x_home[block] = jnp.where(lane < HALF, lower, upper)

    def section_home(block, entry):
        copies = jnp.take_along_axis(x_home[block], entry & (LANES - 1), axis=1)
        return jnp.where(entry < LANES, block * LANES + entry, copies)

    y_home = {}
    for block in range(9):
        dy = block // 3
        if dy > 0:
            lower = section_home(block - 3, pltpu.roll(row_of(block - 3, SEND_AT + 1), LANES - QUARTER, axis=1))
        else:
            lower = none
        if dy < 2:
            upper = section_home(block + 3, pltpu.roll(row_of(block + 3, SEND_AT + 1), QUARTER, axis=1))
        else:
            upper = none
        y_home[block] = jnp.where(lane < QUARTER, lower, jnp.where(lane < HALF, upper, none))

    x_here = x_home[MIDDLE]
    y_here = y_home[MIDDLE]
    y_twice = jnp.where(lane < HALF, y_here, pltpu.roll(y_here, HALF, axis=1))
    y_sides = jnp.where(lane < HALF, y_home[3], pltpu.roll(y_home[5], HALF, axis=1))

    column_ref[...] = jnp.zeros_like(column_ref)
    slots = {}

    def as_column(name, value):
        slots[name] = len(slots)
        column_ref[slots[name] : slots[name] + 1, :] = value[0:1, :].astype(f32)

    as_column("sent", row_of(MIDDLE, SEND_AT))
    as_column("x", x_here)
    as_column("y", y_here)
    as_column("sides", y_sides)
    for block in range(9):
        if block != MIDDLE:
            as_column(("y", block), y_home[block])
    for block in AROUND:
        as_column(("x", block), x_home[block])
    columns = jnp.transpose(column_ref[...])
    place = lax.broadcasted_iota(i32, (LANES, LANES), 0).astype(f32)

    def match(name, target, low=0, high=LANES):
        number = slots[name]
        same = columns[low:high, number : number + 1] == target[0:1, :].astype(f32)
        return rep(jnp.max(jnp.where(same, place[low:high, :], -1.0), axis=0, keepdims=True).astype(i32))

    def gathered(home, blocks, rows, at):
        block_of = home >> 7
        slot = home & (LANES - 1)
        result = jnp.zeros((rows, LANES), f32)
        for block in blocks:
            result = jnp.where(tall(block_of, rows) == block, pick(rows_of(block, at, rows), slot), result)
        return result

    for block, tile in TILE_OF.items():
        table_ref[:, tile * LANES : (tile + 1) * LANES] = rows_of(block, 0, 72)
    table_ref[:, TILE_OWN * LANES : (TILE_OWN + 1) * LANES] = rows_of(MIDDLE, 0, 72)
    table_ref[:, TILE_X * LANES : (TILE_X + 1) * LANES] = gathered(x_here, (3, 5), 72, 0)
    table_ref[:, TILE_Y * LANES : (TILE_Y + 1) * LANES] = gathered(y_twice, AROUND, 72, 0)
    table_ref[:, TILE_LR * LANES : (TILE_LR + 1) * LANES] = gathered(y_sides, AROUND, 72, 0)
    feature_ref[...] = table_ref[0:64, :].astype(bf16)

    def aligned(block, at, rows, count_at, found):
        at_lane = jnp.maximum(found, 0)
        codes = rows_of(block, at, rows).astype(i32) if at == OWN_AT else list_of(block, at)
        codes = pick(codes, at_lane)
        count = jnp.take_along_axis(row_of(block, count_at), at_lane, axis=1)
        return codes, jnp.where(found >= 0, count, 0)

    def renamed(codes, table, offset):
        found = pick(jnp.concatenate([table] * (codes.shape[0] // 8), axis=0), codes & (LANES - 1))
        return jnp.where(found >= 0, found + offset, -1)

    own_home = MIDDLE * LANES + lane
    codes = jnp.concatenate([rows_of(MIDDLE, OWN_AT, OWN_ROWS).astype(i32), jnp.zeros((LIST_ROWS - OWN_ROWS, LANES), i32)], axis=0)
    count = row_of(MIDDLE, COUNT_AT)
    found_low = match("sent", lane, 0, HALF)
    found_low = jnp.where(found_low >= 0, found_low + HALF, -1)
    found_high = match("sent", lane, HALF, LANES)
    found_high = jnp.where(found_high >= 0, found_high - HALF, -1)
    pieces = []
    for block, found in ((3, found_low), (5, found_high)):
        piece, number = aligned(block, X_AT, GHOST_ROWS, COUNT_AT + 1, found)
        pieces.append((renamed(piece, match("x", block * LANES + lane), LANES), number))
    codes, count = merge(codes, count, *join(pieces))
    y_lane = {block: match("y", block * LANES + lane) for block in AROUND}
    for blocks in ((1, 7), (0, 2, 6, 8)):
        pieces = []
        for block in blocks:
            piece, number = aligned(block, Y_AT, GHOST_ROWS, COUNT_AT + 2, match(("y", block), own_home, 0, HALF))
            pieces.append((renamed(piece, y_lane[block], 2 * LANES), number))
        codes, count = merge(codes, count, *join(pieces))
    list_own[...] = codes
    count_own = count

    pieces = []
    for block, tile in ((3, 0), (5, 1)):
        found = jnp.where(x_here >> 7 == block, x_here & (LANES - 1), -1)
        piece, number = aligned(block, OWN_AT, OWN_ROWS, COUNT_AT, found)
        home = pick(jnp.concatenate([x_home[block]] * (OWN_ROWS // 8), axis=0), piece & (LANES - 1))
        copy = jnp.where(home >> 7 == MIDDLE, 2 * LANES + (home & (LANES - 1)), -1)
        piece = jnp.where(
            piece < LANES, piece + tile * LANES, jnp.where(piece < 2 * LANES, copy, piece + LANES + tile * HALF)
        )
        pieces.append((piece, number))
    codes, count = join(pieces)
    codes = jnp.concatenate([codes, jnp.zeros((LIST_ROWS - OWN_ROWS, LANES), i32)], axis=0)
    codes, count = merge(
        codes, count, list_of(MIDDLE, X_AT) + 2 * LANES, row_of(MIDDLE, COUNT_AT + 1)
    )
    side_lane = {block: match("sides", block * LANES + lane) for block in AROUND}
    for blocks in ((1, 7), (0, 2, 6, 8)):
        pieces = []
        for block in blocks:
            piece, number = aligned(block, Y_AT, GHOST_ROWS, COUNT_AT + 2, match(("y", block), x_here, 0, HALF))
            pieces.append((renamed(piece, side_lane[block], 3 * LANES), number))
        codes, count = merge(codes, count, *join(pieces))
    codes_x, count_x = codes, count

    def tiled(home):
        block = home >> 7
        tile = jnp.where(block < 3, block, jnp.where(block > 5, block - 3, jnp.where(block == 3, 6, jnp.where(block == 5, 7, 8))))
        return jnp.where(home >= 0, tile * LANES + (home & (LANES - 1)), -1)

    pieces = []
    for block in AROUND:
        found = jnp.where(y_here >> 7 == block, y_here & (LANES - 1), -1)
        piece, number = aligned(block, OWN_AT, OWN_ROWS, COUNT_AT, found)
        slot = piece & (LANES - 1)
        copy_x = pick(jnp.concatenate([tiled(x_home[block])] * (OWN_ROWS // 8), axis=0), slot)
        copy_y = pick(jnp.concatenate([tiled(y_home[block])] * (OWN_ROWS // 8), axis=0), slot)
        piece = jnp.where(
            piece < LANES, piece + TILE_OF[block] * LANES, jnp.where(piece < 2 * LANES, copy_x, copy_y)
        )
        pieces.append((piece, number))
    codes, count = join(pieces)
    codes = jnp.concatenate([codes, jnp.zeros((LIST_ROWS - OWN_ROWS, LANES), i32)], axis=0)
    pieces = []
    for block in AROUND:
        piece, number = aligned(block, X_AT, GHOST_ROWS, COUNT_AT + 1, match(("x", block), y_here))
        pieces.append((piece + TILE_OF[block] * LANES, number))
    codes, count = merge(codes, count, *join(pieces))
    codes, count = merge(
        codes, count, list_of(MIDDLE, Y_AT) + TILE_OF[MIDDLE] * LANES, row_of(MIDDLE, COUNT_AT + 2)
    )
    pieces = []
    for block in (3, 5):
        piece, number = aligned(block, Y_AT, GHOST_ROWS, COUNT_AT + 2, match(("y", block), y_here, 0, HALF))
        pieces.append((piece + TILE_OF[block] * LANES, number))
    codes, count = merge(codes, count, *join(pieces))
    count = jnp.where(lane < HALF, count, 0)
    codes_y, count_y = codes, count

    earlier = (
        lax.broadcasted_iota(i32, (LIST_ROWS, LIST_ROWS), 1) < lax.broadcasted_iota(i32, (LIST_ROWS, LIST_ROWS), 0)
    ).astype(f32).astype(bf16)
    row = lax.broadcasted_iota(i32, (LIST_ROWS, LANES), 0)

    def own_first(codes, count, first):
        live = row < tall(count, LIST_ROWS)
        kept = live & (codes >= first) & (codes < first + LANES)
        weight = kept.astype(f32)
        total = jnp.sum(weight, axis=0, keepdims=True)
        rest = live.astype(f32) - weight
        rank = plain_dot(earlier, jnp.concatenate([weight, rest], axis=1).astype(bf16))
        place_at = jnp.where(kept, rank[:, 0:LANES], jnp.where(live, rank[:, LANES:] + total, -1.0))
        value = codes.astype(f32)
        rows = [
            jnp.sum(jnp.where(place_at == float(number), value, 0.0), axis=0, keepdims=True).astype(i32)
            for number in range(MOST_PAIRS)
        ]
        return rows, rep(total)

    list_x[...] = jnp.zeros_like(list_x)
    list_y[...] = jnp.zeros_like(list_y)
    rows_x, back_x = own_first(codes_x, count_x, 2 * LANES)
    for number in range(MOST_PAIRS):
        list_x[number : number + 1, :] = rows_x[number]
    rows_y, back_y = own_first(codes_y, count_y, TILE_OF[MIDDLE] * LANES)
    blank = jnp.zeros((1, LANES), i32)
    for number in range(0, MOST_PAIRS, 2):
        odd = rows_y[number + 1] if number + 1 < MOST_PAIRS else blank
        odd = pltpu.roll(rep(odd), HALF, axis=1)
        list_y[number // 2 : number // 2 + 1, :] = jnp.where(lane < HALF, rep(rows_y[number]), odd)[0:1, :]
    count_pack = jnp.where(lane < HALF, (count_y + 1) >> 1, pltpu.roll(count_y, HALF, axis=1) >> 1)

    sums_ref[...] = jnp.zeros_like(sums_ref)

    def most(count):
        return jnp.max(count.astype(f32)).astype(i32)

    pairs_own = (most(count_own) + 15) // 16
    pairs_x = (most(count_x) + 15) // 16
    pairs_y = (most(count_pack) + 15) // 16
    scratch = (table_ref, feature_ref, win_ref, wout_ref, sines_ref, slopes_ref, env_ref, shape_ref, geometry_ref, hidden_ref, radial_ref, partner_ref)
    forward_pairs(scratch, list_own, count_own, TILE_OWN, 3, TILE_OWN, 0, SLOT_OWN, True, 0, pairs_own, sums_ref)
    forward_pairs(scratch, list_x, count_x, 6, 4, TILE_X, LANES, SLOT_X, True, 0, jnp.minimum(pairs_x, 2), sums_ref)
    forward_pairs(scratch, list_x, count_x, 6, 4, TILE_X, LANES, SLOT_FREE, False, 2, pairs_x, sums_ref)
    forward_pairs(scratch, list_y, count_pack, 0, 9, TILE_Y, 2 * LANES, SLOT_Y, True, 0, jnp.minimum(pairs_y, 1), sums_ref)
    forward_pairs(scratch, list_y, count_pack, 0, 9, TILE_Y, 2 * LANES, SLOT_FREE, False, 1, pairs_y, sums_ref)
    sums_y = sums_ref[:, 2 * LANES : 3 * LANES]
    sums_ref[:, 2 * LANES : 3 * LANES] = sums_y + pltpu.roll(sums_y, HALF, axis=1)

    sums = sums_ref[...]
    square = sums * sums
    degree_one = square[64:128] + square[128:192] + square[192:256]
    degree_two = square[256:320] + square[320:384] + square[384:448] + square[448:512] + square[512:576]
    invariant = jnp.concatenate([square[0:64], degree_one, degree_two], axis=0)
    mixed = lax.dot_general(
        mix_ref[...], invariant, (((1,), (0,)), ((), ())), precision=highest, preferred_element_type=f32
    ) + table_ref[0:64, TILE_OWN * LANES : (TILE_Y + 1) * LANES]
    gate = 1.0 / (1.0 + jnp.exp(-mixed))
    weight = outw_ref[...]
    energy = jnp.sum(weight * (mixed * gate)[:, 0:LANES], axis=0, keepdims=True)
    energy_ref[...] = energy + shift_ref[...]
    slope = weight * (gate * (1.0 + mixed * (1.0 - gate)))
    pulled = 2.0 * lax.dot_general(
        mix_ref[...], slope, (((0,), (0,)), ((), ())), precision=highest, preferred_element_type=f32
    )
    for q in range(9):
        degree = (0, 1, 1, 1, 2, 2, 2, 2, 2)[q]
        sums_ref[q * 64 : q * 64 + 64, :] = sums[q * 64 : q * 64 + 64] * pulled[degree * 64 : degree * 64 + 64]

    push_ref[...] = jnp.zeros_like(push_ref)
    scratch = (shape_ref, geometry_ref, radial_ref, partner_ref, pulled_ref)
    steps_own = (most(count_own) + 7) // 8
    steps_x = (most(back_x) + 7) // 8
    steps_y = (most(back_y) + 15) // 16
    backward_steps(scratch, steps_own, SLOT_OWN, 0, 0, sums_ref)
    backward_steps(scratch, steps_x, SLOT_X, 7, LANES, sums_ref)
    backward_steps(scratch, steps_y, SLOT_Y, 10, 2 * LANES, sums_ref)
    forces, pushed = pair_forces(scratch, list_own, 7, steps_own, SLOT_OWN, 0, 0, push_ref)
    pushed = pushed + pair_forces(scratch, list_x, 3, steps_x, SLOT_X, 7, 2 * LANES, push_ref)[1]
    pushed = pushed + pair_forces(scratch, list_y, 2, steps_y, SLOT_Y, 10, TILE_OF[MIDDLE] * LANES, push_ref)[1]
    for axis in range(3):
        force_out[axis : axis + 1, :] = (
            jnp.sum(forces[axis], axis=0, keepdims=True) - pushed[axis : axis + 1, :] - pushed[axis + 3 : axis + 4, :]
        )


def main_pass(strip, low, high, win, wout, mix_weight, out_weight, shift):
    vmem = pl.BlockSpec(memory_space=pltpu.VMEM)
    wide = 8 * LANES
    return pl.pallas_call(
        main_kernel,
        out_shape=(jax.ShapeDtypeStruct((1, LANES), f32), jax.ShapeDtypeStruct((3, LANES), f32)),
        in_specs=[vmem] * 8,
        out_specs=(vmem, vmem),
        scratch_shapes=[
            pltpu.VMEM((72, TILES * LANES), f32),
            pltpu.VMEM((64, TILES * LANES), bf16),
            pltpu.VMEM((LANES, LANES), f32),
            pltpu.VMEM((LIST_ROWS, LANES), i32),
            pltpu.VMEM((LIST_ROWS, LANES), i32),
            pltpu.VMEM((32, LANES), i32),
            pltpu.VMEM((576, 3 * LANES), f32),
            pltpu.VMEM((128, LANES), f32),
            pltpu.VMEM((128, LANES), f32),
            pltpu.VMEM((32, LANES), f32),
            pltpu.VMEM((128, 4 * wide), bf16),
            pltpu.VMEM((12, 576, LANES), f32),
            pltpu.VMEM((12 * 64, LANES), f32),
        ]
        + [pltpu.VMEM((SLOTS, 72, LANES), f32)] * 2
        + [pltpu.VMEM((SLOTS, 40, LANES), f32)] * 2
        + [pltpu.VMEM((SLOTS, 192, 2 * wide), f32)] * 2
        + [pltpu.VMEM((SLOTS, 64, wide), f32)] * 2,
        compiler_params=pltpu.CompilerParams(vmem_limit_bytes=48 * 1024 * 1024),
    )(strip, low, high, win, wout, mix_weight, out_weight[:, None], shift)


def from_ring(block, axis):
    count = lax.axis_size(axis)
    up = [(i, (i + 1) % count) for i in range(count)]
    down = [(target, source) for source, target in up]
    return lax.ppermute(block, axis, up), lax.ppermute(block, axis, down)


def from_both_sides(block, axis):
    count = lax.axis_size(axis)

    def swapped(start):
        pairs = []
        for number in range(count):
            other = number + 1 if (number - start) % 2 == 0 else number - 1
            pairs.append((number, other if 0 <= other < count else number))
        return lax.ppermute(block, axis, pairs)

    even, odd = swapped(0), swapped(1)
    here = lax.axis_index(axis)
    upper_first = here % 2 == 0
    low = jnp.where(here > 0, jnp.where(upper_first, odd, even), 0.0)
    high = jnp.where(here < count - 1, jnp.where(upper_first, even, odd), 0.0)
    return low, high


def local(
    positions, features, species, edge_list, edge_count, send_list_x, send_list_y,
    radial_in, radial_out, mix_weight, out_weight, species_energy,
):
    own = make_payload(edge_list, edge_count, positions, features, send_list_x, send_list_y)
    left, right = from_ring(own, "gx")
    strip = jnp.concatenate([left, own, right], axis=0)
    low, high = from_both_sides(strip, "gy")
    win, wout = stacked_weights(radial_in, radial_out)
    kinds = jnp.arange(species_energy.shape[0], dtype=i32)
    shift = jnp.sum(jnp.where(species[None, :] == kinds[:, None], species_energy[:, None], 0.0), axis=0)[None, :]
    energies, forces = main_pass(strip, low, high, win, wout, mix_weight, out_weight, shift)
    return energies[0], forces


def solution(mesh):
    placed = (
        P(None, ("gx", "gy")), P(None, ("gx", "gy")), P(("gx", "gy")), P(None, ("gx", "gy")), P(("gx", "gy")),
        P(("gx", "gy")), P(("gx", "gy")), P(), P(), P(), P(), P(),
    )
    return jax.shard_map(
        local, mesh=mesh, in_specs=placed, out_specs=(P(("gx", "gy")), P(None, ("gx", "gy"))), check_vma=False,
    )
```

```python
import math

import jax
import jax.numpy as jnp
import numpy as np
from jax import lax
from jax.experimental import pallas as pl
from jax.experimental.pallas import tpu as pltpu
from jax.sharding import PartitionSpec as P

cutoff_radius = 5.0
message_scale = 0.3
highest = lax.Precision.HIGHEST
f32 = jnp.float32
bf16 = jnp.bfloat16
i32 = jnp.int32

LANES = 128
EDGE_STEP = 256
OWN_ROWS = 56
GHOST_ROWS = 24
COUNT_AT, SEND_AT, OWN_AT, X_AT, Y_AT, PAYLOAD = 67, 70, 72, 128, 152, 168
EDGE_PARTS = 7
DEGREE_ROWS = ((0, 1), (1, 4), (4, 9))


def nt_dot(left, right):
    return lax.dot_general(left, right, (((1,), (1,)), ((), ())), preferred_element_type=f32)


def plain_dot(left, right):
    return lax.dot_general(left, right, (((1,), (0,)), ((), ())), preferred_element_type=f32)


def list_kernel(count_ref, edges_hbm, positions_hbm, features_hbm, send_x_hbm, send_y_hbm, out_ref, edges_ref, positions_ref,
                features_ref, send_x_ref, send_y_ref, arrived, count_out, own_acc, ghost_acc, own_base, ghost_base):
    copies = [
        pltpu.make_async_copy(source, target, arrived.at[number])
        for number, (source, target) in enumerate(
            (
                (edges_hbm, edges_ref),
                (positions_hbm, positions_ref),
                (features_hbm, features_ref),
                (send_x_hbm, send_x_ref),
                (send_y_hbm, send_y_ref),
            )
        )
    ]
    for copy in copies:
        copy.start()
    ghosts = ghost_base.shape[0]
    live_total = count_ref[0]
    own_acc[...] = jnp.zeros_like(own_acc)
    ghost_acc[...] = jnp.zeros_like(ghost_acc)
    own_base[...] = jnp.zeros_like(own_base)
    ghost_base[...] = jnp.zeros_like(ghost_base)
    count_out[...] = jnp.zeros_like(count_out)
    out_ref[...] = jnp.zeros_like(out_ref)
    before = lax.broadcasted_iota(i32, (EDGE_STEP, EDGE_STEP), 0) < lax.broadcasted_iota(
        i32, (EDGE_STEP, EDGE_STEP), 1
    )
    earlier = before.astype(f32).astype(bf16)
    every = jnp.ones((EDGE_STEP, EDGE_STEP), bf16)
    row = jnp.ones((8, EDGE_STEP), bf16)
    own_lane = lax.broadcasted_iota(i32, (LANES, EDGE_STEP), 0)
    ghost_lane = lax.broadcasted_iota(i32, (ghosts, EDGE_STEP), 0) + LANES
    own_rank = lax.broadcasted_iota(i32, (own_acc.shape[0], EDGE_STEP), 0).astype(f32)
    ghost_rank = lax.broadcasted_iota(i32, (ghost_acc.shape[0], EDGE_STEP), 0).astype(f32)
    span = EDGE_PARTS * EDGE_STEP
    copies[0].wait()

    def step(number, carry):
        blocks = []
        for part in range(EDGE_PARTS):
            offset = pl.multiple_of(number * span + part * EDGE_STEP, EDGE_STEP)
            first = edges_ref[0:1, pl.ds(offset, EDGE_STEP)]
            second = edges_ref[1:2, pl.ds(offset, EDGE_STEP)]
            live = offset + lax.broadcasted_iota(i32, (1, EDGE_STEP), 1) < live_total
            first = jnp.where(live, first, -1)
            second = jnp.where(live, second, -1)
            hot = [(own_lane == first).astype(f32), (own_lane == second).astype(f32), (ghost_lane == second).astype(f32)]
            low = [one.astype(bf16) for one in hot]
            ahead = [plain_dot(one, earlier) for one in low]
            total = [plain_dot(one, every) for one in low]
            blocks.append(((first - 160).astype(f32), (second - 160).astype(f32), hot, low, ahead, total))
        own_start = own_base[...]
        ghost_start = ghost_base[...]
        own_new, ghost_new = own_acc[...], ghost_acc[:, 0:ghosts]
        own_count, ghost_count = count_out[:, 0:LANES], count_out[:, LANES : LANES + ghosts]
        for first_code, second_code, hot, low, ahead, total in blocks:
            first_rank = jnp.sum(hot[0] * (own_start + ahead[0]), axis=0, keepdims=True)
            own_start = own_start + total[0]
            second_rank = jnp.sum(hot[1] * (own_start + ahead[1]), axis=0, keepdims=True)
            own_start = own_start + total[1]
            second_rank += jnp.sum(hot[2] * (ghost_start + ahead[2]), axis=0, keepdims=True)
            ghost_start = ghost_start + total[2]
            place_first = jnp.where(own_rank == first_rank, second_code, 0.0).astype(bf16)
            place_second = jnp.where(own_rank == second_rank, first_code, 0.0).astype(bf16)
            place_ghost = jnp.where(ghost_rank == second_rank, first_code, 0.0).astype(bf16)
            own_new = own_new + nt_dot(place_first, low[0]) + nt_dot(place_second, low[1])
            ghost_new = ghost_new + nt_dot(place_ghost, low[2])
            own_count = own_count + nt_dot(row, low[0]) + nt_dot(row, low[1])
            ghost_count = ghost_count + nt_dot(row, low[2])
        own_base[...] = own_start
        ghost_base[...] = ghost_start
        own_acc[...] = own_new
        ghost_acc[:, 0:ghosts] = ghost_new
        count_out[:, 0:LANES] = own_count
        count_out[:, LANES : LANES + ghosts] = ghost_count
        return carry

    lax.fori_loop(0, (live_total + span - 1) // span, step, 0)
    for copy in copies[1:]:
        copy.wait()
    own_code = own_acc[0:OWN_ROWS, :] + 160.0
    ghost_code = ghost_acc[0:GHOST_ROWS, :] + 160.0
    counts = count_out[0:1, :].astype(i32)
    own_live = lax.broadcasted_iota(i32, (OWN_ROWS, LANES), 0) < counts[:, 0:LANES]
    ghost_live = lax.broadcasted_iota(i32, ghost_code.shape, 0) < counts[:, LANES:]
    out_ref[0:64, :] = features_ref[...].astype(f32)
    out_ref[64:67, :] = positions_ref[...]
    out_ref[OWN_AT : OWN_AT + OWN_ROWS, :] = jnp.where(own_live, own_code, 0.0)
    ghost_code = jnp.where(ghost_live, ghost_code, 0.0)
    out_ref[X_AT : X_AT + GHOST_ROWS, :] = ghost_code[:, 0:LANES]
    copies_y = ghost_code[:, LANES:]
    out_ref[Y_AT : Y_AT + 16, :] = copies_y[0:16, :]
    lane = lax.broadcasted_iota(i32, (8, LANES), 1)
    out_ref[Y_AT : Y_AT + 8, :] = jnp.where(lane < LANES // 2, copies_y[0:8, :], pltpu.roll(copies_y[16:24, :], LANES // 2, axis=1))
    for group in range(3):
        out_ref[COUNT_AT + group : COUNT_AT + group + 1, :] = count_out[0:1, group * LANES : (group + 1) * LANES]
    out_ref[SEND_AT : SEND_AT + 1, :] = send_x_ref[...].astype(f32)
    out_ref[SEND_AT + 1 : SEND_AT + 2, 0 : send_y_ref.shape[1]] = send_y_ref[...].astype(f32)


def make_payload(edge_list, edge_count, positions, features, send_list_x, send_list_y):
    ghosts = send_list_x.shape[0] + send_list_y.shape[0]
    operands = (edge_list, positions, features, send_list_x[None, :], send_list_y[None, :])
    return pl.pallas_call(
        list_kernel,
        out_shape=jax.ShapeDtypeStruct((PAYLOAD, LANES), f32),
        in_specs=[pl.BlockSpec(memory_space=pltpu.SMEM)] + [pl.BlockSpec(memory_space=pl.ANY)] * 5,
        out_specs=pl.BlockSpec(memory_space=pltpu.VMEM),
        scratch_shapes=[pltpu.VMEM(operand.shape, operand.dtype) for operand in operands]
        + [
            pltpu.SemaphoreType.DMA((5,)),
            pltpu.VMEM((8, 3 * LANES), f32),
            pltpu.VMEM((64, LANES), f32),
            pltpu.VMEM((32, 2 * LANES), f32),
            pltpu.VMEM((LANES, EDGE_STEP), f32),
            pltpu.VMEM((ghosts, EDGE_STEP), f32),
        ],
        compiler_params=pltpu.CompilerParams(vmem_limit_bytes=56 * 1024 * 1024),
    )(edge_count, *operands)


def spread_row(ref, row, rows):
    return jnp.broadcast_to(ref[pl.ds(row, 1), :], (rows, LANES))


def lookup(table_ref, row, tile0, tiles, slot, block):
    result = None
    for number in range(tiles):
        at = (tile0 + number) * LANES
        entries = jnp.broadcast_to(table_ref[row : row + 1, at : at + LANES], (8, LANES))
        value = jnp.take_along_axis(entries, slot, axis=1)
        result = value if result is None else jnp.where(block == number, value, result)
    return result


def sine_cosine(scaled):
    angle = math.pi * (scaled - 0.5)
    square = angle * angle
    cosine = 1.0
    sine = 1.0
    for order in range(7, 0, -1):
        cosine = 1.0 - square * cosine * (1.0 / ((2 * order - 1) * (2 * order)))
        sine = 1.0 - square * sine * (1.0 / ((2 * order) * (2 * order + 1)))
    return cosine, -(angle * sine)


def pair_geometry(table_ref, codes, live, tile0, tiles, target, basis, tangent, sines_ref, slopes_ref):
    slot = codes & (LANES - 1)
    block = codes >> 7
    relative = []
    for axis in range(3):
        partner = lookup(table_ref, 64 + axis, tile0, tiles, slot, block)
        here = jnp.broadcast_to(
            table_ref[64 + axis : 65 + axis, target * LANES : (target + 1) * LANES], (8, LANES)
        )
        relative.append(jnp.where(live, partner - here, 2.0 if axis == 0 else 0.0))
    distance = jnp.sqrt(relative[0] * relative[0] + relative[1] * relative[1] + relative[2] * relative[2])
    inverse = 1.0 / distance
    direction = [part * inverse for part in relative]
    inside = live & (distance < cutoff_radius)
    scaled = jnp.minimum(distance, cutoff_radius) * (1.0 / cutoff_radius)
    room = 1.0 - scaled * scaled
    envelope = jnp.where(inside, message_scale * room * room, 0.0)
    envelope_slope = jnp.where(inside, (-4.0 * message_scale / cutoff_radius) * scaled * room, 0.0)
    sine, cosine = sine_cosine(scaled)
    twice = 2.0 * cosine
    scale = math.sqrt(2.0 / cutoff_radius)
    last_sine, last_cosine = jnp.zeros_like(sine), jnp.ones_like(sine)
    for order in range(1, basis + 1):
        wave = scale * sine * inverse
        sines_ref[(order - 1) * 8 : order * 8, :] = wave
        if tangent:
            slope = (scale * order * math.pi / cutoff_radius) * cosine * inverse - wave * inverse
            slopes_ref[(order - 1) * 8 : order * 8, :] = slope
        sine, last_sine = twice * sine - last_sine, sine
        cosine, last_cosine = twice * cosine - last_cosine, cosine
    return direction, inverse, envelope, envelope_slope, inside


def split_rows(ref, basis, at):
    pieces = []
    for row in range(8):
        whole = ref[pl.ds(at + row, basis, stride=8), :]
        high = whole.astype(bf16).astype(f32)
        rest = whole - high
        middle = rest.astype(bf16).astype(f32)
        low = rest - middle
        pieces.append(jnp.concatenate([high, middle, high, middle, low, high], axis=0).astype(bf16))
    return jnp.concatenate(pieces, axis=1)


def high_low(value):
    high = value.astype(bf16)
    low = (value - high.astype(f32)).astype(bf16)
    return high, low


def shapes_of(direction):
    x, y, z = direction
    three, five, fifteen = math.sqrt(3.0), math.sqrt(5.0), math.sqrt(15.0)
    return [
        jnp.ones_like(x),
        three * x,
        three * y,
        three * z,
        fifteen * x * y,
        fifteen * y * z,
        0.5 * five * (3.0 * z * z - 1.0),
        fifteen * x * z,
        0.5 * fifteen * (x * x - y * y),
    ]


def hot_codes(list_ref, offset, size, first):
    columns = []
    lane = lax.broadcasted_iota(i32, (size, LANES), 0) + first
    for row in range(8):
        codes = jnp.broadcast_to(list_ref[pl.ds(offset + row, 1), :], (size, LANES))
        columns.append((lane == codes).astype(f32).astype(bf16))
    return jnp.concatenate(columns, axis=1)


def forward_geometry(refs, basis, list_ref, count, tile0, tiles, target, shape0, chunks, tangents):
    table_ref, sines_ref, slopes_ref, env_ref, shape_ref, geometry_ref = refs
    rows_in = 8 * basis
    for block in range(chunks):
        part, slot = block % 2, shape0 + block // 2
        tangent = block < tangents
        at = shape0 * 2 + block
        codes = list_ref[block * 8 : block * 8 + 8, :]
        live = (block * 8 + lax.broadcasted_iota(i32, (8, LANES), 0) < count) & (codes >= 0)
        direction, inverse, envelope, envelope_slope, inside = pair_geometry(
            table_ref, codes, live, tile0, tiles, target, basis, tangent,
            sines_ref.at[pl.ds(at * rows_in, rows_in), :], slopes_ref.at[pl.ds(at * rows_in, rows_in), :],
        )
        env_ref[at * 16 : at * 16 + 8, :] = envelope
        shapes = shapes_of(direction)
        for q in range(1, 9):
            shape_ref[part][slot, q * 8 : q * 8 + 8, :] = shapes[q]
        if tangent:
            env_ref[at * 16 + 8 : at * 16 + 16, :] = envelope_slope
            for axis in range(3):
                geometry_ref[part][slot, axis * 8 : axis * 8 + 8, :] = direction[axis]
            geometry_ref[part][slot, 24:32, :] = inverse
            geometry_ref[part][slot, 32:40, :] = inside.astype(f32)


def forward_pairs(refs, list_ref, tile0, tiles, lane0, slot0, shape0, tangent, start, stop, out_ref):
    (table_ref, feature_ref, win_ref, wout_ref, sines_ref, slopes_ref, env_ref, shape_ref, geometry_ref, hidden_ref, radial_ref, partner_ref) = refs
    basis = win_ref.shape[1] // 6
    size = tiles * LANES
    first = tile0 * LANES
    wide = 8 * LANES
    rows_in = 8 * basis

    def step(number, carry):
        both = (0, 1)
        offset = [pl.multiple_of(number * 16 + part * 8, 8) for part in both]
        slot = slot0 + number if tangent else slot0
        shapes_at = shape0 + number
        chunk = [shapes_at * 2 + part for part in both]
        span = 2 * wide if tangent else wide
        stacked = []
        for part in both:
            stacked.append(split_rows(sines_ref, basis, chunk[part] * rows_in))
            if tangent:
                stacked.append(split_rows(slopes_ref, basis, chunk[part] * rows_in))
        value = plain_dot(win_ref[...], jnp.concatenate(stacked, axis=1))
        for part in both:
            if tiles > 4:
                hot = hot_codes(list_ref, offset[part], size, 0)
                partner_ref[part][slot] = plain_dot(feature_ref[:, first : first + size], hot)
            else:
                for row in range(8):
                    codes = jnp.broadcast_to(list_ref[pl.ds(offset[part] + row, 1), :], (8, LANES))
                    at_lane = codes & (LANES - 1)
                    tile = codes >> 7
                    for block in range(8):
                        result = None
                        for other in range(tiles):
                            entries = table_ref[block * 8 : block * 8 + 8, first + other * LANES : first + (other + 1) * LANES]
                            entry = jnp.take_along_axis(entries, at_lane, axis=1)
                            result = entry if result is None else jnp.where(tile == other, entry, result)
                        partner_ref[part][slot, block * 8 : block * 8 + 8, row * LANES : (row + 1) * LANES] = result
        for part in both:
            for row in range(8):
                lanes = slice(part * span + row * LANES, part * span + (row + 1) * LANES)
                here = value[:, lanes]
                scale = spread_row(env_ref, chunk[part] * 16 + row, 64)
                gate = 1.0 / (1.0 + jnp.exp(-here))
                hidden = here * gate
                high, low = high_low(hidden * scale)
                hidden_ref[0:64, lanes] = high
                hidden_ref[64:128, lanes] = low
                if tangent:
                    later = slice(lanes.start + wide, lanes.stop + wide)
                    hidden_slope = gate * (1.0 + here * (1.0 - gate)) * value[:, later]
                    scale_slope = spread_row(env_ref, chunk[part] * 16 + 8 + row, 64)
                    high, low = high_low(hidden * scale_slope + hidden_slope * scale)
                    hidden_ref[0:64, later] = high
                    hidden_ref[64:128, later] = low
        hidden = hidden_ref[:, 0 : 2 * span]
        radial = plain_dot(wout_ref[...], jnp.concatenate([hidden, hidden], axis=0))
        for part in both:
            radial_ref[part][slot, :, 0:span] = radial[:, part * span : (part + 1) * span]
        for block in range(8):
            sums = [
                out_ref[q * 64 + block * 8 : q * 64 + block * 8 + 8, lane0 : lane0 + LANES]
                for q in range(9)
            ]
            for part in both:
                for row in range(8):
                    lanes = slice(row * LANES, (row + 1) * LANES)
                    feature = partner_ref[part][slot, block * 8 : block * 8 + 8, lanes]
                    for degree, (low, high) in enumerate(DEGREE_ROWS):
                        at = degree * 64 + block * 8
                        weight = radial_ref[part][slot, at : at + 8, lanes] * feature
                        for q in range(low, high):
                            if q == 0:
                                sums[q] = sums[q] + weight
                            else:
                                shape = jnp.broadcast_to(shape_ref[part][shapes_at, q * 8 + row : q * 8 + row + 1, :], (8, LANES))
                                sums[q] = sums[q] + weight * shape
            for q in range(9):
                out_ref[q * 64 + block * 8 : q * 64 + block * 8 + 8, lane0 : lane0 + LANES] = sums[q]
        return carry

    lax.fori_loop(start, stop, step, 0)


def backward_steps(refs, steps, slot0, shape0, chunk0, lane0, gradient_ref):
    shape_ref, geometry_ref, radial_ref, partner_ref, pulled_ref = refs
    wide = 8 * LANES

    def block_step(number, part, chunk):
        slot = slot0 + number
        for row in range(8):
            lanes = slice(row * LANES, (row + 1) * LANES)
            later = slice(wide + row * LANES, wide + (row + 1) * LANES)
            pulled = [jnp.zeros((8, LANES), f32) for q in range(9)]
            spoke = pulled[0]
            shapes = [None] + [
                jnp.broadcast_to(shape_ref[part][shape0 + number, q * 8 + row : q * 8 + row + 1, :], (8, LANES)) for q in range(1, 9)
            ]
            for block in range(8):
                feature = partner_ref[part][slot, block * 8 : block * 8 + 8, lanes]
                for degree, (low, high) in enumerate(DEGREE_ROWS):
                    at = degree * 64 + block * 8
                    weight = radial_ref[part][slot, at : at + 8, lanes] * feature
                    weight_slope = radial_ref[part][slot, at : at + 8, later] * feature
                    mixed = None
                    for q in range(low, high):
                        gradient = gradient_ref[q * 64 + block * 8 : q * 64 + block * 8 + 8, lane0 : lane0 + LANES]
                        if q > 0:
                            pulled[q] = pulled[q] + weight * gradient
                            gradient = gradient * shapes[q]
                        mixed = gradient if mixed is None else mixed + gradient
                    spoke = spoke + weight_slope * mixed
            pulled[0] = spoke
            for q in range(9):
                pulled_ref[chunk, q * 64 + row * 8 : q * 64 + row * 8 + 8, :] = pulled[q]

    def step(number, carry):
        block_step(number, 0, chunk0 + number * 2)

        @pl.when(number * 2 + 1 < steps)
        def _():
            block_step(number, 1, chunk0 + number * 2 + 1)

        return carry

    lax.fori_loop(0, (steps + 1) // 2, step, 0)


def pair_forces(refs, list_ref, chunks, steps, slot0, chunk0, own_code, push_ref):
    shape_ref, geometry_ref, radial_ref, partner_ref, pulled_ref = refs
    three, five, fifteen = math.sqrt(3.0), math.sqrt(5.0), math.sqrt(15.0)
    on_target = [jnp.zeros((8, LANES), f32) for axis in range(3)]
    on_partner = jnp.zeros((8, LANES), f32)
    for chunk in range(chunks):
        part, slot = chunk % 2, slot0 + chunk // 2
        x, y, z = direction = [geometry_ref[part][slot, axis * 8 : axis * 8 + 8, :] for axis in range(3)]
        inverse = geometry_ref[part][slot, 24:32, :]
        inside = (geometry_ref[part][slot, 32:40, :] > 0.5) & (chunk < steps)
        p = []
        for q in range(9):
            parts = [pulled_ref[chunk0 + chunk, pl.ds(q * 64 + sub, 8, stride=8), :] for sub in range(8)]
            while len(parts) > 1:
                parts = [parts[i] + parts[i + 1] for i in range(0, len(parts), 2)]
            p.append(parts[0])
        turn = [
            three * p[1] + fifteen * (y * p[4] + z * p[7] + x * p[8]),
            three * p[2] + fifteen * (x * p[4] + z * p[5] - y * p[8]),
            three * p[3] + fifteen * (y * p[5] + x * p[7]) + (3.0 * five) * z * p[6],
        ]
        along = x * turn[0] + y * turn[1] + z * turn[2]
        base = (chunk0 + chunk) * 64
        for axis in range(3):
            force = (turn[axis] - direction[axis] * along) * inverse + direction[axis] * p[0]
            force = jnp.where(inside, force, 0.0)
            on_target[axis] = on_target[axis] + force
            high = force.astype(bf16).astype(f32)
            push_ref[base + axis * 8 : base + axis * 8 + 8, :] = high
            push_ref[base + 24 + axis * 8 : base + 32 + axis * 8, :] = force - high
        push = jnp.concatenate([push_ref[pl.ds(base + row, 8, stride=8), :] for row in range(8)], axis=1)
        hot = hot_codes(list_ref, chunk * 8, LANES, own_code)
        on_partner = on_partner + nt_dot(push.astype(bf16), hot)
    return on_target, on_partner


def rounded(value):
    return lax.reduce_precision(value, 8, 7)


def stacked_weights(radial_in, radial_out):
    high = rounded(radial_in)
    middle = rounded(radial_in - high)
    low = rounded(radial_in - high - middle)
    win = jnp.concatenate([high, high, middle, middle, high, low], axis=1).astype(bf16)
    high = rounded(radial_out)
    low = rounded(radial_out - high)
    wout = jnp.concatenate([high, high, low, low], axis=1).astype(bf16)
    return win, wout


HALF = LANES // 2
QUARTER = LANES // 4
MIDDLE = 4
AROUND = (0, 1, 2, 6, 7, 8)
TILE_OF = {0: 0, 1: 1, 2: 2, 6: 3, 7: 4, 8: 5, 3: 6, 5: 7, 4: 8}
TILE_LR, TILE_OWN, TILE_X, TILE_Y, TILES = 9, 10, 11, 12, 13
LIST_ROWS = 64
MOST_PAIRS = 49
SLOT_OWN, SLOT_X, SLOT_Y, SLOT_FREE, SLOTS = 0, 4, 6, 7, 8
SHAPE_OWN, SHAPE_X, SHAPE_Y, SHAPES = 0, 4, 8, 10


def rep(row):
    return jnp.broadcast_to(row, (8, LANES))


def tall(value, rows):
    return jnp.concatenate([value] * (rows // 8), axis=0)


def pick(values, slots):
    return jnp.take_along_axis(values, tall(slots, values.shape[0]) if slots.shape[0] != values.shape[0] else slots, axis=1)


def merge(base, count, segment, more):
    rows = base.shape[0]
    if segment.shape[0] < rows:
        segment = jnp.concatenate([segment, jnp.zeros((rows - segment.shape[0], LANES), i32)], axis=0)
    shift = tall(count, rows)
    for bit in (1, 2, 4, 8, 16, 32):
        segment = jnp.where((shift & bit) != 0, pltpu.roll(segment, bit, axis=0), segment)
    row = lax.broadcasted_iota(i32, (rows, LANES), 0)
    return jnp.where(row < shift, base, segment), count + more


def join(pieces):
    codes, count = pieces[0]
    for other, number in pieces[1:]:
        codes = jnp.where(tall(number, other.shape[0]) > 0, other, codes)
        count = count + number
    return codes, count


def main_kernel(strip_ref, low_ref, high_ref, win_ref, wout_ref, mix_ref, outw_ref, shift_ref,
                energy_ref, force_out, table_ref, feature_ref, column_ref, list_own, list_x, list_y,
                sums_ref, sines_ref, slopes_ref, env_ref, hidden_ref, pulled_ref, push_ref, *kept):
    shape_ref, geometry_ref, radial_ref, partner_ref = (kept[number : number + 2] for number in range(0, 8, 2))
    refs = (low_ref, strip_ref, high_ref)

    def rows_of(block, at, size):
        start = (block % 3) * PAYLOAD + at
        return refs[block // 3][start : start + size, :]

    def list_of(block, at):
        if at == X_AT:
            return rows_of(block, at, GHOST_ROWS).astype(i32)
        folded = rows_of(block, at, 16)
        return jnp.concatenate([folded, pltpu.roll(folded[0:8, :], HALF, axis=1)], axis=0).astype(i32)

    def row_of(block, at):
        return rep(rows_of(block, at, 1).astype(i32))

    lane = lax.broadcasted_iota(i32, (8, LANES), 1)
    none = jnp.full((8, LANES), -1, i32)

    x_home = {}
    for block in range(9):
        dx = block % 3
        lower = (block - 1) * LANES + pltpu.roll(row_of(block - 1, SEND_AT), HALF, axis=1) if dx > 0 else none
        upper = (block + 1) * LANES + pltpu.roll(row_of(block + 1, SEND_AT), HALF, axis=1) if dx < 2 else none
        x_home[block] = jnp.where(lane < HALF, lower, upper)

    def section_home(block, entry):
        copies = jnp.take_along_axis(x_home[block], entry & (LANES - 1), axis=1)
        return jnp.where(entry < LANES, block * LANES + entry, copies)

    y_home = {}
    for block in range(9):
        dy = block // 3
        if dy > 0:
            lower = section_home(block - 3, pltpu.roll(row_of(block - 3, SEND_AT + 1), LANES - QUARTER, axis=1))
        else:
            lower = none
        if dy < 2:
            upper = section_home(block + 3, pltpu.roll(row_of(block + 3, SEND_AT + 1), QUARTER, axis=1))
        else:
            upper = none
        y_home[block] = jnp.where(lane < QUARTER, lower, jnp.where(lane < HALF, upper, none))

    x_here = x_home[MIDDLE]
    y_here = y_home[MIDDLE]
    y_twice = jnp.where(lane < HALF, y_here, pltpu.roll(y_here, HALF, axis=1))
    y_sides = jnp.where(lane < HALF, y_home[3], pltpu.roll(y_home[5], HALF, axis=1))

    column_ref[...] = jnp.zeros_like(column_ref)
    slots = {}

    def as_column(name, value):
        slots[name] = len(slots)
        column_ref[slots[name] : slots[name] + 1, :] = value[0:1, :].astype(f32)

    as_column("sent", row_of(MIDDLE, SEND_AT))
    as_column("x", x_here)
    as_column("y", y_here)
    as_column("sides", y_sides)
    for block in range(9):
        if block != MIDDLE:
            as_column(("y", block), y_home[block])
    for block in AROUND:
        as_column(("x", block), x_home[block])
    columns = jnp.transpose(column_ref[...])
    place = lax.broadcasted_iota(i32, (LANES, LANES), 0).astype(f32)

    def match(name, target, low=0, high=LANES):
        number = slots[name]
        same = columns[low:high, number : number + 1] == target[0:1, :].astype(f32)
        return rep(jnp.max(jnp.where(same, place[low:high, :], -1.0), axis=0, keepdims=True).astype(i32))

    def gathered(home, blocks, rows, at):
        block_of = home >> 7
        slot = home & (LANES - 1)
        result = jnp.zeros((rows, LANES), f32)
        for block in blocks:
            result = jnp.where(tall(block_of, rows) == block, pick(rows_of(block, at, rows), slot), result)
        return result

    for block, tile in TILE_OF.items():
        table_ref[:, tile * LANES : (tile + 1) * LANES] = rows_of(block, 0, 72)
    table_ref[:, TILE_OWN * LANES : (TILE_OWN + 1) * LANES] = rows_of(MIDDLE, 0, 72)
    table_ref[:, TILE_X * LANES : (TILE_X + 1) * LANES] = gathered(x_here, (3, 5), 72, 0)
    table_ref[:, TILE_Y * LANES : (TILE_Y + 1) * LANES] = gathered(y_twice, AROUND, 72, 0)
    table_ref[:, TILE_LR * LANES : (TILE_LR + 1) * LANES] = gathered(y_sides, AROUND, 72, 0)
    feature_ref[...] = table_ref[0:64, :].astype(bf16)

    def aligned(block, at, rows, count_at, found):
        at_lane = jnp.maximum(found, 0)
        codes = rows_of(block, at, rows).astype(i32) if at == OWN_AT else list_of(block, at)
        codes = pick(codes, at_lane)
        count = jnp.take_along_axis(row_of(block, count_at), at_lane, axis=1)
        return codes, jnp.where(found >= 0, count, 0)

    def renamed(codes, table, offset):
        found = pick(jnp.concatenate([table] * (codes.shape[0] // 8), axis=0), codes & (LANES - 1))
        return jnp.where(found >= 0, found + offset, -1)

    own_home = MIDDLE * LANES + lane
    codes = jnp.concatenate([rows_of(MIDDLE, OWN_AT, OWN_ROWS).astype(i32), jnp.zeros((LIST_ROWS - OWN_ROWS, LANES), i32)], axis=0)
    count = row_of(MIDDLE, COUNT_AT)
    found_low = match("sent", lane, 0, HALF)
    found_low = jnp.where(found_low >= 0, found_low + HALF, -1)
    found_high = match("sent", lane, HALF, LANES)
    found_high = jnp.where(found_high >= 0, found_high - HALF, -1)
    pieces = []
    for block, found in ((3, found_low), (5, found_high)):
        piece, number = aligned(block, X_AT, GHOST_ROWS, COUNT_AT + 1, found)
        pieces.append((renamed(piece, match("x", block * LANES + lane), LANES), number))
    codes, count = merge(codes, count, *join(pieces))
    y_lane = {block: match("y", block * LANES + lane) for block in AROUND}
    for blocks in ((1, 7), (0, 2, 6, 8)):
        pieces = []
        for block in blocks:
            piece, number = aligned(block, Y_AT, GHOST_ROWS, COUNT_AT + 2, match(("y", block), own_home, 0, HALF))
            pieces.append((renamed(piece, y_lane[block], 2 * LANES), number))
        codes, count = merge(codes, count, *join(pieces))
    list_own[...] = codes
    count_own = count

    pieces = []
    for block, tile in ((3, 0), (5, 1)):
        found = jnp.where(x_here >> 7 == block, x_here & (LANES - 1), -1)
        piece, number = aligned(block, OWN_AT, OWN_ROWS, COUNT_AT, found)
        home = pick(jnp.concatenate([x_home[block]] * (OWN_ROWS // 8), axis=0), piece & (LANES - 1))
        copy = jnp.where(home >> 7 == MIDDLE, 2 * LANES + (home & (LANES - 1)), -1)
        piece = jnp.where(
            piece < LANES, piece + tile * LANES, jnp.where(piece < 2 * LANES, copy, piece + LANES + tile * HALF)
        )
        pieces.append((piece, number))
    codes, count = join(pieces)
    codes = jnp.concatenate([codes, jnp.zeros((LIST_ROWS - OWN_ROWS, LANES), i32)], axis=0)
    codes, count = merge(
        codes, count, list_of(MIDDLE, X_AT) + 2 * LANES, row_of(MIDDLE, COUNT_AT + 1)
    )
    side_lane = {block: match("sides", block * LANES + lane) for block in AROUND}
    for blocks in ((1, 7), (0, 2, 6, 8)):
        pieces = []
        for block in blocks:
            piece, number = aligned(block, Y_AT, GHOST_ROWS, COUNT_AT + 2, match(("y", block), x_here, 0, HALF))
            pieces.append((renamed(piece, side_lane[block], 3 * LANES), number))
        codes, count = merge(codes, count, *join(pieces))
    codes_x, count_x = codes, count

    def tiled(home):
        block = home >> 7
        tile = jnp.where(block < 3, block, jnp.where(block > 5, block - 3, jnp.where(block == 3, 6, jnp.where(block == 5, 7, 8))))
        return jnp.where(home >= 0, tile * LANES + (home & (LANES - 1)), -1)

    pieces = []
    for block in AROUND:
        found = jnp.where(y_here >> 7 == block, y_here & (LANES - 1), -1)
        piece, number = aligned(block, OWN_AT, OWN_ROWS, COUNT_AT, found)
        slot = piece & (LANES - 1)
        copy_x = pick(jnp.concatenate([tiled(x_home[block])] * (OWN_ROWS // 8), axis=0), slot)
        copy_y = pick(jnp.concatenate([tiled(y_home[block])] * (OWN_ROWS // 8), axis=0), slot)
        piece = jnp.where(
            piece < LANES, piece + TILE_OF[block] * LANES, jnp.where(piece < 2 * LANES, copy_x, copy_y)
        )
        pieces.append((piece, number))
    codes, count = join(pieces)
    codes = jnp.concatenate([codes, jnp.zeros((LIST_ROWS - OWN_ROWS, LANES), i32)], axis=0)
    pieces = []
    for block in AROUND:
        piece, number = aligned(block, X_AT, GHOST_ROWS, COUNT_AT + 1, match(("x", block), y_here))
        pieces.append((piece + TILE_OF[block] * LANES, number))
    codes, count = merge(codes, count, *join(pieces))
    codes, count = merge(
        codes, count, list_of(MIDDLE, Y_AT) + TILE_OF[MIDDLE] * LANES, row_of(MIDDLE, COUNT_AT + 2)
    )
    pieces = []
    for block in (3, 5):
        piece, number = aligned(block, Y_AT, GHOST_ROWS, COUNT_AT + 2, match(("y", block), y_here, 0, HALF))
        pieces.append((piece + TILE_OF[block] * LANES, number))
    codes, count = merge(codes, count, *join(pieces))
    count = jnp.where(lane < HALF, count, 0)
    codes_y, count_y = codes, count

    earlier = (
        lax.broadcasted_iota(i32, (LIST_ROWS, LIST_ROWS), 1) < lax.broadcasted_iota(i32, (LIST_ROWS, LIST_ROWS), 0)
    ).astype(f32).astype(bf16)
    row = lax.broadcasted_iota(i32, (LIST_ROWS, LANES), 0)

    def own_first(codes, count, first):
        live = row < tall(count, LIST_ROWS)
        kept = live & (codes >= first) & (codes < first + LANES)
        weight = kept.astype(f32)
        total = jnp.sum(weight, axis=0, keepdims=True)
        rest = live.astype(f32) - weight
        rank = plain_dot(earlier, jnp.concatenate([weight, rest], axis=1).astype(bf16))
        place_at = jnp.where(kept, rank[:, 0:LANES], jnp.where(live, rank[:, LANES:] + total, -1.0))
        value = codes.astype(f32)
        rows = [
            jnp.sum(jnp.where(place_at == float(number), value, 0.0), axis=0, keepdims=True).astype(i32)
            for number in range(MOST_PAIRS)
        ]
        return rows, rep(total)

    list_x[...] = jnp.zeros_like(list_x)
    list_y[...] = jnp.zeros_like(list_y)
    rows_x, back_x = own_first(codes_x, count_x, 2 * LANES)
    for number in range(MOST_PAIRS):
        list_x[number : number + 1, :] = rows_x[number]
    rows_y, back_y = own_first(codes_y, count_y, TILE_OF[MIDDLE] * LANES)
    blank = jnp.zeros((1, LANES), i32)
    for number in range(0, MOST_PAIRS, 2):
        odd = rows_y[number + 1] if number + 1 < MOST_PAIRS else blank
        odd = pltpu.roll(rep(odd), HALF, axis=1)
        list_y[number // 2 : number // 2 + 1, :] = jnp.where(lane < HALF, rep(rows_y[number]), odd)[0:1, :]
    count_pack = jnp.where(lane < HALF, (count_y + 1) >> 1, pltpu.roll(count_y, HALF, axis=1) >> 1)

    sums_ref[...] = jnp.zeros_like(sums_ref)

    def most(count):
        return jnp.max(count.astype(f32)).astype(i32)

    pairs_own = (most(count_own) + 15) // 16
    pairs_x = (most(count_x) + 15) // 16
    pairs_y = (most(count_pack) + 15) // 16
    scratch = (table_ref, feature_ref, win_ref, wout_ref, sines_ref, slopes_ref, env_ref, shape_ref, geometry_ref, hidden_ref, radial_ref, partner_ref)
    basis = win_ref.shape[1] // 6
    places = (table_ref, sines_ref, slopes_ref, env_ref, shape_ref, geometry_ref)
    forward_geometry(places, basis, list_own, count_own, TILE_OWN, 3, TILE_OWN, SHAPE_OWN, 8, 8)
    forward_geometry(places, basis, list_x, count_x, 6, 4, TILE_X, SHAPE_X, 8, 4)
    forward_geometry(places, basis, list_y, count_pack, 0, 9, TILE_Y, SHAPE_Y, 4, 2)
    forward_pairs(scratch, list_own, TILE_OWN, 3, 0, SLOT_OWN, SHAPE_OWN, True, 0, pairs_own, sums_ref)
    forward_pairs(scratch, list_x, 6, 4, LANES, SLOT_X, SHAPE_X, True, 0, jnp.minimum(pairs_x, 2), sums_ref)
    forward_pairs(scratch, list_x, 6, 4, LANES, SLOT_FREE, SHAPE_X, False, 2, pairs_x, sums_ref)
    forward_pairs(scratch, list_y, 0, 9, 2 * LANES, SLOT_Y, SHAPE_Y, True, 0, jnp.minimum(pairs_y, 1), sums_ref)
    forward_pairs(scratch, list_y, 0, 9, 2 * LANES, SLOT_FREE, SHAPE_Y, False, 1, pairs_y, sums_ref)
    sums_y = sums_ref[:, 2 * LANES : 3 * LANES]
    sums_ref[:, 2 * LANES : 3 * LANES] = sums_y + pltpu.roll(sums_y, HALF, axis=1)

    sums = sums_ref[...]
    square = sums * sums
    degree_one = square[64:128] + square[128:192] + square[192:256]
    degree_two = square[256:320] + square[320:384] + square[384:448] + square[448:512] + square[512:576]
    invariant = jnp.concatenate([square[0:64], degree_one, degree_two], axis=0)
    mixed = lax.dot_general(
        mix_ref[...], invariant, (((1,), (0,)), ((), ())), precision=highest, preferred_element_type=f32
    ) + table_ref[0:64, TILE_OWN * LANES : (TILE_Y + 1) * LANES]
    gate = 1.0 / (1.0 + jnp.exp(-mixed))
    weight = outw_ref[...]
    energy = jnp.sum(weight * (mixed * gate)[:, 0:LANES], axis=0, keepdims=True)
    energy_ref[...] = energy + shift_ref[...]
    slope = weight * (gate * (1.0 + mixed * (1.0 - gate)))
    pulled = 2.0 * lax.dot_general(
        mix_ref[...], slope, (((0,), (0,)), ((), ())), precision=highest, preferred_element_type=f32
    )
    for q in range(9):
        degree = (0, 1, 1, 1, 2, 2, 2, 2, 2)[q]
        sums_ref[q * 64 : q * 64 + 64, :] = sums[q * 64 : q * 64 + 64] * pulled[degree * 64 : degree * 64 + 64]

    push_ref[...] = jnp.zeros_like(push_ref)
    scratch = (shape_ref, geometry_ref, radial_ref, partner_ref, pulled_ref)
    steps_own = (most(count_own) + 7) // 8
    steps_x = (most(back_x) + 7) // 8
    steps_y = (most(back_y) + 15) // 16
    backward_steps(scratch, steps_own, SLOT_OWN, SHAPE_OWN, 0, 0, sums_ref)
    backward_steps(scratch, steps_x, SLOT_X, SHAPE_X, 7, LANES, sums_ref)
    backward_steps(scratch, steps_y, SLOT_Y, SHAPE_Y, 10, 2 * LANES, sums_ref)
    forces, pushed = pair_forces(scratch, list_own, 7, steps_own, SHAPE_OWN, 0, 0, push_ref)
    pushed = pushed + pair_forces(scratch, list_x, 3, steps_x, SHAPE_X, 7, 2 * LANES, push_ref)[1]
    pushed = pushed + pair_forces(scratch, list_y, 2, steps_y, SHAPE_Y, 10, TILE_OF[MIDDLE] * LANES, push_ref)[1]
    for axis in range(3):
        force_out[axis : axis + 1, :] = (
            jnp.sum(forces[axis], axis=0, keepdims=True) - pushed[axis : axis + 1, :] - pushed[axis + 3 : axis + 4, :]
        )


def main_pass(strip, low, high, win, wout, mix_weight, out_weight, shift):
    vmem = pl.BlockSpec(memory_space=pltpu.VMEM)
    wide = 8 * LANES
    return pl.pallas_call(
        main_kernel,
        out_shape=(jax.ShapeDtypeStruct((1, LANES), f32), jax.ShapeDtypeStruct((3, LANES), f32)),
        in_specs=[vmem] * 8,
        out_specs=(vmem, vmem),
        scratch_shapes=[
            pltpu.VMEM((72, TILES * LANES), f32),
            pltpu.VMEM((64, TILES * LANES), bf16),
            pltpu.VMEM((LANES, LANES), f32),
            pltpu.VMEM((LIST_ROWS, LANES), i32),
            pltpu.VMEM((LIST_ROWS, LANES), i32),
            pltpu.VMEM((32, LANES), i32),
            pltpu.VMEM((576, 3 * LANES), f32),
            pltpu.VMEM((SHAPES * 128, LANES), f32),
            pltpu.VMEM((SHAPES * 128, LANES), f32),
            pltpu.VMEM((SHAPES * 32, LANES), f32),
            pltpu.VMEM((128, 4 * wide), bf16),
            pltpu.VMEM((12, 576, LANES), f32),
            pltpu.VMEM((12 * 64, LANES), f32),
        ]
        + [pltpu.VMEM((SHAPES, 72, LANES), f32)] * 2
        + [pltpu.VMEM((SHAPES, 40, LANES), f32)] * 2
        + [pltpu.VMEM((SLOTS, 192, 2 * wide), f32)] * 2
        + [pltpu.VMEM((SLOTS, 64, wide), f32)] * 2,
        compiler_params=pltpu.CompilerParams(vmem_limit_bytes=48 * 1024 * 1024),
    )(strip, low, high, win, wout, mix_weight, out_weight[:, None], shift)


def from_ring(block, axis):
    count = lax.axis_size(axis)
    up = [(i, (i + 1) % count) for i in range(count)]
    down = [(target, source) for source, target in up]
    return lax.ppermute(block, axis, up), lax.ppermute(block, axis, down)


def from_both_sides(block, axis):
    count = lax.axis_size(axis)

    def swapped(start):
        pairs = []
        for number in range(count):
            other = number + 1 if (number - start) % 2 == 0 else number - 1
            pairs.append((number, other if 0 <= other < count else number))
        return lax.ppermute(block, axis, pairs)

    even, odd = swapped(0), swapped(1)
    here = lax.axis_index(axis)
    upper_first = here % 2 == 0
    low = jnp.where(here > 0, jnp.where(upper_first, odd, even), 0.0)
    high = jnp.where(here < count - 1, jnp.where(upper_first, even, odd), 0.0)
    return low, high


def local(
    positions, features, species, edge_list, edge_count, send_list_x, send_list_y,
    radial_in, radial_out, mix_weight, out_weight, species_energy,
):
    own = make_payload(edge_list, edge_count, positions, features, send_list_x, send_list_y)
    left, right = from_ring(own, "gx")
    strip = jnp.concatenate([left, own, right], axis=0)
    low, high = from_both_sides(strip, "gy")
    win, wout = stacked_weights(radial_in, radial_out)
    kinds = jnp.arange(species_energy.shape[0], dtype=i32)
    shift = jnp.sum(jnp.where(species[None, :] == kinds[:, None], species_energy[:, None], 0.0), axis=0)[None, :]
    energies, forces = main_pass(strip, low, high, win, wout, mix_weight, out_weight, shift)
    return energies[0], forces


def solution(mesh):
    placed = (
        P(None, ("gx", "gy")), P(None, ("gx", "gy")), P(("gx", "gy")), P(None, ("gx", "gy")), P(("gx", "gy")),
        P(("gx", "gy")), P(("gx", "gy")), P(), P(), P(), P(), P(),
    )
    return jax.shard_map(
        local, mesh=mesh, in_specs=placed, out_specs=(P(("gx", "gy")), P(None, ("gx", "gy"))), check_vma=False,
    )
```
